32 devices in a mesh: dom: 8 (over z, y), pipe: 4 (over x, core).
Axes of the slice: x: 2, y: 2, z: 4, core: 2. Of those that a mesh axis runs over, the one named last changes fastest.
Arguments:
- inputs: bfloat16 [2, 2048, 512], P(None, 'dom'), may hold values from -6 to 6
- cotangent: bfloat16 [2, 2048, 512], P(None, 'dom'), may hold values from -6 to 6
- w_send: bfloat16 [4, 512, 512], P('pipe'), may hold values from -0.25 to 0.25
- w_recv: bfloat16 [4, 512, 512], P('pipe'), may hold values from -0.25 to 0.25
- w_message: bfloat16 [4, 512, 512], P('pipe'), may hold values from -0.25 to 0.25
- w_node: bfloat16 [4, 512, 512], P('pipe'), may hold values from -0.25 to 0.25
- w_aggregate: bfloat16 [4, 512, 512], P('pipe'), may hold values from -0.25 to 0.25
- gains: float32 [4, 512], P('pipe'), may hold values from 0.1 to 1.9
- edge_send: int32 [16, 128], P('dom'), may hold values from 0 to 511, as said below
- edge_recv: int32 [16, 128], P('dom'), may hold values from 0 to 255, as said below
- edge_count: int32 [16], P('dom'), may hold values from 1 to 128, as said below
- halo_send: int32 [8, 2, 1], P('dom'), may hold values from 0 to 1, as said below
Outputs:
- section_out: bfloat16 [4, 2, 2048, 512], P('pipe', None, 'dom')
- input_grad: bfloat16 [4, 2, 2048, 512], P('pipe', None, 'dom')
The draws below stay inside these ranges and needn't reach their ends.
Inputs may be any that keep to these rules, and one draw needn't show every extreme that they name: `edge_send`: rows 0 to 255 are the partition's own rows, the next 128 the blocks received from the previous partition in list order, the last 128 those from the next partition. The largest and smallest values are reached. `edge_recv`: both ends are reached. `edge_count`: the live slots of a block are its first ones; one block is full and one has a single live slot. `halo_send`: each list names 1 distinct own blocks. Lists wrap around the partitions.
All inputs are finite; a program needn't handle non-finite values.
Results may differ from the reference program's by a relative error of at most 0.015.
Values may be sent and summed in bfloat16 or wider, within the bound.
No kernel may reach another device: no remote copies, remote signals or barrier semaphores. Data moves between devices by JAX's collectives and lax.ppermute only.
A program may use at most 64 MiB of HBM per device.

```python
import jax
import jax.numpy as jnp
from jax import lax

D = 512
BLOCK = 128
NB = 2
HB = 1
EB = 2
MICRO = 2
PARTITIONS = 8
SECTIONS = 4
NODES = 2048


def draw_halo_send(key, part):
    scores = jax.random.randint(jax.random.fold_in(key, 11), (PARTITIONS, 2, NB), 0, 1 << 20) * NB + jnp.arange(NB)
    orders = jnp.argsort(scores, axis=-1, stable=True).astype(jnp.int32)
    return orders[:, :, :HB].astype(jnp.int32)


def draw_edge_send(key, part):
    own_rows = NB * BLOCK
    halo_span = HB * BLOCK
    kinds = jax.random.randint(jax.random.fold_in(key, 13), (PARTITIONS * EB, BLOCK), 0, 8)
    lower = jnp.where(kinds < 6, 0, jnp.where(kinds == 6, own_rows, own_rows + halo_span))
    upper = jnp.where(kinds < 6, own_rows, jnp.where(kinds == 6, own_rows + halo_span, own_rows + 2 * halo_span))
    drawn = jax.random.randint(jax.random.fold_in(key, 17), (PARTITIONS * EB, BLOCK), lower, upper)
    row_ids = jnp.arange(PARTITIONS * EB)[:, None]
    column_ids = jnp.arange(BLOCK)[None, :]
    drawn = jnp.where((row_ids == 0) & (column_ids == 0), own_rows + 2 * halo_span - 1, drawn)
    drawn = jnp.where((row_ids == 0) & (column_ids == 1), 0, drawn)
    return drawn.astype(jnp.int32)


def draw_edge_recv(key, part):
    own_rows = NB * BLOCK
    drawn = jax.random.randint(jax.random.fold_in(key, 19), (PARTITIONS * EB, BLOCK), 0, own_rows)
    row_ids = jnp.arange(PARTITIONS * EB)[:, None]
    column_ids = jnp.arange(BLOCK)[None, :]
    drawn = jnp.where((row_ids == 0) & (column_ids == 0), own_rows - 1, drawn)
    drawn = jnp.where((row_ids == 0) & (column_ids == 1), 0, drawn)
    return drawn.astype(jnp.int32)


def draw_edge_count(key, part):
    heavy = jax.random.randint(jax.random.fold_in(key, 23), (PARTITIONS,), 0, 4) == 0
    device = jnp.arange(PARTITIONS * EB) // EB
    lower = jnp.where(heavy, BLOCK // 2, BLOCK // 4)[device]
    upper = jnp.where(heavy, BLOCK + 1, 3 * BLOCK // 4 + 1)[device]
    drawn = jax.random.randint(jax.random.fold_in(key, 29), (PARTITIONS * EB,), lower, upper)
    positions = jnp.arange(PARTITIONS * EB)
    drawn = jnp.where(positions == 0, BLOCK, drawn)
    drawn = jnp.where(positions == 1, 1, drawn)
    return drawn.astype(jnp.int32)


def block_scale(own_key, extent, pieces, smallest, top_value):
    level, own = 1.0, jax.random.fold_in(own_key, 6)
    for dim, blocks in pieces:
        steps = jnp.exp(jax.random.uniform(jax.random.fold_in(own, dim), (blocks,), jnp.float32, smallest / len(pieces), top_value / len(pieces)))
        level = level * jnp.repeat(steps, extent[dim] // blocks).reshape([-1 if axis == dim else 1 for axis in range(len(extent))])
    return level


def bell_draw(rng, shape, deviation, bound, cuts=(), kind=jnp.bfloat16):
    result = deviation * jax.random.normal(rng, shape, jnp.float32)
    if cuts:
        result = result * block_scale(rng, shape, cuts, -0.22, 0.18)
    return jnp.clip(result, -bound, bound).astype(kind)


def setup_inputs(seed: int = 0) -> dict:
    arg_keys = jax.random.split(jax.random.key(seed), 13)
    inputs = bell_draw(arg_keys[0], (MICRO, NODES, D), 1.0, 6.0, ((1, 8),))
    cotangent = bell_draw(arg_keys[1], (MICRO, NODES, D), 1.0, 6.0, ((1, 8),))
    w_send = bell_draw(arg_keys[2], (SECTIONS, D, D), D ** -0.5, 0.25, ((0, 4),))
    w_recv = bell_draw(arg_keys[3], (SECTIONS, D, D), D ** -0.5, 0.25, ((0, 4),))
    w_message = bell_draw(arg_keys[4], (SECTIONS, D, D), D ** -0.5, 0.25, ((0, 4),))
    w_node = bell_draw(arg_keys[5], (SECTIONS, D, D), D ** -0.5, 0.25, ((0, 4),))
    w_aggregate = bell_draw(arg_keys[6], (SECTIONS, D, D), D ** -0.5, 0.25, ((0, 4),))
    gains = jnp.clip(1.0 + 0.18 * jax.random.normal(arg_keys[7], (SECTIONS, D), jnp.float32), 0.1, 1.9)
    edge_send = draw_edge_send(jax.random.fold_in(arg_keys[12], 71), 0)
    edge_recv = draw_edge_recv(jax.random.fold_in(arg_keys[12], 71), 0)
    edge_count = draw_edge_count(jax.random.fold_in(arg_keys[12], 71), 0)
    halo_send = draw_halo_send(jax.random.fold_in(arg_keys[12], 71), 0)
    return dict(inputs=inputs, cotangent=cotangent, w_send=w_send, w_recv=w_recv, w_message=w_message, w_node=w_node, w_aggregate=w_aggregate, gains=gains, edge_send=edge_send, edge_recv=edge_recv, edge_count=edge_count, halo_send=halo_send)


EPSILON = 1e-05

def dot_plain(operand, matrix):
    return jnp.dot(operand, matrix, preferred_element_type=jnp.float32)

def dot_transposed(operand, matrix):
    return lax.dot_general(operand, matrix, (((1,), (1,)), ((), ())), preferred_element_type=jnp.float32)

def silu_slope(values):
    sigmoid_value = jax.nn.sigmoid(values)
    return sigmoid_value * (1.0 + values * (1.0 - sigmoid_value))

def normalize(activated):
    mean_value = lax.optimization_barrier(jnp.mean(activated, axis=-1, keepdims=True))
    centred = activated - mean_value
    variance = lax.optimization_barrier(jnp.mean(centred * centred, axis=-1, keepdims=True))
    scale_inverse = lax.rsqrt(variance + EPSILON)
    return (centred * scale_inverse, scale_inverse)

def edge_rows(edge_send, edge_recv, edge_count, halo_send):
    own_rows = NB * BLOCK
    halo_span = HB * BLOCK
    block_total = edge_send.shape[0]
    device = (jnp.arange(block_total, dtype=jnp.int32) // EB)[:, None]
    is_own = edge_send < own_rows
    is_prev = (edge_send >= own_rows) & (edge_send < own_rows + halo_span)
    offset = jnp.where(is_prev, edge_send - own_rows, edge_send - own_rows - halo_span)
    offset = jnp.clip(offset, 0, halo_span - 1)
    which_block = offset // BLOCK
    row_offset = offset % BLOCK
    prev_device = (device - 1) % PARTITIONS
    next_device = (device + 1) % PARTITIONS
    prev_block = halo_send[prev_device, 0, which_block]
    next_block = halo_send[next_device, 1, which_block]
    from_prev = prev_device * own_rows + prev_block * BLOCK + row_offset
    from_next = next_device * own_rows + next_block * BLOCK + row_offset
    senders = jnp.where(is_own, device * own_rows + edge_send, jnp.where(is_prev, from_prev, from_next))
    receivers = device * own_rows + edge_recv
    live_mask = jnp.arange(BLOCK, dtype=jnp.int32)[None, :] < edge_count[:, None]
    return (senders.reshape(-1).astype(jnp.int32), receivers.reshape(-1).astype(jnp.int32), live_mask.reshape(-1))

def layer_forward(hidden, matrices, senders, receivers, live_float):
    send_matrix, recv_matrix, message_matrix, node_matrix, aggregate_matrix = matrices
    projected = dot_plain(hidden, send_matrix).astype(jnp.bfloat16)
    recv_part = dot_plain(hidden, recv_matrix)
    pre_edge = jnp.take(projected, senders, axis=0).astype(jnp.float32) + jnp.take(recv_part, receivers, axis=0)
    edge_hidden = jax.nn.silu(pre_edge).astype(jnp.bfloat16)
    messages = dot_plain(edge_hidden, message_matrix) * live_float
    aggregate = jax.ops.segment_sum(messages, receivers, num_segments=hidden.shape[0]).astype(jnp.bfloat16)
    node_pre = dot_plain(hidden, node_matrix) + dot_plain(aggregate, aggregate_matrix)
    return (pre_edge, node_pre)

def layer_backward(upstream, pre_edge, node_pre, matrices, gain_row, senders, receivers, live_float):
    send_matrix, recv_matrix, message_matrix, node_matrix, aggregate_matrix = matrices
    row_total = node_pre.shape[0]
    unit, scale_inverse = normalize(jax.nn.silu(node_pre))
    upstream_float = upstream.astype(jnp.float32)
    grad_unit = upstream_float * gain_row
    grad_activated = scale_inverse * (grad_unit - lax.optimization_barrier(jnp.mean(grad_unit, axis=-1, keepdims=True)) - unit * lax.optimization_barrier(jnp.mean(grad_unit * unit, axis=-1, keepdims=True)))
    grad_node_pre = (grad_activated * silu_slope(node_pre)).astype(jnp.bfloat16)
    grad_aggregate = dot_transposed(grad_node_pre, aggregate_matrix).astype(jnp.bfloat16)
    grad_rows = upstream_float + dot_transposed(grad_node_pre, node_matrix)
    grad_message = jnp.take(grad_aggregate, receivers, axis=0) * live_float.astype(jnp.bfloat16)
    grad_edge = (dot_transposed(grad_message, message_matrix) * silu_slope(pre_edge)).astype(jnp.bfloat16)
    grad_rows = grad_rows + jax.ops.segment_sum(dot_transposed(grad_edge, recv_matrix), receivers, num_segments=row_total)
    grad_rows = grad_rows + jax.ops.segment_sum(dot_transposed(grad_edge, send_matrix), senders, num_segments=row_total)
    return grad_rows.astype(jnp.bfloat16)

def reference(inputs, cotangent, w_send, w_recv, w_message, w_node, w_aggregate, gains, edge_send, edge_recv, edge_count, halo_send):
    senders, receivers, live_mask = edge_rows(edge_send, edge_recv, edge_count, halo_send)
    live_float = live_mask.astype(jnp.float32)[:, None]
    phase_inputs = []
    outputs = []
    current = [inputs[position] for position in range(MICRO)]
    for section in range(SECTIONS):
        matrices = (w_send[section], w_recv[section], w_message[section], w_node[section], w_aggregate[section])
        phase_inputs.append(current)
        produced = []
        for micro_index in range(MICRO):
            hidden = current[micro_index]
            pre_edge, node_pre = layer_forward(hidden, matrices, senders, receivers, live_float)
            unit, scale_inverse = normalize(jax.nn.silu(node_pre))
            produced.append((hidden.astype(jnp.float32) + unit * gains[section]).astype(jnp.bfloat16))
        outputs.append(jnp.stack(produced))
        current = produced
    gradients = [None] * SECTIONS
    upstream_list = [cotangent[position] for position in range(MICRO)]
    for section in range(SECTIONS - 1, -1, -1):
        matrices = (w_send[section], w_recv[section], w_message[section], w_node[section], w_aggregate[section])
        results = []
        for micro_index in range(MICRO):
            hidden = phase_inputs[section][micro_index]
            pre_edge, node_pre = layer_forward(hidden, matrices, senders, receivers, live_float)
            results.append(layer_backward(upstream_list[micro_index], pre_edge, node_pre, matrices, gains[section], senders, receivers, live_float))
        gradients[section] = jnp.stack(results)
        upstream_list = results
    return (jnp.stack(outputs), jnp.stack(gradients))
```

```python
import functools

import jax
import jax.numpy as jnp
from jax import lax
from jax.experimental import pallas as pl
from jax.experimental.pallas import tpu as pltpu
from jax.sharding import PartitionSpec as P

EPSILON = 1e-05
F32 = jnp.float32
BF16 = jnp.bfloat16
AXES = ("dom", "pipe")
PIPE, A_NEXT, A_PREV, B_NEXT, B_PREV = range(5)


def mul(a, b):
    return jnp.dot(a, b, preferred_element_type=F32)


def mul_t(a, b):
    return lax.dot_general(a, b, (((1,), (1,)), ((), ())), preferred_element_type=F32)


def slope(v):
    s = jax.nn.sigmoid(v)
    return s * (1.0 + v * (1.0 - s))


def normalize(z):
    centred = z - jnp.mean(z, axis=-1, keepdims=True)
    inverse = lax.rsqrt(jnp.mean(centred * centred, axis=-1, keepdims=True) + EPSILON)
    return centred * inverse, inverse


def block_at(scalars, place, base, rows):
    return pl.ds(pl.multiple_of(base + scalars[place] * rows, rows), rows)


def fold_kernel(a, b, out):
    out[...] = mul(a[...], b[...]).astype(BF16)


def forward_own_kernel(tick, scalars, h, gown, ginner, w_send, w_recv, w_node, a_out, u_out):
    @pl.when(scalars[PIPE] == tick)
    def _():
        rows = h.shape[0] // 2
        edges = ginner.shape[1]
        block = ginner.shape[2]
        for i in range(2):
            own = mul(gown[i], h[i * rows : (i + 1) * rows, :])
            if i == 0:
                inner = h[block_at(scalars, B_PREV, rows, block), :]
            else:
                inner = h[block_at(scalars, A_NEXT, 0, block), :]
            sent = (own[:edges] + mul(ginner[i], inner)).astype(BF16)
            received = own[edges:].astype(BF16)
            a_out[i * edges : (i + 1) * edges, :] = mul(sent, w_send[...]) + mul(received, w_recv[...])
        u_out[...] = mul(h[...], w_node[...])


def forward_kernel(
    tick, scalars, h, a_own, u_own, prev, after, gouter, gown_t, w_send, w_fold, gain, h_out, to_prev, to_next, a_out, u_out
):
    @pl.when(scalars[PIPE] == tick)
    def _():
        rows = h.shape[0] // 2
        edges = gouter.shape[1]
        block = gouter.shape[2]
        outer = jnp.concatenate([mul(gouter[0], prev[...]), mul(gouter[1], after[...])], axis=0).astype(BF16)
        a = a_own[...] + mul(outer, w_send[...])
        a_out[...] = a
        q = (a * jax.nn.sigmoid(a)).astype(BF16)
        summed = jnp.concatenate(
            [mul(gown_t[i, :, edges:], q[i * edges : (i + 1) * edges]) for i in range(2)], axis=0
        ).astype(BF16)
        u = u_own[...] + mul(summed, w_fold[...])
        u_out[...] = u
        t, _ = normalize(u * jax.nn.sigmoid(u))
        h_out[...] = (h[...].astype(F32) + t * gain[...]).astype(BF16)
        to_prev[...] = h_out[block_at(scalars, A_PREV, 0, block), :]
        to_next[...] = h_out[block_at(scalars, B_NEXT, rows, block), :]


def save_kernel(tick, scalars, a, u, h, *refs):
    t_out, r_out, s_out, h_out = refs[-4:]

    @pl.when(scalars[PIPE] == tick)
    def _():
        s_out[...] = slope(a[...])
        u_value = u[...]
        t, inverse = normalize(u_value * jax.nn.sigmoid(u_value))
        t_out[...] = t
        r_out[...] = inverse * slope(u_value)
        h_out[...] = h[...]


def backward_kernel(
    tick,
    scalars,
    upstream,
    from_prev,
    from_next,
    t_in,
    r_in,
    s_in,
    gain,
    gown,
    gouter_t,
    w_fold,
    w_send,
    c_out,
    cb_out,
    du_out,
    da_out,
    es_out,
    to_prev,
    to_next,
):
    @pl.when(scalars[PIPE] == tick)
    def _():
        rows = upstream.shape[0] // 2
        edges = gouter_t.shape[2]
        block = gouter_t.shape[1]
        c_out[...] = upstream[...].astype(F32)
        if from_prev is not None:
            at = block_at(scalars, A_PREV, 0, block)
            c_out[at, :] = c_out[at, :] + from_prev[...].astype(F32)
            at = block_at(scalars, B_NEXT, rows, block)
            c_out[at, :] = c_out[at, :] + from_next[...].astype(F32)
            cb_out[...] = c_out[...].astype(BF16)
        g = c_out[...] * gain[...]
        t = t_in[...]
        centre = jnp.mean(g, axis=-1, keepdims=True)
        along = jnp.mean(g * t, axis=-1, keepdims=True)
        du = ((g - centre - t * along) * r_in[...]).astype(BF16)
        du_out[...] = du
        spread = jnp.concatenate(
            [mul(gown[i, edges:, :], du[i * rows : (i + 1) * rows]) for i in range(2)], axis=0
        ).astype(BF16)
        da = (mul_t(spread, w_fold[...]) * s_in[...]).astype(BF16)
        da_out[...] = da
        es = mul_t(da, w_send[...]).astype(BF16)
        es_out[...] = es
        to_prev[...] = mul(gouter_t[0], es[:edges]).astype(BF16)
        to_next[...] = mul(gouter_t[1], es[edges:]).astype(BF16)


def backward_own_kernel(
    tick, scalars, c, du, da, es, gown_t, ginner_t, w_node, w_recv, out, total
):
    @pl.when(scalars[PIPE] == tick)
    def _():
        rows = c.shape[0] // 2
        edges = ginner_t.shape[2]
        block = ginner_t.shape[1]
        er = mul_t(da[...], w_recv[...]).astype(BF16)
        direct = mul_t(du[...], w_node[...])
        for i in range(2):
            here = slice(i * rows, (i + 1) * rows)
            there = slice(i * edges, (i + 1) * edges)
            both = jnp.concatenate([es[there, :], er[there]], axis=0)
            total[here, :] = c[here, :] + direct[here] + mul(gown_t[i], both)
        at = block_at(scalars, B_PREV, rows, block)
        total[at, :] = total[at, :] + mul(ginner_t[0], es[:edges, :])
        at = block_at(scalars, A_NEXT, 0, block)
        total[at, :] = total[at, :] + mul(ginner_t[1], es[edges:, :])
        out[...] = total[...].astype(BF16)


def run(kernel, operands, outs, scratch=(), aliases=None, flops=0):
    specs = [pl.BlockSpec(memory_space=pltpu.SMEM)] + [pl.BlockSpec(memory_space=pltpu.VMEM)] * (len(operands) - 1)
    return pl.pallas_call(
        kernel,
        out_shape=[jax.ShapeDtypeStruct(s, t) for s, t in outs],
        in_specs=specs,
        out_specs=[pl.BlockSpec(memory_space=pltpu.VMEM)] * len(outs),
        scratch_shapes=list(scratch),
        input_output_aliases=aliases or {},
        compiler_params=pltpu.CompilerParams(vmem_limit_bytes=24 * 2**20),
        cost_estimate=pl.CostEstimate(flops=flops, bytes_accessed=2**20, transcendentals=0),
    )(*operands)


def shards(
    inputs,
    cotangent,
    w_send,
    w_recv,
    w_message,
    w_node,
    w_aggregate,
    gains,
    edge_send,
    edge_recv,
    edge_count,
    halo_send,
):
    sections = lax.axis_size("pipe")
    last = sections - 1
    pairs_total = lax.axis_size("dom") // 2
    phase = lax.axis_index("pipe")
    y = lax.rem(lax.axis_index("dom"), 2)
    rows, latent = inputs.shape[1:]
    edge_blocks, block = edge_send.shape
    edges = edge_blocks * block
    w_send, w_recv, w_node = w_send[0], w_recv[0], w_node[0]

    def device(pair, which, pipe):
        return (2 * (pair % pairs_total) + which) * sections + pipe

    def table(rule):
        pairs = []
        for pair in range(pairs_total):
            for which in range(2):
                for pipe in range(sections):
                    target = rule(pair, which, pipe)
                    if target is not None and 0 <= target[2] < sections:
                        pairs.append((device(pair, which, pipe), device(*target)))
        return pairs

    def send(value, rule):
        return lax.ppermute(value, AXES, table(rule))

    numbers = jnp.concatenate([edge_count, halo_send[0, :, 0]])
    packed = jnp.concatenate(
        [edge_send, edge_recv, jnp.pad(numbers, (0, block - numbers.shape[0]))[None]], axis=0
    )
    packed_other = send(packed, lambda z, w, p: (z, 1 - w, p))

    source = jnp.where(phase == last, cotangent, inputs)
    here = lax.dynamic_index_in_dim(source, y, 0, keepdims=False)
    there = lax.dynamic_index_in_dim(source, 1 - y, 0, keepdims=False)
    out_block = jnp.where(y == 1, halo_send[0, 0, 0], halo_send[0, 1, 0])
    boundary = lax.dynamic_slice(inputs, (jnp.minimum(phase, 1), out_block * block, 0), (1, block, latent))[0]
    start_prev = send(boundary, lambda z, w, p: (z + 1, p, 0) if w == 1 and p <= 1 else None)
    start_next = send(boundary, lambda z, w, p: (z - 1, p, 0) if w == 0 and p <= 1 else None)
    arrived = send(there, lambda z, w, p: (z, 1 - w, p) if p in (0, last) else None)
    start = jnp.where(
        y == 0, jnp.concatenate([here, arrived], axis=0), jnp.concatenate([arrived, here], axis=0)
    )

    first = jnp.where(y == 0, packed, packed_other)
    second = jnp.where(y == 0, packed_other, packed)
    both = jnp.stack([first, second])
    senders = both[:, :edge_blocks].reshape(2, edges)
    receivers = both[:, edge_blocks : 2 * edge_blocks].reshape(2, edges)
    counts = both[:, 2 * edge_blocks, :edge_blocks]
    lists = both[:, 2 * edge_blocks, edge_blocks : edge_blocks + 2]
    live = (jnp.arange(block)[None, None, :] < counts[:, :, None]).reshape(2, edges)
    senders = jnp.where(live, senders, -1)
    receivers = jnp.where(live, receivers, -1)
    scalars = jnp.concatenate([phase[None], lists.reshape(-1)]).astype(jnp.int32)

    inner_base = jnp.array([rows + block, rows], jnp.int32)[:, None]
    outer_base = jnp.array([rows, rows + block], jnp.int32)[:, None]

    def one_hot(index, width):
        return (index[:, :, None] == jnp.arange(width, dtype=jnp.int32)).astype(BF16)

    def one_hot_t(index, width):
        return (index[:, None, :] == jnp.arange(width, dtype=jnp.int32)[None, :, None]).astype(BF16)

    gown = one_hot(jnp.concatenate([senders, receivers], axis=1), rows)
    gown_t = one_hot_t(jnp.concatenate([senders, receivers], axis=1), rows)
    ginner = one_hot(senders - inner_base, block)
    ginner_t = one_hot_t(senders - inner_base, block)
    gouter = one_hot(senders - outer_base, block)
    gouter_t = one_hot_t(senders - outer_base, block)

    wide = (2 * rows, latent)
    edge_wide = (2 * edges, latent)
    narrow = (block, latent)
    unit = 2 * 2 * rows * latent * latent

    w_fold = pl.pallas_call(
        fold_kernel,
        out_shape=jax.ShapeDtypeStruct(w_message.shape[1:], BF16),
        in_specs=[pl.BlockSpec(memory_space=pltpu.VMEM)] * 2,
        out_specs=pl.BlockSpec(memory_space=pltpu.VMEM),
        compiler_params=pltpu.CompilerParams(vmem_limit_bytes=24 * 2**20),
    )(w_message[0], w_aggregate[0])

    hidden, from_prev, from_next = start, start_prev, start_next
    state = ()
    for tick in range(sections):
        a_own, u_own = run(
            functools.partial(forward_own_kernel, tick),
            (scalars, hidden, gown, ginner, w_send, w_recv, w_node),
            [(edge_wide, F32), (wide, F32)],
            flops=4 * unit,
        )
        hidden, to_prev, to_next, a, u = run(
            functools.partial(forward_kernel, tick),
            (scalars, hidden, a_own, u_own, from_prev, from_next, gouter, gown_t, w_send, w_fold, gains),
            [(wide, BF16), (narrow, BF16), (narrow, BF16), (edge_wide, F32), (wide, F32)],
            flops=4 * unit,
        )
        produced = hidden
        if tick < last:
            from_next = send(to_prev, lambda z, w, p: (z - 1, w, p + 1) if p == tick else None)
            from_prev = send(to_next, lambda z, w, p: (z + 1, w, p + 1) if p == tick else None)
            hidden = send(hidden, lambda z, w, p: (z, w, p + 1) if p == tick else None)
        state = run(
            functools.partial(save_kernel, tick),
            (scalars, a, u, produced) + tuple(state),
            [(wide, F32), (wide, F32), (edge_wide, F32), (wide, BF16)],
            aliases={4 + k: k for k in range(4)} if state else None,
        )
    t_saved, r_saved, s_saved, h_saved = state

    upstream = start
    from_prev = from_next = None
    returned = jnp.zeros(wide, BF16)
    for tick in range(last, -1, -1):
        operands = (t_saved, r_saved, s_saved, gains, gown, gouter_t, w_fold, w_send)
        outs = [
            (wide, F32),
            (wide, BF16),
            (wide, BF16),
            (edge_wide, BF16),
            (edge_wide, BF16),
            (narrow, BF16),
            (narrow, BF16),
        ]
        if from_prev is None:

            def body(scalars, upstream, *refs, tick=tick):
                backward_kernel(tick, scalars, upstream, None, None, *refs)

            c, cb, du, da, es, to_prev, to_next = run(body, (scalars, upstream) + operands, outs, flops=4 * unit)
        else:
            c, cb, du, da, es, to_prev, to_next = run(
                functools.partial(backward_kernel, tick),
                (scalars, upstream, from_prev, from_next) + operands,
                outs,
                flops=4 * unit,
            )
            back = send(cb, lambda z, w, p: (z, w, p + 1) if p == tick else None)
            returned = jnp.where(phase == tick + 1, back, returned)
        [own] = run(
            functools.partial(backward_own_kernel, tick),
            (scalars, c, du, da, es, gown_t, ginner_t, w_node, w_recv),
            [(wide, BF16)],
            scratch=[pltpu.VMEM(wide, F32)],
            flops=4 * unit,
        )
        if tick > 0:
            from_next = send(to_prev, lambda z, w, p: (z - 1, w, p - 1) if p == tick else None)
            from_prev = send(to_next, lambda z, w, p: (z + 1, w, p - 1) if p == tick else None)
            upstream = send(own, lambda z, w, p: (z, w, p - 1) if p == tick else None)

    across = jnp.where(y == 0, to_prev, to_next)
    along = jnp.where(y == 0, to_next, to_prev)
    across = send(across, lambda z, w, p: None if p else (z - 1, 1, 0) if w == 0 else (z + 1, 0, 0))
    along = send(along, lambda z, w, p: None if p else (z + 1, 0, 0) if w == 0 else (z - 1, 1, 0))

    def mine(value):
        return lax.dynamic_slice(value, (y * rows, 0), (rows, latent))

    def others(value):
        return lax.dynamic_slice(value, ((1 - y) * rows, 0), (rows, latent))

    def swap(value):
        return send(others(value), lambda z, w, p: (z, 1 - w, p))

    h_other = swap(h_saved)
    final = jnp.where(phase == 0, own, returned)
    g_other = swap(final)
    g_mine = mine(final)
    at = jnp.where(y == 1, halo_send[0, 0, 0], halo_send[0, 1, 0])
    covered = ((jnp.arange(rows) // block == at) & (phase == 0))[:, None]

    def place(value, halo):
        tiled = jnp.concatenate([halo] * (rows // block), axis=0)
        return (value.astype(F32) + jnp.where(covered, tiled.astype(F32), 0.0)).astype(BF16)

    g_mine = place(g_mine, along)
    g_other = place(g_other, across)

    def by_micro(value, other):
        return jnp.where(y == 0, jnp.stack([value, other]), jnp.stack([other, value]))[None]

    return by_micro(mine(h_saved), h_other), by_micro(g_mine, g_other)


def solution(mesh):
    in_specs = (
        P(None, "dom", None),
        P(None, "dom", None),
        P("pipe", None, None),
        P("pipe", None, None),
        P("pipe", None, None),
        P("pipe", None, None),
        P("pipe", None, None),
        P("pipe", None),
        P("dom", None),
        P("dom", None),
        P("dom"),
        P("dom", None, None),
    )
    out_specs = (P("pipe", None, "dom", None), P("pipe", None, "dom", None))
    return jax.shard_map(shards, mesh=mesh, in_specs=in_specs, out_specs=out_specs, check_vma=False)
```

```python
import functools

import jax
import jax.numpy as jnp
from jax import lax
from jax.experimental import pallas as pl
from jax.experimental.pallas import tpu as pltpu
from jax.sharding import PartitionSpec as P

EPSILON = 1e-05
F32 = jnp.float32
BF16 = jnp.bfloat16
AXES = ("dom", "pipe")
INNER, OUTER = 0, 1


def mul(a, b):
    return jnp.dot(a, b, preferred_element_type=F32)


def mul_t(a, b):
    return lax.dot_general(a, b, (((1,), (1,)), ((), ())), preferred_element_type=F32)


def slope(v):
    s = jax.nn.sigmoid(v)
    return s * (1.0 + v * (1.0 - s))


def normalize(z):
    centred = z - jnp.mean(z, axis=-1, keepdims=True)
    inverse = lax.rsqrt(jnp.mean(centred * centred, axis=-1, keepdims=True) + EPSILON)
    return centred * inverse, inverse


def on_plane(plane):
    return pl.when(lax.axis_index("pipe") // 2 == plane)


def listed(lists, side, value, block):
    at = lists[side : side + 1, :1]
    picked = value[:block]
    for number in range(1, value.shape[0] // block):
        picked = jnp.where(at == number, value[number * block : (number + 1) * block], picked)
    return picked


def add_listed(lists, side, target, value, block):
    at = lists[side : side + 1, :1]
    for number in range(target.shape[0] // block):
        rows = slice(number * block, (number + 1) * block)
        target[rows, :] = target[rows, :] + jnp.where(at == number, value, 0.0)


def fold_kernel(a, b, out):
    out[...] = mul(a[...], b[...]).astype(BF16)


def forward_own_kernel(plane, h, gown, w_send, w_recv, w_node, a_out, u_out):
    @on_plane(plane)
    def _():
        edges = gown.shape[0] // 2
        own = mul(gown[...], h[...]).astype(BF16)
        a_out[...] = mul(own[:edges], w_send[...]) + mul(own[edges:], w_recv[...])
        u_out[...] = mul(h[...], w_node[...])


def forward_kernel(
    plane, lists, h, a_own, u_own, inner, outer, ghalo, gown_t, w_send, w_fold, gain, h_out, to_inner, to_outer, a_out, u_out
):
    @on_plane(plane)
    def _():
        edges = ghalo.shape[0]
        block = inner.shape[0]
        halo = (mul(ghalo[:, :block], inner[...]) + mul(ghalo[:, block:], outer[...])).astype(BF16)
        a = a_own[...] + mul(halo, w_send[...])
        a_out[...] = a
        q = (a * jax.nn.sigmoid(a)).astype(BF16)
        u = u_own[...] + mul(mul(gown_t[:, edges:], q).astype(BF16), w_fold[...])
        u_out[...] = u
        t, _ = normalize(u * jax.nn.sigmoid(u))
        out = (h[...].astype(F32) + t * gain[...]).astype(BF16)
        h_out[...] = out
        to_inner[...] = listed(lists, INNER, out, block)
        to_outer[...] = listed(lists, OUTER, out, block)


def save_kernel(plane, a, u, h, *refs):
    t_out, r_out, s_out, h_out = refs[-4:]

    @on_plane(plane)
    def _():
        s_out[...] = slope(a[...])
        u_value = u[...]
        t, inverse = normalize(u_value * jax.nn.sigmoid(u_value))
        t_out[...] = t
        r_out[...] = inverse * slope(u_value)
        h_out[...] = h[...]


def backward_kernel(
    plane,
    lists,
    upstream,
    inner,
    outer,
    t_in,
    r_in,
    s_in,
    gain,
    gown,
    ghalo_t,
    w_fold,
    w_send,
    c_out,
    cb_out,
    du_out,
    da_out,
    es_out,
    to_inner,
    to_outer,
):
    @on_plane(plane)
    def _():
        edges = gown.shape[0] // 2
        block = to_inner.shape[0]
        c_out[...] = upstream[...].astype(F32)
        if inner is not None:
            add_listed(lists, INNER, c_out, inner[...].astype(F32), block)
            add_listed(lists, OUTER, c_out, outer[...].astype(F32), block)
            cb_out[...] = c_out[...].astype(BF16)
        g = c_out[...] * gain[...]
        t = t_in[...]
        centre = jnp.mean(g, axis=-1, keepdims=True)
        along = jnp.mean(g * t, axis=-1, keepdims=True)
        du = ((g - centre - t * along) * r_in[...]).astype(BF16)
        du_out[...] = du
        spread = mul(gown[edges:, :], du).astype(BF16)
        da = (mul_t(spread, w_fold[...]) * s_in[...]).astype(BF16)
        da_out[...] = da
        es = mul_t(da, w_send[...]).astype(BF16)
        es_out[...] = es
        halo = mul(ghalo_t[...], es).astype(BF16)
        to_inner[...] = halo[:block]
        to_outer[...] = halo[block:]


def backward_own_kernel(plane, c, du, da, es, gown_t, w_node, w_recv, out, out_half):
    @on_plane(plane)
    def _():
        er = mul_t(da[...], w_recv[...]).astype(BF16)
        both = jnp.concatenate([es[...], er], axis=0)
        total = c[...] + mul_t(du[...], w_node[...]) + mul(gown_t[...], both)
        out[...] = total
        out_half[...] = total.astype(BF16)


def run(kernel, operands, outs, aliases=None, flops=0):
    return pl.pallas_call(
        kernel,
        out_shape=[jax.ShapeDtypeStruct(s, t) for s, t in outs],
        in_specs=[pl.BlockSpec(memory_space=pltpu.VMEM)] * len(operands),
        out_specs=[pl.BlockSpec(memory_space=pltpu.VMEM)] * len(outs),
        input_output_aliases=aliases or {},
        compiler_params=pltpu.CompilerParams(vmem_limit_bytes=24 * 2**20),
        cost_estimate=pl.CostEstimate(flops=flops, bytes_accessed=2**20, transcendentals=0),
    )(*operands)


def shards(
    inputs,
    cotangent,
    w_send,
    w_recv,
    w_message,
    w_node,
    w_aggregate,
    gains,
    edge_send,
    edge_recv,
    edge_count,
    halo_send,
):
    sections = lax.axis_size("pipe")
    pairs_total = lax.axis_size("dom") // 2
    phase = lax.axis_index("pipe")
    y = lax.rem(lax.axis_index("dom"), 2)
    core = lax.rem(phase, 2)
    plane_here = phase // 2
    rows, latent = inputs.shape[1:]
    edge_blocks, block = edge_send.shape
    edges = edge_blocks * block

    def send(value, rule):
        table = []
        for z in range(pairs_total):
            for which in range(2):
                for x in range(sections // 2):
                    for c in range(2):
                        tz, ty, tx, tc = rule(z, which, x, c)
                        target = (2 * (tz % pairs_total) + ty) * sections + 2 * (tx % (sections // 2)) + tc
                        table.append(((2 * z + which) * sections + 2 * x + c, target))
        return lax.ppermute(value, AXES, table)

    def flip_y(value):
        return send(value, lambda z, y, x, c: (z, 1 - y, x, c))

    def flip_core(value):
        return send(value, lambda z, y, x, c: (z, y, x, 1 - c))

    def to_home(value):
        return send(value, lambda z, y, x, c: (z, c, x, y))

    def towards(value, side, step):
        if side == INNER:
            return send(value, lambda z, y, x, c: (z, y, x + step, 1 - c))
        return send(value, lambda z, y, x, c: (z + 2 * c - 1, y, x + step, 1 - c))

    first_list = halo_send[0, :, 0]
    out_block = jnp.where(y == 1, first_list[0], first_list[1])
    boundary = lax.dynamic_slice(inputs, (core, out_block * block, 0), (1, block, latent))[0]
    numbers = jnp.concatenate([edge_count, first_list])
    packed = jnp.concatenate(
        [edge_send, edge_recv, jnp.pad(numbers, (0, block - numbers.shape[0]))[None]], axis=0
    )
    here = lax.dynamic_index_in_dim(inputs, y, 0, keepdims=False)
    there = flip_y(lax.dynamic_index_in_dim(inputs, 1 - y, 0, keepdims=False))
    outer = send(boundary, lambda z, y, x, c: (z + 2 * y - 1, c, x, 1 - y))
    packed_there = flip_y(packed)
    grad_here = lax.dynamic_index_in_dim(cotangent, y, 0, keepdims=False)
    grad_there = flip_y(lax.dynamic_index_in_dim(cotangent, 1 - y, 0, keepdims=False))

    local = core == y
    hidden = jnp.where(local, here, there)
    mine = jnp.where(local, packed, packed_there)
    mate = jnp.where(local, packed_there, packed)
    last_row = 2 * edge_blocks
    mate_list = jnp.where(core == 0, mate[last_row, edge_blocks + 1], mate[last_row, edge_blocks])
    inner = lax.dynamic_slice(jnp.where(local, there, here), (mate_list * block, 0), (block, latent))

    live = (jnp.arange(block)[None, :] < mine[last_row, :edge_blocks][:, None]).reshape(edges)
    senders = jnp.where(live, mine[:edge_blocks].reshape(edges), -1)
    receivers = jnp.where(live, mine[edge_blocks:last_row].reshape(edges), -1)
    list_next, list_prev = mine[last_row, edge_blocks], mine[last_row, edge_blocks + 1]
    sides = jnp.where(core == 0, jnp.stack([list_next, list_prev]), jnp.stack([list_prev, list_next]))
    lists = jnp.broadcast_to(sides[:, None], (2, block))

    halo_at = senders - rows
    halo_at = jnp.where(halo_at >= 0, jnp.where(core == 0, (halo_at + block) % (2 * block), halo_at), -1)
    own_at = jnp.concatenate([senders, receivers])

    def one_hot(index, width):
        return (index[:, None] == jnp.arange(width, dtype=jnp.int32)[None, :]).astype(BF16)

    def one_hot_t(index, width):
        return (index[None, :] == jnp.arange(width, dtype=jnp.int32)[:, None]).astype(BF16)

    gown = one_hot(own_at, rows)
    gown_t = one_hot_t(own_at, rows)
    ghalo = one_hot(halo_at, 2 * block)
    ghalo_t = one_hot_t(halo_at, 2 * block)

    [w_fold] = run(fold_kernel, (w_message[0], w_aggregate[0]), [(w_message.shape[1:], BF16)])
    weights = (w_send[0], w_recv[0], w_node[0], w_fold, gains)
    swapped = [flip_core(value) for value in weights]
    even = [jnp.where(core == 0, a, b) for a, b in zip(weights, swapped)]
    odd = [jnp.where(core == 0, b, a) for a, b in zip(weights, swapped)]

    wide = (rows, latent)
    edge_wide = (edges, latent)
    narrow = (block, latent)
    unit = 2 * rows * latent * latent

    saved = [(), ()]
    for tick in range(sections):
        plane, parity = tick // 2, tick % 2
        send_w, recv_w, node_w, fold_w, gain = (even, odd)[parity]
        a_own, u_own = run(
            functools.partial(forward_own_kernel, plane),
            (hidden, gown, send_w, recv_w, node_w),
            [(edge_wide, F32), (wide, F32)],
            flops=4 * unit,
        )
        hidden, to_inner, to_outer, a, u = run(
            functools.partial(forward_kernel, plane),
            (lists, hidden, a_own, u_own, inner, outer, ghalo, gown_t, send_w, fold_w, gain),
            [(wide, BF16), (narrow, BF16), (narrow, BF16), (edge_wide, F32), (wide, F32)],
            flops=4 * unit,
        )
        produced = hidden
        if tick < sections - 1:
            step = (tick + 1) // 2 - plane
            outer = towards(to_outer, OUTER, step)
            inner = towards(to_inner, INNER, step)
            if step:
                hidden = send(hidden, lambda z, y, x, c: (z, y, x + 1, c))
        saved[parity] = run(
            functools.partial(save_kernel, plane),
            (a, u, produced) + tuple(saved[parity]),
            [(wide, F32), (wide, F32), (edge_wide, F32), (wide, BF16)],
            aliases={3 + k: k for k in range(4)} if saved[parity] else None,
            flops=unit,
        )

    upstream = jnp.where(local, grad_here, grad_there)
    inner = outer = None
    finished = [None] * sections
    for tick in range(sections - 1, -1, -1):
        plane, parity = tick // 2, tick % 2
        send_w, recv_w, node_w, fold_w, gain = (even, odd)[parity]
        operands = tuple(saved[parity][:3]) + (gain, gown, ghalo_t, fold_w, send_w)
        outs = [
            (wide, F32),
            (wide, BF16),
            (wide, BF16),
            (edge_wide, BF16),
            (edge_wide, BF16),
            (narrow, BF16),
            (narrow, BF16),
        ]
        if inner is None:

            def body(lists, upstream, *refs, plane=plane):
                backward_kernel(plane, lists, upstream, None, None, *refs)

            c, cb, du, da, es, to_inner, to_outer = run(body, (lists, upstream) + operands, outs, flops=4 * unit)
        else:
            c, cb, du, da, es, to_inner, to_outer = run(
                functools.partial(backward_kernel, plane),
                (lists, upstream, inner, outer) + operands,
                outs,
                flops=4 * unit,
            )
            finished[tick + 1] = cb
        if tick > 0:
            step = (tick - 1) // 2 - plane
            outer = towards(to_outer, OUTER, step)
            inner = towards(to_inner, INNER, step)
        upstream, own_half = run(
            functools.partial(backward_own_kernel, plane),
            (c, du, da, es, gown_t, node_w, recv_w),
            [(wide, F32), (wide, BF16)],
            flops=4 * unit,
        )
        if tick > 0 and step:
            upstream = send(own_half, lambda z, y, x, c: (z, y, x + 1, c))

    def both_micro(evens, odds):
        swap = flip_core(jnp.where(core == 1, evens, odds))
        return jnp.where(core == 0, jnp.stack([evens, swap]), jnp.stack([swap, odds]))[None]

    section_out = both_micro(to_home(saved[0][3]), to_home(saved[1][3]))

    odds = to_home(jnp.where(plane_here == 0, finished[1], finished[3]))
    second = send(finished[2], lambda z, y, x, c: (z, y, x + 1, c))
    final_outer = send(to_outer, lambda z, y, x, c: (z + 2 * c - 1, 1 - c, x, y))
    final_inner = send(to_inner, lambda z, y, x, c: (z, 1 - c, x, y))
    evens = to_home(jnp.where(plane_here == 0, own_half, second))

    def added(value, side, halo):
        at = jnp.where((y == 0) == (side == INNER), first_list[0], first_list[1])
        covered = ((jnp.arange(rows) // block == at) & (plane_here == 0))[:, None]
        return value + jnp.where(covered, jnp.concatenate([halo] * (rows // block), axis=0).astype(F32), 0.0)

    evens = added(added(evens.astype(F32), INNER, final_inner), OUTER, final_outer).astype(BF16)
    return section_out, both_micro(evens, odds)


def solution(mesh):
    in_specs = (
        P(None, "dom", None),
        P(None, "dom", None),
        P("pipe", None, None),
        P("pipe", None, None),
        P("pipe", None, None),
        P("pipe", None, None),
        P("pipe", None, None),
        P("pipe", None),
        P("dom", None),
        P("dom", None),
        P("dom"),
        P("dom", None, None),
    )
    out_specs = (P("pipe", None, "dom", None), P("pipe", None, "dom", None))
    return jax.shard_map(shards, mesh=mesh, in_specs=in_specs, out_specs=out_specs, check_vma=False)
```

```python
import functools

import jax
import jax.numpy as jnp
from jax import lax
from jax.experimental import pallas as pl
from jax.experimental.pallas import tpu as pltpu
from jax.sharding import PartitionSpec as P

EPSILON = 1e-05
F32 = jnp.float32
BF16 = jnp.bfloat16
AXES = ("dom", "pipe")
INNER, OUTER = 0, 1


def mul(a, b):
    return jnp.dot(a, b, preferred_element_type=F32)


def mul_t(a, b):
    return lax.dot_general(a, b, (((1,), (1,)), ((), ())), preferred_element_type=F32)


def slope(v):
    s = jax.nn.sigmoid(v)
    return s * (1.0 + v * (1.0 - s))


def normalize(z):
    centred = z - jnp.mean(z, axis=-1, keepdims=True)
    inverse = lax.rsqrt(jnp.mean(centred * centred, axis=-1, keepdims=True) + EPSILON)
    return centred * inverse, inverse


def here_is(plane=None, parity=None):
    pipe = lax.axis_index("pipe")
    wanted = jnp.bool_(True)
    if plane is not None:
        wanted = pipe // 2 == plane
    if parity is not None:
        wanted = wanted & (pipe % 2 == parity)
    return wanted


def is_local():
    return lax.axis_index("pipe") % 2 == lax.axis_index("dom") % 2


def listed(at, value, block):
    picked = value[:block]
    for number in range(1, value.shape[0] // block):
        picked = jnp.where(at == number, value[number * block : (number + 1) * block], picked)
    return picked


def add_listed(at, target, value, block):
    for number in range(target.shape[0] // block):
        rows = slice(number * block, (number + 1) * block)
        target[rows, :] = target[rows, :] + jnp.where(at == number, value, 0.0)


def rows_kernel(inputs, here, there, sems):
    micro = lax.axis_index("dom") % 2
    first = pltpu.make_async_copy(inputs.at[1 - micro], there, sems.at[0])
    second = pltpu.make_async_copy(inputs.at[micro], here, sems.at[1])
    first.start()
    second.start()
    first.wait()
    second.wait()


def boundary_kernel(lists, inputs, out, sem):
    block = out.shape[0]
    number = jnp.where(lax.axis_index("dom") % 2 == 1, lists[0], lists[1])
    start = pl.multiple_of(number * block, block)
    copy = pltpu.make_async_copy(inputs.at[lax.axis_index("pipe") % 2, pl.ds(start, block), :], out, sem)
    copy.start()
    copy.wait()


def graph_kernel(edge_blocks, packed, packed_there, gown, gown_t, ghalo, ghalo_t, lists, mate):
    block = packed.shape[1]
    rows = gown_t.shape[0]
    edges = edge_blocks * block
    first_core = lax.axis_index("pipe") % 2 == 0
    mine = jnp.where(is_local(), packed[...], packed_there[...])
    other = jnp.where(is_local(), packed_there[...], packed[...])
    tail = 2 * edge_blocks
    lane = lax.broadcasted_iota(jnp.int32, (1, block), 1)
    row = lax.broadcasted_iota(jnp.int32, (rows, block), 0)
    halo_row = lax.broadcasted_iota(jnp.int32, (2 * block, block), 0)
    for number in range(edge_blocks):
        live = lane < mine[tail : tail + 1, number : number + 1]
        sender = jnp.where(live, mine[number : number + 1], -1)
        receiver = jnp.where(live, mine[edge_blocks + number : edge_blocks + number + 1], -1)
        halo = sender - rows
        turned = jnp.where(halo < block, halo + block, halo - block)
        halo = jnp.where(halo >= 0, jnp.where(first_core, turned, halo), -1)
        here = slice(number * block, (number + 1) * block)
        received = slice(edges + number * block, edges + (number + 1) * block)
        for index, at, table, table_t in (
            (sender, here, gown, gown_t),
            (receiver, received, gown, gown_t),
            (halo, here, ghalo, ghalo_t),
        ):
            hot = (index == (halo_row if table is ghalo else row)).astype(F32)
            table_t[:, at] = hot.astype(BF16)
            table[at, :] = hot.T.astype(BF16)
    to_next, to_prev = mine[tail : tail + 1, edge_blocks : edge_blocks + 1], mine[tail : tail + 1, edge_blocks + 1 : edge_blocks + 2]
    lists[0:1, :] = jnp.broadcast_to(jnp.where(first_core, to_next, to_prev), (1, block))
    lists[1:2, :] = jnp.broadcast_to(jnp.where(first_core, to_prev, to_next), (1, block))
    to_next, to_prev = other[tail : tail + 1, edge_blocks : edge_blocks + 1], other[tail : tail + 1, edge_blocks + 1 : edge_blocks + 2]
    mate[...] = jnp.broadcast_to(jnp.where(first_core, to_prev, to_next), (1, block))


def entry_kernel(mate, here, there, hidden, inner):
    block = inner.shape[0]

    @pl.when(is_local())
    def _():
        hidden[...] = here[...]
        inner[...] = listed(mate[:, :1], there[...], block)

    @pl.when(jnp.logical_not(is_local()))
    def _():
        hidden[...] = there[...]
        inner[...] = listed(mate[:, :1], here[...], block)


def local_kernel(here, there, out):
    @pl.when(is_local())
    def _():
        out[...] = here[...]

    @pl.when(jnp.logical_not(is_local()))
    def _():
        out[...] = there[...]


def fold_kernel(a, b, out):
    out[...] = mul(a[...], b[...]).astype(BF16)


def forward_own_kernel(take, h, gown, a_out, u_out):
    w_send, w_recv, w_node, _, _ = take
    edges = gown.shape[0] // 2
    own = mul(gown[...], h[...]).astype(BF16)
    a_out[...] = mul(own[:edges], w_send[...]) + mul(own[edges:], w_recv[...])
    u_out[...] = mul(h[...], w_node[...])


def forward_kernel(take, lists, h, a_own, u_own, inner, outer, ghalo, gown_t, h_out, a_out, u_out, *to):
    w_send, _, _, w_fold, gain = take
    edges = ghalo.shape[0]
    block = inner.shape[0]
    halo = (mul(ghalo[:, :block], inner[...]) + mul(ghalo[:, block:], outer[...])).astype(BF16)
    a = a_own[...] + mul(halo, w_send[...])
    a_out[...] = a
    q = (a * jax.nn.sigmoid(a)).astype(BF16)
    u = u_own[...] + mul(mul(gown_t[:, edges:], q).astype(BF16), w_fold[...])
    u_out[...] = u
    t, _ = normalize(u * jax.nn.sigmoid(u))
    out = (h[...].astype(F32) + t * gain[...]).astype(BF16)
    h_out[...] = out
    for side, ref in enumerate(to):
        ref[...] = listed(lists[side : side + 1, :1], out, block)


def save_kernel(plane, a, u, h, *refs):
    t_out, r_out, s_out, h_out = refs[-4:]

    @pl.when(here_is(plane))
    def _():
        s_out[...] = slope(a[...])
        u_value = u[...]
        t, inverse = normalize(u_value * jax.nn.sigmoid(u_value))
        t_out[...] = t
        r_out[...] = inverse * slope(u_value)
        h_out[...] = h[...]


def backward_kernel(halo_in, finish, take, lists, upstream, *refs):
    w_send, _, _, w_fold, gain = take
    if halo_in:
        inner, outer, *refs = refs
    t_in, r_in, s_in, gown, ghalo_t, c_out, du_out, da_out, es_out, to_inner, to_outer, *rest = refs
    edges = gown.shape[0] // 2
    block = to_inner.shape[0]
    c_out[...] = upstream[...].astype(F32)
    if halo_in:
        add_listed(lists[INNER : INNER + 1, :1], c_out, inner[...].astype(F32), block)
        add_listed(lists[OUTER : OUTER + 1, :1], c_out, outer[...].astype(F32), block)
    if finish:
        rest[0][...] = c_out[...].astype(BF16)
    g = c_out[...] * gain[...]
    t = t_in[...]
    centre = jnp.mean(g, axis=-1, keepdims=True)
    along = jnp.mean(g * t, axis=-1, keepdims=True)
    du = ((g - centre - t * along) * r_in[...]).astype(BF16)
    du_out[...] = du
    spread = mul(gown[edges:, :], du).astype(BF16)
    da = (mul_t(spread, w_fold[...]) * s_in[...]).astype(BF16)
    da_out[...] = da
    es = mul_t(da, w_send[...]).astype(BF16)
    es_out[...] = es
    halo = mul(ghalo_t[...], es).astype(BF16)
    to_inner[...] = halo[:block]
    to_outer[...] = halo[block:]


def backward_own_kernel(take, c, du, da, es, gown_t, out):
    _, w_recv, w_node, _, _ = take
    er = mul_t(da[...], w_recv[...]).astype(BF16)
    both = jnp.concatenate([es[...], er], axis=0)
    total = c[...] + mul_t(du[...], w_node[...]) + mul(gown_t[...], both)
    out[...] = total.astype(out.dtype)


def add_kernel(plane, lists, value, inner, outer, *refs):
    *other, out, total = refs
    block = inner.shape[0]

    @pl.when(here_is(plane))
    def _():
        total[...] = value[...].astype(F32)
        add_listed(lists[INNER : INNER + 1, :1], total, inner[...].astype(F32), block)
        add_listed(lists[OUTER : OUTER + 1, :1], total, outer[...].astype(F32), block)
        out[...] = total[...].astype(BF16)

    if other:

        @pl.when(jnp.logical_not(here_is(plane)))
        def _():
            out[...] = other[0][...]


def turn_kernel(evens, odds, out):
    @pl.when(here_is(parity=1))
    def _():
        out[...] = evens[...]

    @pl.when(here_is(parity=0))
    def _():
        out[...] = odds[...]


def write_kernel(evens, odds, arrived, out, sems):
    core = lax.axis_index("pipe") % 2
    other = pltpu.make_async_copy(arrived, out.at[0, 1 - core], sems.at[1])
    other.start()

    @pl.when(core == 0)
    def _():
        own = pltpu.make_async_copy(evens, out.at[0, 0], sems.at[0])
        own.start()
        own.wait()

    @pl.when(core == 1)
    def _():
        own = pltpu.make_async_copy(odds, out.at[0, 1], sems.at[0])
        own.start()
        own.wait()

    other.wait()


def run(kernel, operands, outs, aliases=None, flops=0, first=pltpu.VMEM, out_space=pltpu.VMEM, scratch=()):
    spaces = [first] + [pltpu.VMEM] * (len(operands) - 1)
    return pl.pallas_call(
        kernel,
        out_shape=[jax.ShapeDtypeStruct(s, t) for s, t in outs],
        in_specs=[pl.BlockSpec(memory_space=space) for space in spaces],
        out_specs=[pl.BlockSpec(memory_space=out_space)] * len(outs),
        scratch_shapes=list(scratch),
        input_output_aliases=aliases or {},
        compiler_params=pltpu.CompilerParams(vmem_limit_bytes=16 * 2**20),
        cost_estimate=pl.CostEstimate(flops=flops, bytes_accessed=2**20, transcendentals=0),
    )(*operands)


def run_section(body, plane, parity, weights, operands, outs, flops):
    count = len(weights) // 2

    def kernel(*refs):
        mine, swapped, rest = refs[:count], refs[count : 2 * count], refs[2 * count :]

        @pl.when(here_is(plane, parity))
        def _():
            body(mine, *rest)

        @pl.when(here_is(plane, 1 - parity))
        def _():
            body(swapped, *rest)

    return run(kernel, tuple(weights) + tuple(operands), outs, flops=flops)


def shards(
    inputs,
    cotangent,
    w_send,
    w_recv,
    w_message,
    w_node,
    w_aggregate,
    gains,
    edge_send,
    edge_recv,
    edge_count,
    halo_send,
):
    sections = lax.axis_size("pipe")
    pairs_total = lax.axis_size("dom") // 2
    phase = lax.axis_index("pipe")
    y = lax.rem(lax.axis_index("dom"), 2)
    plane_here = phase // 2
    rows, latent = inputs.shape[1:]
    edge_blocks, block = edge_send.shape
    edges = edge_blocks * block

    def send(value, rule):
        table = []
        for z in range(pairs_total):
            for which in range(2):
                for x in range(sections // 2):
                    for c in range(2):
                        tz, ty, tx, tc = rule(z, which, x, c)
                        target = (2 * (tz % pairs_total) + ty) * sections + 2 * (tx % (sections // 2)) + tc
                        table.append(((2 * z + which) * sections + 2 * x + c, target))
        return lax.ppermute(value, AXES, table)

    def flip_y(value):
        return send(value, lambda z, y, x, c: (z, 1 - y, x, c))

    def flip_core(value):
        return send(value, lambda z, y, x, c: (z, y, x, 1 - c))

    def to_home(value):
        return send(value, lambda z, y, x, c: (z, c, x, y))

    def towards(value, side, step):
        if side == INNER:
            return send(value, lambda z, y, x, c: (z, y, x + step, 1 - c))
        return send(value, lambda z, y, x, c: (z + 2 * c - 1, y, x + step, 1 - c))

    wide = (rows, latent)
    edge_wide = (edges, latent)
    narrow = (block, latent)
    unit = 2 * rows * latent * latent
    dma = pltpu.SemaphoreType.DMA

    first_list = halo_send[0, :, 0]
    here, there = run(rows_kernel, (inputs,), [(wide, BF16)] * 2, first=pl.ANY, scratch=[dma((2,))])
    there = flip_y(there)
    [boundary] = pl.pallas_call(
        boundary_kernel,
        out_shape=[jax.ShapeDtypeStruct(narrow, BF16)],
        in_specs=[pl.BlockSpec(memory_space=pltpu.SMEM), pl.BlockSpec(memory_space=pl.ANY)],
        out_specs=[pl.BlockSpec(memory_space=pltpu.VMEM)],
        scratch_shapes=[dma(())],
    )(first_list, inputs)
    outer = send(boundary, lambda z, y, x, c: (z + 2 * y - 1, c, x, 1 - y))
    numbers = jnp.concatenate([edge_count, first_list])
    packed = jnp.concatenate(
        [edge_send, edge_recv, jnp.pad(numbers, (0, block - numbers.shape[0]))[None]], axis=0
    )
    packed_there = flip_y(packed)
    gown, gown_t, ghalo, ghalo_t, lists, mate = run(
        functools.partial(graph_kernel, edge_blocks),
        (packed, packed_there),
        [
            ((2 * edges, rows), BF16),
            ((rows, 2 * edges), BF16),
            ((edges, 2 * block), BF16),
            ((2 * block, edges), BF16),
            ((2, block), jnp.int32),
            ((1, block), jnp.int32),
        ],
    )
    hidden, inner = run(entry_kernel, (mate, here, there), [(wide, BF16), (narrow, BF16)])
    home_sides = jnp.where(y == 0, first_list, first_list[::-1])
    home_lists = jnp.broadcast_to(home_sides[:, None], (2, block))

    [w_fold] = run(fold_kernel, (w_message[0], w_aggregate[0]), [(w_message.shape[1:], BF16)])
    weights = (w_send[0], w_recv[0], w_node[0], w_fold, gains)
    weights = weights + tuple(flip_core(value) for value in weights)

    grad_here, grad_there = run(rows_kernel, (cotangent,), [(wide, BF16)] * 2, first=pl.ANY, scratch=[dma((2,))])
    grad_there = flip_y(grad_there)

    saved = [(), ()]
    for tick in range(sections):
        plane, parity = tick // 2, tick % 2
        a_own, u_own = run_section(
            forward_own_kernel, plane, parity, weights, (hidden, gown), [(edge_wide, F32), (wide, F32)], 4 * unit
        )
        to_send = [(narrow, BF16)] * 2 if tick < sections - 1 else []
        hidden, a, u, *to = run_section(
            forward_kernel,
            plane,
            parity,
            weights,
            (lists, hidden, a_own, u_own, inner, outer, ghalo, gown_t),
            [(wide, BF16), (edge_wide, F32), (wide, F32)] + to_send,
            4 * unit,
        )
        produced = hidden
        if to:
            step = (tick + 1) // 2 - plane
            outer = towards(to[OUTER], OUTER, step)
            if step:
                hidden = send(hidden, lambda z, y, x, c: (z, y, x + 1, c))
            inner = towards(to[INNER], INNER, step)
        saved[parity] = run(
            functools.partial(save_kernel, plane),
            (a, u, produced) + tuple(saved[parity]),
            [(wide, F32), (wide, F32), (edge_wide, F32), (wide, BF16)],
            aliases={3 + k: k for k in range(4)} if saved[parity] else None,
            flops=unit,
        )

    def both_micro(evens, odds):
        [turned] = run(turn_kernel, (evens, odds), [(wide, BF16)])
        [out] = run(
            write_kernel,
            (evens, odds, flip_core(turned)),
            [((1, 2) + wide, BF16)],
            out_space=pl.ANY,
            scratch=[dma((2,))],
        )
        return out

    [upstream] = run(local_kernel, (grad_here, grad_there), [(wide, BF16)])
    inner = outer = None
    finished = {}
    for tick in range(sections - 1, -1, -1):
        plane, parity = tick // 2, tick % 2
        step = (tick - 1) // 2 - plane if tick else 0
        crossing = tick > 0 and step != 0
        halo_in = inner is not None
        finish = halo_in and tick % 2 == 0
        outs = [
            (wide, F32),
            (wide, BF16),
            (edge_wide, BF16),
            (edge_wide, BF16),
            (narrow, BF16),
            (narrow, BF16),
        ] + ([(wide, BF16)] if finish else [])
        c, du, da, es, to_inner, to_outer, *done = run_section(
            functools.partial(backward_kernel, halo_in, finish),
            plane,
            parity,
            weights,
            (lists, upstream)
            + ((inner, outer) if halo_in else ())
            + tuple(saved[parity][:3])
            + (gown, ghalo_t),
            outs,
            4 * unit,
        )
        if done:
            finished[tick + 1] = done[0]
        if tick:
            outer = towards(to_outer, OUTER, step)
            inner = towards(to_inner, INNER, step)
        [upstream] = run_section(
            backward_own_kernel,
            plane,
            parity,
            weights,
            (c, du, da, es, gown_t),
            [(wide, F32 if tick and not crossing else BF16)],
            4 * unit,
        )
        if crossing:
            own = upstream
            upstream = send(own, lambda z, y, x, c: (z, y, x + 1, c))
            own_outer = towards(to_outer, OUTER, 0)
            own_inner = towards(to_inner, INNER, 0)
            even_h, odd_h, _ = lax.optimization_barrier((saved[0][3], saved[1][3], own))
            even_h, odd_h = to_home(even_h), to_home(odd_h)
            upstream, inner, outer, own_outer, own_inner, even_h, odd_h = lax.optimization_barrier(
                (upstream, inner, outer, own_outer, own_inner, even_h, odd_h)
            )
            [finished[tick]] = run(
                functools.partial(add_kernel, plane),
                (lists, own, own_inner, own_outer),
                [(wide, BF16)],
                scratch=[pltpu.VMEM(wide, F32)],
            )
            section_out = both_micro(even_h, odd_h)

    final_outer = send(to_outer, lambda z, y, x, c: (z + 2 * c - 1, 1 - c, x, y))
    final_inner = send(to_inner, lambda z, y, x, c: (z, 1 - c, x, y))
    last_of = [finished[1], finished[3]]
    odds = to_home(jnp.where(plane_here == 0, *last_of))
    evens = to_home(jnp.where(plane_here == 0, upstream, finished[2]))
    [evens] = run(
        functools.partial(add_kernel, 0),
        (home_lists, evens, final_inner, final_outer, evens),
        [(wide, BF16)],
        scratch=[pltpu.VMEM(wide, F32)],
    )
    return section_out, both_micro(evens, odds)


def solution(mesh):
    in_specs = (
        P(None, "dom", None),
        P(None, "dom", None),
        P("pipe", None, None),
        P("pipe", None, None),
        P("pipe", None, None),
        P("pipe", None, None),
        P("pipe", None, None),
        P("pipe", None),
        P("dom", None),
        P("dom", None),
        P("dom"),
        P("dom", None, None),
    )
    out_specs = (P("pipe", None, "dom", None), P("pipe", None, "dom", None))
    return jax.shard_map(shards, mesh=mesh, in_specs=in_specs, out_specs=out_specs, check_vma=False)
```

```python
import functools

import jax
import jax.numpy as jnp
from jax import lax
from jax.experimental import pallas as pl
from jax.experimental.pallas import tpu as pltpu
from jax.sharding import PartitionSpec as P

EPSILON = 1e-05
F32 = jnp.float32
BF16 = jnp.bfloat16
AXES = ("dom", "pipe")
INNER, OUTER = 0, 1
BESIDE = 4 * 10**9


def mul(a, b):
    return jnp.dot(a, b, preferred_element_type=F32)


def mul_t(a, b):
    return lax.dot_general(a, b, (((1,), (1,)), ((), ())), preferred_element_type=F32)


def slope(v):
    s = jax.nn.sigmoid(v)
    return s * (1.0 + v * (1.0 - s))


def normalize(z):
    centred = z - jnp.mean(z, axis=-1, keepdims=True)
    inverse = lax.rsqrt(jnp.mean(centred * centred, axis=-1, keepdims=True) + EPSILON)
    return centred * inverse, inverse


def thirds(packed):
    depth = packed.shape[0] // 3
    return [packed.at[pl.ds(number * depth, depth), :] for number in range(3)]


def here_is(plane=None, parity=None):
    pipe = lax.axis_index("pipe")
    wanted = jnp.bool_(True)
    if plane is not None:
        wanted = pipe // 2 == plane
    if parity is not None:
        wanted = wanted & (pipe % 2 == parity)
    return wanted


def is_local():
    return lax.axis_index("pipe") % 2 == lax.axis_index("dom") % 2


def listed(at, value, block):
    picked = value[:block]
    for number in range(1, value.shape[0] // block):
        picked = jnp.where(at == number, value[number * block : (number + 1) * block], picked)
    return picked


def add_listed(at, target, value, block):
    for number in range(target.shape[0] // block):
        rows = slice(number * block, (number + 1) * block)
        target[rows, :] = target[rows, :] + jnp.where(at == number, value, 0.0)


def prepare_kernel(count, halo, inputs, cotangent, send_in, recv_in, here, there, boundary, packed, sems):
    micro = lax.axis_index("dom") % 2
    block = boundary.shape[0]
    edge_blocks = send_in.shape[0]
    number = jnp.where(micro == 1, halo[0, 0, 0], halo[0, 1, 0])
    start = pl.multiple_of(number * block, block)
    edge_copies = [
        pltpu.make_async_copy(ref, packed.at[place, pl.ds(0, edge_blocks), :], sems.at[3 + place])
        for place, ref in enumerate((send_in, recv_in))
    ]
    for copy in edge_copies:
        copy.start()
    lane = lax.broadcasted_iota(jnp.int32, packed.shape[1:], 1)
    tail = jnp.where(lane == 0, halo[0, 0, 0], halo[0, 1, 0])
    for place in range(edge_blocks):
        tail = jnp.where(lane == 2 + place, count[place], tail)
    packed[2] = tail

    def fetch(source):
        copies = [
            pltpu.make_async_copy(source.at[1 - micro], there, sems.at[0]),
            pltpu.make_async_copy(
                source.at[lax.axis_index("pipe") % 2, pl.ds(start, block), :], boundary, sems.at[1]
            ),
            pltpu.make_async_copy(source.at[micro], here, sems.at[2]),
        ]
        for copy in copies:
            copy.start()
        for copy in copies:
            copy.wait()

    @pl.when(here_is(0))
    def _():
        fetch(inputs)

    @pl.when(jnp.logical_not(here_is(0)))
    def _():
        fetch(cotangent)

    for copy in edge_copies:
        copy.wait()


def fold_kernel(a, b, _, out):
    out[...] = mul(a[...], b[...]).astype(BF16)


def arrange_kernel(*refs):
    *given, even, odd = refs
    count = len(given) // 2
    mine, swapped = given[:count], given[count:]
    depth = mine[0].shape[0]

    def fill(out, sources):
        for number, source in enumerate(sources):
            out[number * depth : (number + 1) * depth, :] = source[...]

    @pl.when(here_is(parity=0))
    def _():
        fill(even, mine)
        fill(odd, swapped)

    @pl.when(here_is(parity=1))
    def _():
        fill(even, swapped)
        fill(odd, mine)


def graph_kernel(edge_blocks, packed, packed_there, gown, gown_t, ghalo, ghalo_t, lists, mate, home_lists):
    block = packed.shape[2]
    rows = gown_t.shape[0]
    edges = edge_blocks * block
    local = is_local()
    first_core = lax.axis_index("pipe") % 2 == 0
    mine = [jnp.where(local, packed[k], packed_there[k]) for k in range(3)]
    tails = mine[2], jnp.where(local, packed_there[2], packed[2])
    lane = lax.broadcasted_iota(jnp.int32, (1, block), 1)
    row = lax.broadcasted_iota(jnp.int32, (rows, block), 0)
    halo_row = lax.broadcasted_iota(jnp.int32, (2 * block, block), 0)
    for number in range(edge_blocks):
        live = lane < tails[0][:1, 2 + number : 3 + number]
        sender = jnp.where(live, mine[0][number : number + 1], -1)
        receiver = jnp.where(live, mine[1][number : number + 1], -1)
        outside = sender - rows
        turned = jnp.where(outside < block, outside + block, outside - block)
        outside = jnp.where(outside >= 0, jnp.where(first_core, turned, outside), -1)
        here = slice(number * block, (number + 1) * block)
        received = slice(edges + number * block, edges + (number + 1) * block)
        for index, at, table, table_t in (
            (sender, here, gown, gown_t),
            (receiver, received, gown, gown_t),
            (outside, here, ghalo, ghalo_t),
        ):
            hot = (index == (halo_row if table is ghalo else row)).astype(F32)
            table_t[:, at] = hot.astype(BF16)
            table[at, :] = hot.T.astype(BF16)

    def whole(tail, place):
        return jnp.broadcast_to(tail[:1, place : place + 1], (1, block))

    to_next, to_prev = whole(tails[0], 0), whole(tails[0], 1)
    lists[0:1, :] = jnp.where(first_core, to_next, to_prev)
    lists[1:2, :] = jnp.where(first_core, to_prev, to_next)
    mate[...] = jnp.where(first_core, whole(tails[1], 1), whole(tails[1], 0))
    to_next, to_prev = whole(packed[2], 0), whole(packed[2], 1)
    home_first = lax.axis_index("dom") % 2 == 0
    home_lists[0:1, :] = jnp.where(home_first, to_next, to_prev)
    home_lists[1:2, :] = jnp.where(home_first, to_prev, to_next)


def entry_kernel(mate, here, there, hidden, inner):
    block = inner.shape[0]

    @pl.when(is_local())
    def _():
        hidden[...] = here[...]
        inner[...] = listed(mate[:, :1], there[...], block)

    @pl.when(jnp.logical_not(is_local()))
    def _():
        hidden[...] = there[...]
        inner[...] = listed(mate[:, :1], here[...], block)


def forward_own_kernel(take, h, gown, a_out, u_out):
    w_send, w_recv, w_node = thirds(take[0])
    edges = gown.shape[0] // 2
    own = mul(gown[...], h[...]).astype(BF16)
    a_out[...] = mul(own[:edges], w_send[...]) + mul(own[edges:], w_recv[...])
    u_out[...] = mul(h[...], w_node[...])


def forward_kernel(take, lists, h, a_own, u_own, inner, outer, ghalo, gown_t, h_out, a_out, u_out, *to):
    packed, w_fold, gain = take
    w_send = thirds(packed)[0]
    edges = ghalo.shape[0]
    block = inner.shape[0]
    halo = (mul(ghalo[:, :block], inner[...]) + mul(ghalo[:, block:], outer[...])).astype(BF16)
    a = a_own[...] + mul(halo, w_send[...])
    a_out[...] = a
    q = (a * jax.nn.sigmoid(a)).astype(BF16)
    u = u_own[...] + mul(mul(gown_t[:, edges:], q).astype(BF16), w_fold[...])
    u_out[...] = u
    t, _ = normalize(u * jax.nn.sigmoid(u))
    out = (h[...].astype(F32) + t * gain[...]).astype(BF16)
    h_out[...] = out
    for side, ref in enumerate(to):
        ref[...] = listed(lists[side : side + 1, :1], out, block)


def save_kernel(plane, parity, a, u, h, *refs):
    t_out, r_out, s_out, h_out = refs[-4:]
    rows, edges = h.shape[0], a.shape[0]
    at = slice(parity * rows, (parity + 1) * rows)

    @pl.when(here_is(plane))
    def _():
        s_out[parity * edges : (parity + 1) * edges, :] = slope(a[...]).astype(BF16)
        u_value = u[...]
        t, inverse = normalize(u_value * jax.nn.sigmoid(u_value))
        t_out[at, :] = t.astype(BF16)
        r_out[at, :] = (inverse * slope(u_value)).astype(BF16)
        h_out[at, :] = h[...]


def pick_kernel(first, second, out):
    @pl.when(here_is(0))
    def _():
        out[...] = first[...]

    @pl.when(jnp.logical_not(here_is(0)))
    def _():
        out[...] = second[...]


def backward_kernel(halo_in, parity, take, lists, upstream, *refs):
    packed, w_fold, gain = take
    w_send = thirds(packed)[0]
    if halo_in:
        inner, outer, *refs = refs
    t_in, r_in, s_in, gown, ghalo_t, c_out, du_out, da_out, es_out, to_inner, to_outer, *rest = refs
    edges = gown.shape[0] // 2
    rows = upstream.shape[0]
    block = to_inner.shape[0]
    at = slice(parity * rows, (parity + 1) * rows)
    at_edges = slice(parity * edges, (parity + 1) * edges)
    c_out[...] = upstream[...].astype(F32)
    if halo_in:
        add_listed(lists[INNER : INNER + 1, :1], c_out, inner[...].astype(F32), block)
        add_listed(lists[OUTER : OUTER + 1, :1], c_out, outer[...].astype(F32), block)
    if rest:
        rest[0][...] = c_out[...].astype(BF16)
    g = c_out[...] * gain[...]
    t = t_in[at, :].astype(F32)
    centre = jnp.mean(g, axis=-1, keepdims=True)
    along = jnp.mean(g * t, axis=-1, keepdims=True)
    du = ((g - centre - t * along) * r_in[at, :].astype(F32)).astype(BF16)
    du_out[...] = du
    spread = mul(gown[edges:, :], du).astype(BF16)
    da = (mul_t(spread, w_fold[...]) * s_in[at_edges, :].astype(F32)).astype(BF16)
    da_out[...] = da
    es = mul_t(da, w_send[...]).astype(BF16)
    es_out[...] = es
    halo = mul(ghalo_t[...], es).astype(BF16)
    to_inner[...] = halo[:block]
    to_outer[...] = halo[block:]


def backward_own_kernel(take, c, du, da, es, gown_t, *refs):
    _, w_recv, w_node = thirds(take[0])
    out = refs[-1]
    er = mul_t(da[...], w_recv[...]).astype(BF16)
    both = jnp.concatenate([es[...], er], axis=0)
    total = c[...] + mul_t(du[...], w_node[...]) + mul(gown_t[...], both)
    out[...] = total.astype(out.dtype)


def add_kernel(plane, lists, value, inner, outer, *refs):
    *other, out, total = refs
    block = inner.shape[0]

    @pl.when(here_is(plane))
    def _():
        total[...] = value[...].astype(F32)
        add_listed(lists[INNER : INNER + 1, :1], total, inner[...].astype(F32), block)
        add_listed(lists[OUTER : OUTER + 1, :1], total, outer[...].astype(F32), block)
        out[...] = total[...].astype(BF16)

    if other:

        @pl.when(jnp.logical_not(here_is(plane)))
        def _():
            out[...] = other[0][...]


def turn_kernel(evens, odds, out):
    @pl.when(here_is(parity=1))
    def _():
        out[...] = evens[...]

    @pl.when(here_is(parity=0))
    def _():
        out[...] = odds[...]


def write_kernel(evens, odds, arrived, out, sems):
    core = lax.axis_index("pipe") % 2
    other = pltpu.make_async_copy(arrived, out.at[0, 1 - core], sems.at[1])
    other.start()

    @pl.when(core == 0)
    def _():
        own = pltpu.make_async_copy(evens, out.at[0, 0], sems.at[0])
        own.start()
        own.wait()

    @pl.when(core == 1)
    def _():
        own = pltpu.make_async_copy(odds, out.at[0, 1], sems.at[0])
        own.start()
        own.wait()

    other.wait()


def run(kernel, operands, outs, spaces=(), aliases=None, out_space=pltpu.VMEM, scratch=(), cost=1, vmem=12):
    spaces = tuple(spaces) + (pltpu.VMEM,) * (len(operands) - len(spaces))
    return pl.pallas_call(
        kernel,
        out_shape=[jax.ShapeDtypeStruct(s, t) for s, t in outs],
        in_specs=[pl.BlockSpec(memory_space=space) for space in spaces],
        out_specs=[pl.BlockSpec(memory_space=out_space)] * len(outs),
        scratch_shapes=list(scratch),
        input_output_aliases=aliases or {},
        compiler_params=pltpu.CompilerParams(vmem_limit_bytes=vmem * 2**20),
        cost_estimate=pl.CostEstimate(flops=cost, bytes_accessed=1, transcendentals=0),
    )(*operands)


def run_section(body, plane, matrices, operands, outs, elsewhere=None, cost=1):
    def kernel(*refs):
        take, rest = refs[: len(matrices)], refs[len(matrices) :]

        @pl.when(here_is(plane))
        def _():
            body(take, *rest)

        if elsewhere is not None:

            @pl.when(jnp.logical_not(here_is(plane)))
            def _():
                rest[-1][...] = rest[elsewhere][...]

    return run(kernel, tuple(matrices) + tuple(operands), outs, cost=cost)


def shards(
    inputs,
    cotangent,
    w_send,
    w_recv,
    w_message,
    w_node,
    w_aggregate,
    gains,
    edge_send,
    edge_recv,
    edge_count,
    halo_send,
):
    sections = lax.axis_size("pipe")
    pairs_total = lax.axis_size("dom") // 2
    phase = lax.axis_index("pipe")
    y = lax.rem(lax.axis_index("dom"), 2)
    plane_here = phase // 2
    rows, latent = inputs.shape[1:]
    edge_blocks, block = edge_send.shape
    edges = edge_blocks * block

    def send(value, rule):
        table = []
        for z in range(pairs_total):
            for which in range(2):
                for x in range(sections // 2):
                    for c in range(2):
                        if (target := rule(z, which, x, c)) is None:
                            continue
                        tz, ty, tx, tc = target
                        target = (2 * (tz % pairs_total) + ty) * sections + 2 * (tx % (sections // 2)) + tc
                        table.append(((2 * z + which) * sections + 2 * x + c, target))
        return lax.ppermute(value, AXES, table)

    def flip_y(value):
        return send(value, lambda z, y, x, c: (z, 1 - y, x, c))

    def flip_core(value):
        return send(value, lambda z, y, x, c: (z, y, x, 1 - c))

    def to_home(value):
        return send(value, lambda z, y, x, c: (z, c, x, y))

    def towards(value, side, step):
        if side == INNER:
            return send(value, lambda z, y, x, c: (z, y, x + step, 1 - c))
        return send(value, lambda z, y, x, c: (z + 2 * c - 1, y, x + step, 1 - c))

    wide = (rows, latent)
    edge_wide = (edges, latent)
    narrow = (block, latent)
    unit = 2 * rows * latent * latent
    dma = pltpu.SemaphoreType.DMA

    here, there, boundary, packed = run(
        prepare_kernel,
        (edge_count, halo_send, inputs, cotangent, edge_send, edge_recv),
        [(wide, BF16), (wide, BF16), (narrow, BF16), ((3, 8, block), jnp.int32)],
        spaces=(pltpu.SMEM, pltpu.SMEM) + (pltpu.HBM,) * 4,
        scratch=[dma((5,))],
    )
    packed_there = send(packed, lambda z, y, x, c: (z, 1 - y, x, 1 - c))
    there = flip_y(there)
    outer = send(boundary, lambda z, y, x, c: (z + 2 * y - 1, c, x, 1 - y))
    plain = (w_send[0], w_recv[0], w_node[0])
    swapped = tuple(flip_core(value) for value in plain)
    even, odd = run(arrange_kernel, plain + swapped, [((3 * latent, latent), BF16)] * 2, cost=BESIDE)
    [fold] = run(fold_kernel, (w_message[0], w_aggregate[0], packed_there), [((latent, latent), BF16)], cost=BESIDE)
    fold_even, fold_odd = run(arrange_kernel, (fold, flip_core(fold)), [((latent, latent), BF16)] * 2)
    gain_even, gain_odd = run(arrange_kernel, (gains, flip_core(gains)), [((1, latent), F32)] * 2)
    matrices = ((even, fold_even, gain_even), (odd, fold_odd, gain_odd))

    gown, gown_t, ghalo, ghalo_t, lists, mate, home_lists = run(
        functools.partial(graph_kernel, edge_blocks),
        (packed, packed_there),
        [
            ((2 * edges, rows), BF16),
            ((rows, 2 * edges), BF16),
            ((edges, 2 * block), BF16),
            ((2 * block, edges), BF16),
            ((2, block), jnp.int32),
            ((1, block), jnp.int32),
            ((2, block), jnp.int32),
        ],
        cost=BESIDE,
    )
    hidden, inner = run(entry_kernel, (mate, here, there), [(wide, BF16), (narrow, BF16)])
    upstream = hidden

    def both_micro(evens, odds):
        [turned] = run(turn_kernel, (evens, odds), [(wide, BF16)])
        [out] = run(
            write_kernel,
            (evens, odds, flip_core(turned)),
            [((1, 2) + wide, BF16)],
            out_space=pl.ANY,
            scratch=[dma((2,))],
        )
        return out

    def home_of_plane(value, plane):
        return send(value, lambda z, y, x, c: (z, c, x, y) if x == plane else None)

    saved = ()
    first_home = None
    for tick in range(sections):
        plane, parity = tick // 2, tick % 2
        packed, fold, gain = matrices[parity]
        a_own, u_own = run_section(
            forward_own_kernel, plane, (packed,), (hidden, gown), [(edge_wide, F32), (wide, F32)], cost=BESIDE
        )
        if tick == sections - 1:
            first_home, a_own = lax.optimization_barrier((saved[3], a_own))
            first_home = home_of_plane(first_home, 0)
        to_send = [(narrow, BF16)] * 2 if tick < sections - 1 else []
        hidden, a, u, *to = run_section(
            forward_kernel,
            plane,
            (packed, fold, gain),
            (lists, hidden, a_own, u_own, inner, outer, ghalo, gown_t),
            [(wide, BF16), (edge_wide, F32), (wide, F32)] + to_send,
        )
        produced = hidden
        if to:
            step = (tick + 1) // 2 - plane
            outer = towards(to[OUTER], OUTER, step)
            if step:
                hidden = send(hidden, lambda z, y, x, c: (z, y, x + 1, c))
            inner = towards(to[INNER], INNER, step)
        saved = run(
            functools.partial(save_kernel, plane, parity),
            (a, u, produced) + tuple(saved),
            [((2 * rows, latent), BF16), ((2 * rows, latent), BF16), ((2 * edges, latent), BF16), ((2 * rows, latent), BF16)],
            aliases={3 + k: k for k in range(4)} if saved else None,
            cost=BESIDE,
        )

    *states, both = saved
    inner = outer = crossed = None
    finished = {}
    for tick in range(sections - 1, -1, -1):
        plane, parity = tick // 2, tick % 2
        packed, fold, gain = matrices[parity]
        step = (tick - 1) // 2 - plane if tick else 0
        crossing = tick > 0 and step != 0
        halo_in = inner is not None
        finish = halo_in and tick % 2 == 0
        outs = [
            (wide, F32),
            (wide, BF16),
            (edge_wide, BF16),
            (edge_wide, BF16),
            (narrow, BF16),
            (narrow, BF16),
        ] + ([(wide, BF16)] if finish else [])
        late = (finished[3],) if tick == 0 else ()
        c, du, da, es, to_inner, to_outer, *done = run_section(
            lambda take, *refs, halo_in=halo_in, parity=parity, late=len(late): backward_kernel(
                halo_in, parity, take, *refs[late:]
            ),
            plane,
            (packed, fold, gain),
            late + (lists, upstream) + ((inner, outer) if halo_in else ()) + tuple(states) + (gown, ghalo_t),
            outs,
            elsewhere=0 if late else None,
        )
        if done:
            finished[tick + 1] = done[0]
        if tick:
            outer = towards(to_outer, OUTER, step)
            inner = towards(to_inner, INNER, step)
        late = (finished[2],) if tick == 0 else ()
        [upstream] = run_section(
            lambda take, *refs, late=len(late): backward_own_kernel(take, *refs[late:]),
            plane,
            (packed,),
            late + (c, du, da, es, gown_t),
            [(wide, F32 if tick and not crossing else BF16)],
            elsewhere=0 if late else None,
            cost=BESIDE,
        )
        if crossed is not None:
            own, late_inner, late_outer, both, upstream = lax.optimization_barrier(crossed + (both, upstream))
            late_outer = send(late_outer, lambda z, y, x, c: (z + 2 * c - 1, y, x, 1 - c) if x else None)
            late_inner = send(late_inner, lambda z, y, x, c: (z, y, x, 1 - c) if x else None)
            second_home = home_of_plane(both, 1)
            [finished[2]] = run(
                functools.partial(add_kernel, 1),
                (lists, own, late_inner, late_outer),
                [(wide, BF16)],
                scratch=[pltpu.VMEM(wide, F32)],
            )
            crossed = None
        if crossing:
            crossed = (upstream, to_inner, to_outer)
            upstream = send(upstream, lambda z, y, x, c: (z, y, x + 1, c))

    final_outer = send(to_outer, lambda z, y, x, c: (z + 2 * c - 1, 1 - c, x, y))
    final_inner = send(to_inner, lambda z, y, x, c: (z, 1 - c, x, y))
    evens = to_home(upstream)
    odds = to_home(finished[1])
    [evens] = run(
        functools.partial(add_kernel, 0),
        (home_lists, evens, final_inner, final_outer, evens),
        [(wide, BF16)],
        scratch=[pltpu.VMEM(wide, F32)],
    )
    [home] = run(pick_kernel, (first_home, second_home), [((2 * rows, latent), BF16)])
    return both_micro(home[:rows], home[rows:]), both_micro(evens, odds)


def solution(mesh):
    in_specs = (
        P(None, "dom", None),
        P(None, "dom", None),
        P("pipe", None, None),
        P("pipe", None, None),
        P("pipe", None, None),
        P("pipe", None, None),
        P("pipe", None, None),
        P("pipe", None),
        P("dom", None),
        P("dom", None),
        P("dom"),
        P("dom", None, None),
    )
    out_specs = (P("pipe", None, "dom", None), P("pipe", None, "dom", None))
    return jax.shard_map(shards, mesh=mesh, in_specs=in_specs, out_specs=out_specs, check_vma=False)
```

```python
import functools

import jax
import jax.numpy as jnp
from jax import lax
from jax.experimental import pallas as pl
from jax.experimental.pallas import tpu as pltpu
from jax.sharding import PartitionSpec as P

EPSILON = 1e-05
F32 = jnp.float32
BF16 = jnp.bfloat16
AXES = ("dom", "pipe")
INNER, OUTER = 0, 1
BESIDE = 4 * 10**9
LONG = 2 * 10**10


def mul(a, b):
    return jnp.dot(a, b, preferred_element_type=F32)


def mul_t(a, b):
    return lax.dot_general(a, b, (((1,), (1,)), ((), ())), preferred_element_type=F32)


def slope(v):
    s = jax.nn.sigmoid(v)
    return s * (1.0 + v * (1.0 - s))


def normalize(z):
    centred = z - jnp.mean(z, axis=-1, keepdims=True)
    inverse = lax.rsqrt(jnp.mean(centred * centred, axis=-1, keepdims=True) + EPSILON)
    return centred * inverse, inverse


def quarters(packed):
    depth = packed.shape[0] // 4
    return [packed.at[pl.ds(number * depth, depth), :] for number in range(4)]


def here_is(plane=None, parity=None):
    pipe = lax.axis_index("pipe")
    wanted = jnp.bool_(True)
    if plane is not None:
        wanted = pipe // 2 == plane
    if parity is not None:
        wanted = wanted & (pipe % 2 == parity)
    return wanted


def is_local():
    return lax.axis_index("pipe") % 2 == lax.axis_index("dom") % 2


def listed(at, value, block):
    picked = value[:block]
    for number in range(1, value.shape[0] // block):
        picked = jnp.where(at == number, value[number * block : (number + 1) * block], picked)
    return picked


def add_listed(at, target, value, block):
    for number in range(target.shape[0] // block):
        rows = slice(number * block, (number + 1) * block)
        target[rows, :] = target[rows, :] + jnp.where(at == number, value, 0.0)


def prepare_kernel(
    count,
    halo,
    inputs,
    cotangent,
    send_in,
    recv_in,
    w_send,
    w_recv,
    w_node,
    w_message,
    w_aggregate,
    here,
    there,
    boundary,
    weights,
    packed,
    factors,
    product,
    sems,
    weight_sems,
):
    micro = lax.axis_index("dom") % 2
    block = boundary.shape[0]
    depth = w_send.shape[0]
    edge_blocks = send_in.shape[0]
    number = jnp.where(micro == 1, halo[0, 0, 0], halo[0, 0, 1])
    start = pl.multiple_of(number * block, block)

    def fetch(source):
        return [
            pltpu.make_async_copy(source.at[1 - micro], there, sems.at[0]),
            pltpu.make_async_copy(
                source.at[lax.axis_index("pipe") % 2, pl.ds(start, block), :], boundary, sems.at[1]
            ),
            pltpu.make_async_copy(source.at[micro], here, sems.at[2]),
        ]

    @pl.when(here_is(0))
    def _():
        for copy in fetch(inputs):
            copy.start()

    @pl.when(jnp.logical_not(here_is(0)))
    def _():
        for copy in fetch(cotangent):
            copy.start()

    copies = [
        pltpu.make_async_copy(ref, factors.at[k], weight_sems.at[k]) for k, ref in enumerate((w_message, w_aggregate))
    ]
    copies += [
        pltpu.make_async_copy(ref, packed.at[k, pl.ds(0, edge_blocks), :], sems.at[3 + k])
        for k, ref in enumerate((send_in, recv_in))
    ]
    copies += [
        pltpu.make_async_copy(ref, weights.at[pl.ds(k * depth, depth), :], weight_sems.at[2 + k])
        for k, ref in enumerate((w_send, w_recv, w_node))
    ]
    for copy in copies:
        copy.start()
    lane = lax.broadcasted_iota(jnp.int32, packed.shape[1:], 1)
    tail = jnp.where(lane == 0, halo[0, 0, 0], halo[0, 0, 1])
    for place in range(edge_blocks):
        tail = jnp.where(lane == 2 + place, count[place], tail)
    packed[2] = tail
    for copy in copies[:2]:
        copy.wait()
    product[...] = mul(factors[0], factors[1]).astype(BF16)
    last = pltpu.make_async_copy(product, weights.at[pl.ds(3 * depth, depth), :], weight_sems.at[5])
    last.start()
    for copy in copies[2:] + fetch(inputs):
        copy.wait()
    last.wait()


def arrange_kernel(mine, swapped, even, odd):
    @pl.when(here_is(parity=0))
    def _():
        even[...] = mine[...]
        odd[...] = swapped[...]

    @pl.when(here_is(parity=1))
    def _():
        even[...] = swapped[...]
        odd[...] = mine[...]


def graph_kernel(edge_blocks, _, packed, packed_there, gown, gown_t, ghalo, ghalo_t, lists, mate, home_lists):
    block = packed.shape[2]
    rows = gown_t.shape[0]
    edges = edge_blocks * block
    local = is_local()
    first_core = lax.axis_index("pipe") % 2 == 0
    mine = [jnp.where(local, packed[k], packed_there[k]) for k in range(3)]
    tails = mine[2], jnp.where(local, packed_there[2], packed[2])
    lane = lax.broadcasted_iota(jnp.int32, (1, block), 1)
    row = lax.broadcasted_iota(jnp.int32, (rows, block), 0)
    halo_row = lax.broadcasted_iota(jnp.int32, (2 * block, block), 0)
    for number in range(edge_blocks):
        live = lane < tails[0][:1, 2 + number : 3 + number]
        sender = jnp.where(live, mine[0][number : number + 1], -1)
        receiver = jnp.where(live, mine[1][number : number + 1], -1)
        outside = sender - rows
        turned = jnp.where(outside < block, outside + block, outside - block)
        outside = jnp.where(outside >= 0, jnp.where(first_core, turned, outside), -1)
        here = slice(number * block, (number + 1) * block)
        received = slice(edges + number * block, edges + (number + 1) * block)
        for index, at, table, table_t in (
            (sender, here, gown, gown_t),
            (receiver, received, gown, gown_t),
            (outside, here, ghalo, ghalo_t),
        ):
            hot = (index == (halo_row if table is ghalo else row)).astype(F32)
            table_t[:, at] = hot.astype(BF16)
            table[at, :] = hot.T.astype(BF16)

    def whole(tail, place):
        return jnp.broadcast_to(tail[:1, place : place + 1], (1, block))

    to_next, to_prev = whole(tails[0], 0), whole(tails[0], 1)
    lists[0:1, :] = jnp.where(first_core, to_next, to_prev)
    lists[1:2, :] = jnp.where(first_core, to_prev, to_next)
    mate[...] = jnp.where(first_core, whole(tails[1], 1), whole(tails[1], 0))
    to_next, to_prev = whole(packed[2], 0), whole(packed[2], 1)
    home_first = lax.axis_index("dom") % 2 == 0
    home_lists[0:1, :] = jnp.where(home_first, to_next, to_prev)
    home_lists[1:2, :] = jnp.where(home_first, to_prev, to_next)


def entry_kernel(mate, here, there, hidden, inner):
    block = inner.shape[0]

    @pl.when(is_local())
    def _():
        hidden[...] = here[...]
        inner[...] = listed(mate[:, :1], there[...], block)

    @pl.when(jnp.logical_not(is_local()))
    def _():
        hidden[...] = there[...]
        inner[...] = listed(mate[:, :1], here[...], block)


def forward_own_kernel(take, h, gown, *refs):
    w_send, w_recv, w_node, _ = quarters(take[0])
    a_out, u_out = refs[-2:]
    edges = gown.shape[0] // 2
    own = mul(gown[...], h[...]).astype(BF16)
    a_out[...] = mul(own[:edges], w_send[...]) + mul(own[edges:], w_recv[...])
    u_out[...] = mul(h[...], w_node[...])


def forward_kernel(take, lists, h, a_own, u_own, inner, outer, ghalo, gown_t, h_out, a_out, u_out, *to):
    packed, gain = take
    w_send, _, _, w_fold = quarters(packed)
    edges = ghalo.shape[0]
    block = inner.shape[0]
    halo = (mul(ghalo[:, :block], inner[...]) + mul(ghalo[:, block:], outer[...])).astype(BF16)
    a = a_own[...] + mul(halo, w_send[...])
    a_out[...] = a
    q = (a * jax.nn.sigmoid(a)).astype(BF16)
    u = u_own[...] + mul(mul(gown_t[:, edges:], q).astype(BF16), w_fold[...])
    u_out[...] = u
    t, _ = normalize(u * jax.nn.sigmoid(u))
    out = (h[...].astype(F32) + t * gain[...]).astype(BF16)
    h_out[...] = out
    for side, ref in enumerate(to):
        ref[...] = listed(lists[side : side + 1, :1], out, block)


def save_kernel(plane, parity, a, u, h, *refs):
    t_out, r_out, s_out, h_out = refs[-4:]
    rows, edges = h.shape[0], a.shape[0]
    at = slice(parity * rows, (parity + 1) * rows)

    @pl.when(here_is(plane))
    def _():
        s_out[parity * edges : (parity + 1) * edges, :] = slope(a[...]).astype(BF16)
        u_value = u[...]
        t, inverse = normalize(u_value * jax.nn.sigmoid(u_value))
        t_out[at, :] = t.astype(BF16)
        r_out[at, :] = (inverse * slope(u_value)).astype(BF16)
        h_out[at, :] = h[...]


def backward_kernel(halo_in, finish, parity, kept, take, *refs):
    packed, gain = take
    w_send, _, _, w_fold = quarters(packed)
    lists, upstream, *refs = refs[kept:]
    if halo_in:
        inner, outer, *refs = refs
    t_in, r_in, s_in, gown, ghalo_t, c_out, du_out, da_out, es_out, *done, to_inner, to_outer = refs
    edges = gown.shape[0] // 2
    rows = upstream.shape[0]
    block = to_inner.shape[0]
    at = slice(parity * rows, (parity + 1) * rows)
    at_edges = slice(parity * edges, (parity + 1) * edges)
    c_out[...] = upstream[...].astype(F32)
    if halo_in:
        add_listed(lists[INNER : INNER + 1, :1], c_out, inner[...].astype(F32), block)
        add_listed(lists[OUTER : OUTER + 1, :1], c_out, outer[...].astype(F32), block)
    if finish:
        done[0][...] = c_out[...].astype(BF16)
    g = c_out[...] * gain[...]
    t = t_in[at, :].astype(F32)
    centre = jnp.mean(g, axis=-1, keepdims=True)
    along = jnp.mean(g * t, axis=-1, keepdims=True)
    du = ((g - centre - t * along) * r_in[at, :].astype(F32)).astype(BF16)
    du_out[...] = du
    spread = mul(gown[edges:, :], du).astype(BF16)
    da = (mul_t(spread, w_fold[...]) * s_in[at_edges, :].astype(F32)).astype(BF16)
    da_out[...] = da
    es = mul_t(da, w_send[...]).astype(BF16)
    es_out[...] = es
    halo = mul(ghalo_t[...], es).astype(BF16)
    to_inner[...] = halo[:block]
    to_outer[...] = halo[block:]


def backward_own_kernel(kept, take, *refs):
    _, w_recv, w_node, _ = quarters(take[0])
    first, refs = refs[:kept], refs[kept:]
    *beside, c, du, da, es, gown_t, out = refs
    er = mul_t(da[...], w_recv[...]).astype(BF16)
    both = jnp.concatenate([es[...], er], axis=0)
    total = c[...] + mul_t(du[...], w_node[...]) + mul(gown_t[...], both)
    if first:
        _, other, lists = first
        [inner] = beside
        block = inner.shape[0]
        at = lists[INNER : INNER + 1, :1]
        value = inner[...].astype(F32)
        total = total + jnp.concatenate(
            [jnp.where(at == number, value, 0.0) for number in range(total.shape[0] // block)], axis=0
        )
        out[total.shape[0] :, :] = other[...]
    out[: total.shape[0], :] = total.astype(out.dtype)


def add_kernel(lists, value, inner, outer, other, out, total):
    @pl.when(here_is(1))
    def _():
        rows = value.shape[0]
        total[...] = value[...].astype(F32)
        add_listed(lists[INNER : INNER + 1, :1], total, inner[...].astype(F32), inner.shape[0])
        add_listed(lists[OUTER : OUTER + 1, :1], total, outer[...].astype(F32), outer.shape[0])
        out[:rows, :] = total[...].astype(BF16)
        out[rows:, :] = other[...]


def place_kernel(lists, outer, out):
    block = outer.shape[0]
    at = lists[OUTER : OUTER + 1, :1]
    value = jnp.where(here_is(0), outer[...].astype(F32), 0.0)
    for number in range(out.shape[0] // block):
        out[number * block : (number + 1) * block, :] = jnp.where(at == number, value, 0.0)


def last_kernel(ends, placed, first_home, second_home, grads, home, turned):
    rows = placed.shape[0]
    grads[:rows, :] = (ends[:rows, :].astype(F32) + placed[...]).astype(BF16)
    grads[rows:, :] = ends[rows:, :]

    @pl.when(here_is(0))
    def _():
        home[...] = first_home[...]

    @pl.when(jnp.logical_not(here_is(0)))
    def _():
        home[...] = second_home[...]

    for place, value in enumerate((home, grads)):
        for parity in range(2):

            @pl.when(here_is(parity=1 - parity))
            def _(value=value, place=place, parity=parity):
                turned[place * rows : (place + 1) * rows, :] = value[parity * rows : (parity + 1) * rows, :]


def write_kernel(home, grads, arrived, out_home, out_grads, sems):
    core = lax.axis_index("pipe") % 2
    rows = home.shape[0] // 2
    copies = []
    for place, (value, out) in enumerate(((home, out_home), (grads, out_grads))):
        own = value.at[pl.ds(pl.multiple_of(core * rows, rows), rows), :]
        other = arrived.at[pl.ds(place * rows, rows), :]
        copies.append(pltpu.make_async_copy(own, out.at[0, core], sems.at[2 * place]))
        copies.append(pltpu.make_async_copy(other, out.at[0, 1 - core], sems.at[2 * place + 1]))
    for copy in copies:
        copy.start()
    for copy in copies:
        copy.wait()


def run(kernel, operands, outs, spaces=(), aliases=None, out_spaces=(), scratch=(), cost=1, vmem=12):
    spaces = tuple(spaces) + (pltpu.VMEM,) * (len(operands) - len(spaces))
    out_spaces = tuple(out_spaces) + (pltpu.VMEM,) * (len(outs) - len(out_spaces))
    return pl.pallas_call(
        kernel,
        out_shape=[jax.ShapeDtypeStruct(s, t) for s, t in outs],
        in_specs=[pl.BlockSpec(memory_space=space) for space in spaces],
        out_specs=[pl.BlockSpec(memory_space=space) for space in out_spaces],
        scratch_shapes=list(scratch),
        input_output_aliases=aliases or {},
        compiler_params=pltpu.CompilerParams(vmem_limit_bytes=vmem * 2**20),
        cost_estimate=pl.CostEstimate(flops=cost, bytes_accessed=1, transcendentals=0),
    )(*operands)


def run_section(body, plane, matrices, operands, outs, elsewhere=None, cost=1):
    elsewhere = elsewhere or {}

    def kernel(*refs):
        take, rest = refs[: len(matrices)], refs[len(matrices) :]

        @pl.when(here_is(plane))
        def _():
            body(take, *rest)

        if elsewhere:

            @pl.when(jnp.logical_not(here_is(plane)))
            def _():
                for source, target in elsewhere.items():
                    rest[target][...] = rest[source][...]

    return run(kernel, tuple(matrices) + tuple(operands), outs, cost=cost)


def shards(
    inputs,
    cotangent,
    w_send,
    w_recv,
    w_message,
    w_node,
    w_aggregate,
    gains,
    edge_send,
    edge_recv,
    edge_count,
    halo_send,
):
    sections = lax.axis_size("pipe")
    pairs_total = lax.axis_size("dom") // 2
    phase = lax.axis_index("pipe")
    y = lax.rem(lax.axis_index("dom"), 2)
    plane_here = phase // 2
    rows, latent = inputs.shape[1:]
    edge_blocks, block = edge_send.shape
    edges = edge_blocks * block

    def send(value, rule):
        table = []
        for z in range(pairs_total):
            for which in range(2):
                for x in range(sections // 2):
                    for c in range(2):
                        if (target := rule(z, which, x, c)) is None:
                            continue
                        tz, ty, tx, tc = target
                        target = (2 * (tz % pairs_total) + ty) * sections + 2 * (tx % (sections // 2)) + tc
                        table.append(((2 * z + which) * sections + 2 * x + c, target))
        return lax.ppermute(value, AXES, table)

    def flip_y(value):
        return send(value, lambda z, y, x, c: (z, 1 - y, x, c))

    def flip_core(value):
        return send(value, lambda z, y, x, c: (z, y, x, 1 - c))

    def to_home(value):
        return send(value, lambda z, y, x, c: (z, c, x, y))

    def towards(value, side, step):
        if side == INNER:
            return send(value, lambda z, y, x, c: (z, y, x + step, 1 - c))
        return send(value, lambda z, y, x, c: (z + 2 * c - 1, y, x + step, 1 - c))

    wide = (rows, latent)
    edge_wide = (edges, latent)
    narrow = (block, latent)
    unit = 2 * rows * latent * latent
    dma = pltpu.SemaphoreType.DMA

    here, there, boundary, weights, packed = run(
        prepare_kernel,
        (edge_count, jnp.swapaxes(halo_send, 1, 2), inputs, cotangent, edge_send, edge_recv)
        + (w_send[0], w_recv[0], w_node[0], w_message[0], w_aggregate[0]),
        [
            (wide, BF16),
            (wide, BF16),
            (narrow, BF16),
            ((4 * latent, latent), BF16),
            ((3, 8, block), jnp.int32),
        ],
        spaces=(pltpu.SMEM, pltpu.SMEM) + (pltpu.HBM,) * 9,
        scratch=[pltpu.VMEM((2, latent, latent), BF16), pltpu.VMEM((latent, latent), BF16), dma((5,)), dma((6,))],
        vmem=56,
    )
    packed_there = send(packed, lambda z, y, x, c: (z, 1 - y, x, 1 - c))
    there = flip_y(there)
    outer = send(boundary, lambda z, y, x, c: (z + 2 * y - 1, c, x, 1 - y))
    even, odd = run(arrange_kernel, (weights, flip_core(weights)), [((4 * latent, latent), BF16)] * 2)
    gain_even, gain_odd = run(arrange_kernel, (gains, flip_core(gains)), [((1, latent), F32)] * 2)
    matrices = ((even, gain_even), (odd, gain_odd))

    gown, gown_t, ghalo, ghalo_t, lists, mate, home_lists = run(
        functools.partial(graph_kernel, edge_blocks),
        (even, packed, packed_there),
        [
            ((2 * edges, rows), BF16),
            ((rows, 2 * edges), BF16),
            ((edges, 2 * block), BF16),
            ((2 * block, edges), BF16),
            ((2, block), jnp.int32),
            ((1, block), jnp.int32),
            ((2, block), jnp.int32),
        ],
    )
    hidden, inner = run(entry_kernel, (mate, here, there), [(wide, BF16), (narrow, BF16)])
    upstream = hidden

    def home_of_plane(value, plane):
        return send(value, lambda z, y, x, c: (z, c, x, y) if x == plane else None)

    saved = ()
    arrived = ()
    for tick in range(sections):
        plane, parity = tick // 2, tick % 2
        packed, gain = matrices[parity]
        a_own, u_own = run_section(
            forward_own_kernel, plane, (packed,), (hidden, gown) + arrived, [(edge_wide, F32), (wide, F32)], cost=BESIDE
        )
        to_send = [(narrow, BF16)] * 2 if tick < sections - 1 else []
        hidden, a, u, *to = run_section(
            forward_kernel,
            plane,
            (packed, gain),
            (lists, hidden, a_own, u_own, inner, outer, ghalo, gown_t),
            [(wide, BF16), (edge_wide, F32), (wide, F32)] + to_send,
        )
        produced = hidden
        if to:
            step = (tick + 1) // 2 - plane
            outer = towards(to[OUTER], OUTER, step)
            if step:
                hidden = send(hidden, lambda z, y, x, c: (z, y, x + 1, c))
            inner = towards(to[INNER], INNER, step)
            arrived = () if step else (inner,)
        saved = run(
            functools.partial(save_kernel, plane, parity),
            (a, u, produced) + tuple(saved),
            [((2 * rows, latent), BF16), ((2 * rows, latent), BF16), ((2 * edges, latent), BF16), ((2 * rows, latent), BF16)],
            aliases={3 + k: k for k in range(4)} if saved else None,
            cost=BESIDE,
        )

    *states, both = saved
    inner = outer = None
    handed = ()
    finished = {}
    for tick in range(sections - 1, -1, -1):
        plane, parity = tick // 2, tick % 2
        packed, gain = matrices[parity]
        step = (tick - 1) // 2 - plane if tick else 0
        halo_in = inner is not None
        finish = halo_in and tick % 2 == 0
        outs = [(wide, F32), (wide, BF16), (edge_wide, BF16), (edge_wide, BF16)]
        outs += [(wide, BF16)] if finish else []
        outs += [(narrow, BF16)] * 2
        kept = handed if tick == 1 else ()
        c, du, da, es, *done, to_inner, to_outer = run_section(
            functools.partial(backward_kernel, halo_in, finish, parity, len(kept)),
            plane,
            (packed, gain),
            kept + (lists, upstream) + ((inner, outer) if halo_in else ()) + tuple(states) + (gown, ghalo_t),
            outs,
            elsewhere={0: -2, 1: -1} if tick == 1 else {},
        )
        if done:
            finished[tick + 1] = done[0]
        if step == 0:
            inner = towards(to_inner, INNER, 0)
            if tick:
                outer = towards(to_outer, OUTER, 0)
        else:
            handed = (to_inner, to_outer)
            outer = towards(to_outer, OUTER, step)
            inner = towards(to_inner, INNER, step)
        beside = (inner,) if step == 0 else (first_home,)
        kept = (finished[2], finished[1], lists) if tick == 0 else ()
        [upstream] = run_section(
            functools.partial(backward_own_kernel, len(kept)),
            plane,
            (packed,),
            kept + beside + (c, du, da, es, gown_t),
            [((2 * rows, latent), BF16) if tick == 0 else (wide, BF16 if step else F32)],
            elsewhere={0: -1} if tick == 0 else {},
            cost=BESIDE if tick else 1,
        )
        if tick == sections - 1:
            first_home, upstream = lax.optimization_barrier((both, upstream))
            first_home = home_of_plane(first_home, 0)
        if step:
            own = upstream
            upstream = send(upstream, lambda z, y, x, c: (z, y, x + 1, c))
        elif tick == 1:
            second_home, upstream = lax.optimization_barrier((both, upstream))
            second_home = home_of_plane(second_home, 1)
            [finished[2]] = run(
                add_kernel,
                (lists, own, inner, outer, finished[3]),
                [((2 * rows, latent), BF16)],
                scratch=[pltpu.VMEM(wide, F32)],
            )

    final_outer = send(to_outer, lambda z, y, x, c: (z + 2 * c - 1, 1 - c, x, y))
    ends = to_home(upstream)
    [placed] = run(place_kernel, (home_lists, final_outer), [(wide, F32)], cost=LONG)
    grads, home, turned = run(last_kernel, (ends, placed, first_home, second_home), [((2 * rows, latent), BF16)] * 3)
    return tuple(
        run(
            write_kernel,
            (home, grads, flip_core(turned)),
            [((1, 2) + wide, BF16)] * 2,
            out_spaces=(pltpu.HBM,) * 2,
            scratch=[dma((4,))],
        )
    )


def solution(mesh):
    in_specs = (
        P(None, "dom", None),
        P(None, "dom", None),
        P("pipe", None, None),
        P("pipe", None, None),
        P("pipe", None, None),
        P("pipe", None, None),
        P("pipe", None, None),
        P("pipe", None),
        P("dom", None),
        P("dom", None),
        P("dom"),
        P("dom", None, None),
    )
    out_specs = (P("pipe", None, "dom", None), P("pipe", None, "dom", None))
    return jax.shard_map(shards, mesh=mesh, in_specs=in_specs, out_specs=out_specs, check_vma=False)
```

```python
import functools

import jax
import jax.numpy as jnp
from jax import lax
from jax.experimental import pallas as pl
from jax.experimental.pallas import tpu as pltpu
from jax.sharding import PartitionSpec as P

EPSILON = 1e-05
F32 = jnp.float32
BF16 = jnp.bfloat16
AXES = ("dom", "pipe")
INNER, OUTER = 0, 1
BESIDE = 4 * 10**9
LONG = 2 * 10**10


def mul(a, b):
    return jnp.dot(a, b, preferred_element_type=F32)


def mul_t(a, b):
    return lax.dot_general(a, b, (((1,), (1,)), ((), ())), preferred_element_type=F32)


def slope(v):
    s = jax.nn.sigmoid(v)
    return s * (1.0 + v * (1.0 - s))


def normalize(z):
    centred = z - jnp.mean(z, axis=-1, keepdims=True)
    inverse = lax.rsqrt(jnp.mean(centred * centred, axis=-1, keepdims=True) + EPSILON)
    return centred * inverse, inverse


def quarters(packed):
    depth = packed.shape[0] // 4
    return [packed.at[pl.ds(number * depth, depth), :] for number in range(4)]


def here_is(plane=None, parity=None):
    pipe = lax.axis_index("pipe")
    wanted = jnp.bool_(True)
    if plane is not None:
        wanted = pipe // 2 == plane
    if parity is not None:
        wanted = wanted & (pipe % 2 == parity)
    return wanted


def is_local():
    return lax.axis_index("pipe") % 2 == lax.axis_index("dom") % 2


def listed(at, value, block):
    picked = value[:block]
    for number in range(1, value.shape[0] // block):
        picked = jnp.where(at == number, value[number * block : (number + 1) * block], picked)
    return picked


def add_listed(at, target, value, block):
    for number in range(target.shape[0] // block):
        rows = slice(number * block, (number + 1) * block)
        target[rows, :] = target[rows, :] + jnp.where(at == number, value, 0.0)


def prepare_kernel(
    count,
    halo,
    inputs,
    cotangent,
    send_in,
    recv_in,
    w_send,
    w_recv,
    w_node,
    w_message,
    w_aggregate,
    here,
    there,
    boundary,
    weights,
    packed,
    factors,
    product,
    sems,
    weight_sems,
):
    micro = lax.axis_index("dom") % 2
    block = boundary.shape[0]
    depth = w_send.shape[0]
    edge_blocks = send_in.shape[0]
    number = jnp.where(micro == 1, halo[0, 0, 0], halo[0, 0, 1])
    start = pl.multiple_of(number * block, block)

    def fetch(source):
        return [
            pltpu.make_async_copy(source.at[1 - micro], there, sems.at[0]),
            pltpu.make_async_copy(
                source.at[lax.axis_index("pipe") % 2, pl.ds(start, block), :], boundary, sems.at[1]
            ),
            pltpu.make_async_copy(source.at[micro], here, sems.at[2]),
        ]

    @pl.when(here_is(0))
    def _():
        for copy in fetch(inputs):
            copy.start()

    @pl.when(jnp.logical_not(here_is(0)))
    def _():
        for copy in fetch(cotangent):
            copy.start()

    copies = [
        pltpu.make_async_copy(ref, factors.at[k], weight_sems.at[k]) for k, ref in enumerate((w_message, w_aggregate))
    ]
    copies += [
        pltpu.make_async_copy(ref, packed.at[k, pl.ds(0, edge_blocks), :], sems.at[3 + k])
        for k, ref in enumerate((send_in, recv_in))
    ]
    copies += [
        pltpu.make_async_copy(ref, weights.at[pl.ds(k * depth, depth), :], weight_sems.at[2 + k])
        for k, ref in enumerate((w_send, w_recv, w_node))
    ]
    for copy in copies:
        copy.start()
    lane = lax.broadcasted_iota(jnp.int32, packed.shape[1:], 1)
    tail = jnp.where(lane == 0, halo[0, 0, 0], halo[0, 0, 1])
    for place in range(edge_blocks):
        tail = jnp.where(lane == 2 + place, count[place], tail)
    packed[2] = tail
    for copy in copies[:2]:
        copy.wait()
    product[...] = mul(factors[0], factors[1]).astype(BF16)
    last = pltpu.make_async_copy(product, weights.at[pl.ds(3 * depth, depth), :], weight_sems.at[5])
    last.start()
    for copy in copies[2:] + fetch(inputs):
        copy.wait()
    last.wait()


def arrange_kernel(mine, swapped, even, odd):
    @pl.when(here_is(parity=0))
    def _():
        even[...] = mine[...]
        odd[...] = swapped[...]

    @pl.when(here_is(parity=1))
    def _():
        even[...] = swapped[...]
        odd[...] = mine[...]


def graph_kernel(edge_blocks, _, packed, packed_there, gown, gown_t, ghalo, ghalo_t, lists, mate, home_lists):
    block = packed.shape[2]
    rows = gown_t.shape[0]
    edges = edge_blocks * block
    local = is_local()
    first_core = lax.axis_index("pipe") % 2 == 0
    mine = [jnp.where(local, packed[k], packed_there[k]) for k in range(3)]
    tails = mine[2], jnp.where(local, packed_there[2], packed[2])
    lane = lax.broadcasted_iota(jnp.int32, (1, block), 1)
    row = lax.broadcasted_iota(jnp.int32, (rows, block), 0)
    halo_row = lax.broadcasted_iota(jnp.int32, (2 * block, block), 0)
    for number in range(edge_blocks):
        live = lane < tails[0][:1, 2 + number : 3 + number]
        sender = jnp.where(live, mine[0][number : number + 1], -1)
        receiver = jnp.where(live, mine[1][number : number + 1], -1)
        outside = sender - rows
        turned = jnp.where(outside < block, outside + block, outside - block)
        outside = jnp.where(outside >= 0, jnp.where(first_core, turned, outside), -1)
        here = slice(number * block, (number + 1) * block)
        received = slice(edges + number * block, edges + (number + 1) * block)
        for index, at, table, table_t in (
            (sender, here, gown, gown_t),
            (receiver, received, gown, gown_t),
            (outside, here, ghalo, ghalo_t),
        ):
            hot = (index == (halo_row if table is ghalo else row)).astype(F32)
            table_t[:, at] = hot.astype(BF16)
            table[at, :] = hot.T.astype(BF16)

    def whole(tail, place):
        return jnp.broadcast_to(tail[:1, place : place + 1], (1, block))

    to_next, to_prev = whole(tails[0], 0), whole(tails[0], 1)
    lists[0:1, :] = jnp.where(first_core, to_next, to_prev)
    lists[1:2, :] = jnp.where(first_core, to_prev, to_next)
    mate[...] = jnp.where(first_core, whole(tails[1], 1), whole(tails[1], 0))
    to_next, to_prev = whole(packed[2], 0), whole(packed[2], 1)
    home_first = lax.axis_index("dom") % 2 == 0
    home_lists[0:1, :] = jnp.where(home_first, to_next, to_prev)
    home_lists[1:2, :] = jnp.where(home_first, to_prev, to_next)


def entry_kernel(mate, here, there, hidden, inner):
    block = inner.shape[0]

    @pl.when(is_local())
    def _():
        hidden[...] = here[...]
        inner[...] = listed(mate[:, :1], there[...], block)

    @pl.when(jnp.logical_not(is_local()))
    def _():
        hidden[...] = there[...]
        inner[...] = listed(mate[:, :1], here[...], block)


def forward_own_kernel(take, h, gown, *refs):
    w_send, w_recv, w_node, _ = quarters(take[0])
    a_out, u_out = refs[-2:]
    edges = gown.shape[0] // 2
    own = mul(gown[...], h[...]).astype(BF16)
    a_out[...] = mul(own[:edges], w_send[...]) + mul(own[edges:], w_recv[...])
    u_out[...] = mul(h[...], w_node[...])


def forward_kernel(take, lists, h, a_own, u_own, inner, outer, ghalo, gown_t, h_out, a_out, u_out, *to):
    packed, gain = take
    w_send, _, _, w_fold = quarters(packed)
    edges = ghalo.shape[0]
    block = inner.shape[0]
    halo = (mul(ghalo[:, :block], inner[...]) + mul(ghalo[:, block:], outer[...])).astype(BF16)
    a = a_own[...] + mul(halo, w_send[...])
    a_out[...] = a
    q = (a * jax.nn.sigmoid(a)).astype(BF16)
    u = u_own[...] + mul(mul(gown_t[:, edges:], q).astype(BF16), w_fold[...])
    u_out[...] = u
    t, _ = normalize(u * jax.nn.sigmoid(u))
    out = (h[...].astype(F32) + t * gain[...]).astype(BF16)
    h_out[...] = out
    for side, ref in enumerate(to):
        ref[...] = listed(lists[side : side + 1, :1], out, block)


def save_kernel(plane, parity, a, u, h, *refs):
    t_out, r_out, s_out, h_out = refs[-4:]
    rows, edges = h.shape[0], a.shape[0]
    at = slice(parity * rows, (parity + 1) * rows)

    @pl.when(here_is(plane))
    def _():
        s_out[parity * edges : (parity + 1) * edges, :] = slope(a[...]).astype(BF16)
        u_value = u[...]
        t, inverse = normalize(u_value * jax.nn.sigmoid(u_value))
        t_out[at, :] = t.astype(BF16)
        r_out[at, :] = (inverse * slope(u_value)).astype(BF16)
        h_out[at, :] = h[...]


def backward_kernel(halo_in, finish, parity, kept, take, *refs):
    packed, gain = take
    w_send, _, _, w_fold = quarters(packed)
    lists, upstream, *refs = refs[kept:]
    if halo_in:
        inner, outer, *refs = refs
    t_in, r_in, s_in, gown, ghalo_t, c_out, du_out, da_out, es_out, *done, to_inner, to_outer = refs
    edges = gown.shape[0] // 2
    rows = upstream.shape[0]
    block = to_inner.shape[0]
    at = slice(parity * rows, (parity + 1) * rows)
    at_edges = slice(parity * edges, (parity + 1) * edges)
    c_out[...] = upstream[...].astype(F32)
    if halo_in:
        add_listed(lists[INNER : INNER + 1, :1], c_out, inner[...].astype(F32), block)
        add_listed(lists[OUTER : OUTER + 1, :1], c_out, outer[...].astype(F32), block)
    if finish:
        done[0][...] = c_out[...].astype(BF16)
    g = c_out[...] * gain[...]
    t = t_in[at, :].astype(F32)
    centre = jnp.mean(g, axis=-1, keepdims=True)
    along = jnp.mean(g * t, axis=-1, keepdims=True)
    du = ((g - centre - t * along) * r_in[at, :].astype(F32)).astype(BF16)
    du_out[...] = du
    spread = mul(gown[edges:, :], du).astype(BF16)
    da = (mul_t(spread, w_fold[...]) * s_in[at_edges, :].astype(F32)).astype(BF16)
    da_out[...] = da
    es = mul_t(da, w_send[...]).astype(BF16)
    es_out[...] = es
    halo = mul(ghalo_t[...], es).astype(BF16)
    to_inner[...] = halo[:block]
    to_outer[...] = halo[block:]


def backward_own_kernel(kept, take, *refs):
    _, w_recv, w_node, _ = quarters(take[0])
    first, refs = refs[:kept], refs[kept:]
    refs, out = (refs[:-2], refs[-2:]) if first else (refs[:-1], refs[-1:])
    *beside, c, du, da, es, gown_t = refs
    er = mul_t(da[...], w_recv[...]).astype(BF16)
    both = jnp.concatenate([es[...], er], axis=0)
    total = c[...] + mul_t(du[...], w_node[...]) + mul(gown_t[...], both)
    if not first:
        out[0][...] = total.astype(out[0].dtype)
        return
    *_, other, lists = first
    [inner] = beside
    block = inner.shape[0]
    at = lists[INNER : INNER + 1, :1]
    value = inner[...].astype(F32)
    total = total + jnp.concatenate(
        [jnp.where(at == number, value, 0.0) for number in range(total.shape[0] // block)], axis=0
    )
    order(total.astype(BF16), other[...], *out)


def order(even, odd, first, second):
    zero = lax.axis_index("dom") % 2 == 0

    @pl.when(zero)
    def _():
        first[...] = even
        second[...] = odd

    @pl.when(jnp.logical_not(zero))
    def _():
        first[...] = odd
        second[...] = even


def order_kernel(both, first, second):
    rows = first.shape[0]
    order(both[:rows, :], both[rows:, :], first, second)


def add_kernel(lists, value, inner, outer, other, first, second, total):
    @pl.when(here_is(1))
    def _():
        total[...] = value[...].astype(F32)
        add_listed(lists[INNER : INNER + 1, :1], total, inner[...].astype(F32), inner.shape[0])
        add_listed(lists[OUTER : OUTER + 1, :1], total, outer[...].astype(F32), outer.shape[0])
        order(total[...].astype(BF16), other[...], first, second)


def place_kernel(lists, outer, flipped, first, second):
    block = outer.shape[0]
    at = lists[OUTER : OUTER + 1, :1]
    for value, out in ((outer, first), (flipped, second)):
        for number in range(out.shape[0] // block):
            covered = jnp.broadcast_to(at == number, value.shape) & here_is(0, 0)
            out[number * block : (number + 1) * block, :] = jnp.where(covered, value[...].astype(F32), 0.0).astype(BF16)


def sum_kernel(*refs):
    ends, placed, totals = (refs[2 * k : 2 * k + 2] for k in range(3))
    for k in range(2):
        totals[k][...] = (ends[k][...].astype(F32) + placed[k][...].astype(F32)).astype(BF16)


def write_kernel(*refs):
    first_home, second_home, totals = (refs[2 * k : 2 * k + 2] for k in range(3))
    out_home, out_grads, sems = refs[6:]
    core = lax.axis_index("pipe") % 2
    slots = core, 1 - core

    def outputs(source):
        return [pltpu.make_async_copy(source[k], out_home.at[0, slots[k]], sems.at[k]) for k in range(2)]

    copies = [pltpu.make_async_copy(totals[k], out_grads.at[0, slots[k]], sems.at[2 + k]) for k in range(2)]
    for copy in copies:
        copy.start()

    @pl.when(here_is(0))
    def _():
        for copy in outputs(first_home):
            copy.start()

    @pl.when(jnp.logical_not(here_is(0)))
    def _():
        for copy in outputs(second_home):
            copy.start()

    for copy in copies + outputs(first_home):
        copy.wait()


def run(kernel, operands, outs, spaces=(), aliases=None, out_spaces=(), scratch=(), cost=1, vmem=12):
    spaces = tuple(spaces) + (pltpu.VMEM,) * (len(operands) - len(spaces))
    out_spaces = tuple(out_spaces) + (pltpu.VMEM,) * (len(outs) - len(out_spaces))
    return pl.pallas_call(
        kernel,
        out_shape=[jax.ShapeDtypeStruct(s, t) for s, t in outs],
        in_specs=[pl.BlockSpec(memory_space=space) for space in spaces],
        out_specs=[pl.BlockSpec(memory_space=space) for space in out_spaces],
        scratch_shapes=list(scratch),
        input_output_aliases=aliases or {},
        compiler_params=pltpu.CompilerParams(vmem_limit_bytes=vmem * 2**20),
        cost_estimate=pl.CostEstimate(flops=cost, bytes_accessed=1, transcendentals=0),
    )(*operands)


def run_section(body, plane, matrices, operands, outs, elsewhere=None, cost=1):
    elsewhere = elsewhere or {}

    def kernel(*refs):
        take, rest = refs[: len(matrices)], refs[len(matrices) :]

        @pl.when(here_is(plane))
        def _():
            body(take, *rest)

        if elsewhere:

            @pl.when(jnp.logical_not(here_is(plane)))
            def _():
                for source, target in elsewhere.items():
                    rest[target][...] = rest[source][...]

    return run(kernel, tuple(matrices) + tuple(operands), outs, cost=cost)


def shards(
    inputs,
    cotangent,
    w_send,
    w_recv,
    w_message,
    w_node,
    w_aggregate,
    gains,
    edge_send,
    edge_recv,
    edge_count,
    halo_send,
):
    sections = lax.axis_size("pipe")
    pairs_total = lax.axis_size("dom") // 2
    phase = lax.axis_index("pipe")
    y = lax.rem(lax.axis_index("dom"), 2)
    plane_here = phase // 2
    rows, latent = inputs.shape[1:]
    edge_blocks, block = edge_send.shape
    edges = edge_blocks * block

    def send(value, rule):
        table = []
        for z in range(pairs_total):
            for which in range(2):
                for x in range(sections // 2):
                    for c in range(2):
                        if (target := rule(z, which, x, c)) is None:
                            continue
                        tz, ty, tx, tc = target
                        target = (2 * (tz % pairs_total) + ty) * sections + 2 * (tx % (sections // 2)) + tc
                        table.append(((2 * z + which) * sections + 2 * x + c, target))
        return lax.ppermute(value, AXES, table)

    def flip_y(value):
        return send(value, lambda z, y, x, c: (z, 1 - y, x, c))

    def flip_core(value):
        return send(value, lambda z, y, x, c: (z, y, x, 1 - c))

    def go_home(first, second, plane=None):
        return (
            send(first, lambda z, y, x, c: (z, c, x, y) if plane in (None, x) else None),
            send(second, lambda z, y, x, c: (z, c, x, 1 - y) if plane in (None, x) else None),
        )

    def towards(value, side, step):
        if side == INNER:
            return send(value, lambda z, y, x, c: (z, y, x + step, 1 - c))
        return send(value, lambda z, y, x, c: (z + 2 * c - 1, y, x + step, 1 - c))

    wide = (rows, latent)
    edge_wide = (edges, latent)
    narrow = (block, latent)
    unit = 2 * rows * latent * latent
    dma = pltpu.SemaphoreType.DMA

    here, there, boundary, weights, packed = run(
        prepare_kernel,
        (edge_count, jnp.swapaxes(halo_send, 1, 2), inputs, cotangent, edge_send, edge_recv)
        + (w_send[0], w_recv[0], w_node[0], w_message[0], w_aggregate[0]),
        [
            (wide, BF16),
            (wide, BF16),
            (narrow, BF16),
            ((4 * latent, latent), BF16),
            ((3, 8, block), jnp.int32),
        ],
        spaces=(pltpu.SMEM, pltpu.SMEM) + (pltpu.HBM,) * 9,
        scratch=[pltpu.VMEM((2, latent, latent), BF16), pltpu.VMEM((latent, latent), BF16), dma((5,)), dma((6,))],
        vmem=56,
    )
    packed_there = send(packed, lambda z, y, x, c: (z, 1 - y, x, 1 - c))
    there = flip_y(there)
    outer = send(boundary, lambda z, y, x, c: (z + 2 * y - 1, c, x, 1 - y))
    even, odd = run(arrange_kernel, (weights, flip_core(weights)), [((4 * latent, latent), BF16)] * 2)
    gain_even, gain_odd = run(arrange_kernel, (gains, flip_core(gains)), [((1, latent), F32)] * 2)
    matrices = ((even, gain_even), (odd, gain_odd))

    gown, gown_t, ghalo, ghalo_t, lists, mate, home_lists = run(
        functools.partial(graph_kernel, edge_blocks),
        (even, packed, packed_there),
        [
            ((2 * edges, rows), BF16),
            ((rows, 2 * edges), BF16),
            ((edges, 2 * block), BF16),
            ((2 * block, edges), BF16),
            ((2, block), jnp.int32),
            ((1, block), jnp.int32),
            ((2, block), jnp.int32),
        ],
    )
    hidden, inner = run(entry_kernel, (mate, here, there), [(wide, BF16), (narrow, BF16)])
    upstream = hidden

    saved = ()
    arrived = ()
    for tick in range(sections):
        plane, parity = tick // 2, tick % 2
        packed, gain = matrices[parity]
        a_own, u_own = run_section(
            forward_own_kernel, plane, (packed,), (hidden, gown) + arrived, [(edge_wide, F32), (wide, F32)], cost=BESIDE
        )
        to_send = [(narrow, BF16)] * 2 if tick < sections - 1 else []
        hidden, a, u, *to = run_section(
            forward_kernel,
            plane,
            (packed, gain),
            (lists, hidden, a_own, u_own, inner, outer, ghalo, gown_t),
            [(wide, BF16), (edge_wide, F32), (wide, F32)] + to_send,
        )
        produced = hidden
        if to:
            step = (tick + 1) // 2 - plane
            outer = towards(to[OUTER], OUTER, step)
            if step:
                hidden = send(hidden, lambda z, y, x, c: (z, y, x + 1, c))
            inner = towards(to[INNER], INNER, step)
            arrived = () if step else (inner,)
        saved = run(
            functools.partial(save_kernel, plane, parity),
            (a, u, produced) + tuple(saved),
            [((2 * rows, latent), BF16), ((2 * rows, latent), BF16), ((2 * edges, latent), BF16), ((2 * rows, latent), BF16)],
            aliases={3 + k: k for k in range(4)} if saved else None,
            cost=BESIDE,
        )

    *states, both = saved
    inner = outer = None
    handed = ()
    finished = {}
    for tick in range(sections - 1, -1, -1):
        plane, parity = tick // 2, tick % 2
        packed, gain = matrices[parity]
        step = (tick - 1) // 2 - plane if tick else 0
        halo_in = inner is not None
        finish = halo_in and tick % 2 == 0
        outs = [(wide, F32), (wide, BF16), (edge_wide, BF16), (edge_wide, BF16)]
        outs += [(wide, BF16)] if finish else []
        outs += [(narrow, BF16)] * 2
        kept = handed if tick == 1 else ()
        c, du, da, es, *done, to_inner, to_outer = run_section(
            functools.partial(backward_kernel, halo_in, finish, parity, len(kept)),
            plane,
            (packed, gain),
            kept + (lists, upstream) + ((inner, outer) if halo_in else ()) + tuple(states) + (gown, ghalo_t),
            outs,
            elsewhere={0: -2, 1: -1} if tick == 1 else {},
            cost=BESIDE // 2 if tick == sections - 2 else 1,
        )
        if done:
            finished[tick + 1] = done[0]
        if step == 0:
            inner = towards(to_inner, INNER, 0)
            if tick:
                outer = towards(to_outer, OUTER, 0)
        else:
            handed = (to_inner, to_outer)
            outer = towards(to_outer, OUTER, step)
            inner = towards(to_inner, INNER, step)
        beside = (inner,) if step == 0 else tuple(first_home)
        kept = tuple(ends) + (finished[1], lists) if tick == 0 else ()
        upstream, *rest = run_section(
            functools.partial(backward_own_kernel, len(kept)),
            plane,
            (packed,),
            kept + beside + (c, du, da, es, gown_t),
            [(wide, BF16)] * 2 if tick == 0 else [(wide, BF16 if step else F32)],
            elsewhere={0: -2, 1: -1} if tick == 0 else {},
            cost=BESIDE if tick else 1,
        )
        if tick == sections - 1:
            outputs, upstream = lax.optimization_barrier((both, upstream))
            first_home = go_home(*run(order_kernel, (outputs,), [(wide, BF16)] * 2), plane=0)
        if step:
            own = upstream
            upstream = send(upstream, lambda z, y, x, c: (z, y, x + 1, c))
        elif tick == 1:
            outputs, upstream = lax.optimization_barrier((both, upstream))
            second_home = go_home(*run(order_kernel, (outputs,), [(wide, BF16)] * 2), plane=1)
            ends = run(
                add_kernel,
                (lists, own, inner, outer, finished[3]),
                [(wide, BF16)] * 2,
                scratch=[pltpu.VMEM(wide, F32)],
            )

    final_outer = send(to_outer, lambda z, y, x, c: (z + 2 * c - 1, 1 - c, x, y))
    ends = go_home(upstream, *rest)
    placed = run(
        place_kernel, (home_lists, final_outer, flip_core(final_outer)), [(wide, BF16)] * 2
    )
    totals = run(sum_kernel, tuple(ends) + tuple(placed), [(wide, BF16)] * 2, cost=LONG)
    return tuple(
        run(
            write_kernel,
            tuple(first_home) + tuple(second_home) + tuple(totals),
            [((1, 2) + wide, BF16)] * 2,
            out_spaces=(pltpu.HBM,) * 2,
            scratch=[dma((4,))],
        )
    )


def solution(mesh):
    in_specs = (
        P(None, "dom", None),
        P(None, "dom", None),
        P("pipe", None, None),
        P("pipe", None, None),
        P("pipe", None, None),
        P("pipe", None, None),
        P("pipe", None, None),
        P("pipe", None),
        P("dom", None),
        P("dom", None),
        P("dom"),
        P("dom", None, None),
    )
    out_specs = (P("pipe", None, "dom", None), P("pipe", None, "dom", None))
    return jax.shard_map(shards, mesh=mesh, in_specs=in_specs, out_specs=out_specs, check_vma=False)
```

```python
import functools

import jax
import jax.numpy as jnp
from jax import lax
from jax.experimental import pallas as pl
from jax.experimental.pallas import tpu as pltpu
from jax.sharding import PartitionSpec as P

EPSILON = 1e-05
F32 = jnp.float32
BF16 = jnp.bfloat16
AXES = ("dom", "pipe")
INNER, OUTER = 0, 1
BESIDE = 4 * 10**9
LONG = 2 * 10**10


def mul(a, b):
    return jnp.dot(a, b, preferred_element_type=F32)


def mul_t(a, b):
    return lax.dot_general(a, b, (((1,), (1,)), ((), ())), preferred_element_type=F32)


def slope(v):
    s = jax.nn.sigmoid(v)
    return s * (1.0 + v * (1.0 - s))


def normalize(z):
    centred = z - jnp.mean(z, axis=-1, keepdims=True)
    inverse = lax.rsqrt(jnp.mean(centred * centred, axis=-1, keepdims=True) + EPSILON)
    return centred * inverse, inverse


def quarters(packed):
    depth = packed.shape[0] // 4
    return [packed.at[pl.ds(number * depth, depth), :] for number in range(4)]


def here_is(plane=None, parity=None):
    pipe = lax.axis_index("pipe")
    wanted = jnp.bool_(True)
    if plane is not None:
        wanted = pipe // 2 == plane
    if parity is not None:
        wanted = wanted & (pipe % 2 == parity)
    return wanted


def is_local():
    return lax.axis_index("pipe") % 2 == lax.axis_index("dom") % 2


def listed(at, value, block):
    picked = value[:block]
    for number in range(1, value.shape[0] // block):
        picked = jnp.where(at == number, value[number * block : (number + 1) * block], picked)
    return picked


def add_listed(at, target, value, block):
    for number in range(target.shape[0] // block):
        rows = slice(number * block, (number + 1) * block)
        target[rows, :] = target[rows, :] + jnp.where(at == number, value, 0.0)


def encode(values):
    high = lax.shift_right_logical(values, 4)
    low = values - high * 16
    return jnp.concatenate([high.astype(F32), low.astype(F32)], axis=0).astype(BF16)


def decode(tile):
    half = tile.shape[0] // 2
    tile = tile.astype(F32)
    return (tile[:half] * 16.0 + tile[half:]).astype(jnp.int32)


def prepare_kernel(
    count_in,
    halo_in,
    inputs,
    cotangent,
    send_in,
    recv_in,
    here,
    there,
    boundary,
    packed,
    count,
    halo,
    here_rows,
    there_rows,
    boundary_rows,
    edges,
    sems,
    out_sems,
):
    micro = lax.axis_index("dom") % 2
    block = boundary.shape[0]
    edge_blocks = send_in.shape[0]
    rows = here.shape[0]
    lists = [
        pltpu.make_async_copy(halo_in, halo, sems.at[0]),
        pltpu.make_async_copy(count_in, count, sems.at[1]),
    ]
    ids = [
        pltpu.make_async_copy(ref, edges.at[k, pl.ds(0, edge_blocks), :], sems.at[2 + k])
        for k, ref in enumerate((send_in, recv_in))
    ]
    def fetch(source):
        return [
            pltpu.make_async_copy(source.at[1 - micro], there_rows.at[pl.ds(0, rows), :], sems.at[4]),
            pltpu.make_async_copy(source.at[micro], here_rows, sems.at[5]),
        ]

    def fetch_boundary(source, number):
        start = pl.multiple_of(number * block, block)
        place = source.at[lax.axis_index("pipe") % 2, pl.ds(start, block), :]
        return pltpu.make_async_copy(place, boundary_rows, sems.at[6])

    for copy in lists + ids:
        copy.start()

    @pl.when(here_is(0))
    def _():
        for copy in fetch(inputs):
            copy.start()

    @pl.when(jnp.logical_not(here_is(0)))
    def _():
        for copy in fetch(cotangent):
            copy.start()

    for copy in lists:
        copy.wait()
    number = jnp.where(micro == 1, halo[0, 0, 0], halo[0, 0, 1])
    fetch_boundary(inputs, number).start()
    for copy in ids:
        copy.wait()
    lane = lax.broadcasted_iota(jnp.int32, (1, block), 1)
    tail = jnp.where(lane == 0, halo[0, 0, 0], jnp.where(lane == 1, halo[0, 0, 1], 0))
    for place in range(edge_blocks):
        tail = jnp.where(lane == 2 + place, count[place], tail)
    spare = jnp.zeros((7 - 2 * edge_blocks, block), jnp.int32)
    tile = encode(jnp.concatenate([edges[0, :edge_blocks, :], edges[1, :edge_blocks, :], tail, spare], axis=0))
    packed[...] = tile
    there_rows[rows:, :] = jnp.zeros((there_rows.shape[0] - rows, there_rows.shape[1]), BF16)
    there_rows[rows:, :block] = tile
    fetched = fetch(inputs)
    leaving = [
        pltpu.make_async_copy(there_rows, there, out_sems.at[0]),
        pltpu.make_async_copy(here_rows, here, out_sems.at[1]),
        pltpu.make_async_copy(boundary_rows, boundary, out_sems.at[2]),
    ]
    fetched[0].wait()
    leaving[0].start()
    fetched[1].wait()
    leaving[1].start()
    fetch_boundary(inputs, number).wait()
    leaving[2].start()
    for copy in leaving:
        copy.wait()


def weights_kernel(w_send, w_recv, w_node, w_message, w_aggregate, out, factors, sems):
    depth = w_send.shape[0]
    copies = [pltpu.make_async_copy(ref, factors.at[k], sems.at[k]) for k, ref in enumerate((w_message, w_aggregate))]
    copies += [
        pltpu.make_async_copy(ref, out.at[pl.ds(k * depth, depth), :], sems.at[2 + k])
        for k, ref in enumerate((w_send, w_recv, w_node))
    ]
    for copy in copies:
        copy.start()
    for copy in copies[:2]:
        copy.wait()
    out[3 * depth :, :] = mul(factors[0], factors[1]).astype(BF16)
    for copy in copies[2:]:
        copy.wait()


def arrange_kernel(mine, swapped, _, even, odd):
    @pl.when(here_is(parity=0))
    def _():
        even[...] = mine[...]
        odd[...] = swapped[...]

    @pl.when(here_is(parity=1))
    def _():
        even[...] = swapped[...]
        odd[...] = mine[...]


def graph_kernel(edge_blocks, packed, there, gown, gown_t, ghalo, ghalo_t, lists, mate, home_lists):
    block = packed.shape[1]
    rows = gown_t.shape[0]
    edges = edge_blocks * block
    local = is_local()
    first_core = lax.axis_index("pipe") % 2 == 0
    last = 2 * edge_blocks
    tiles = decode(packed[...]), decode(there[rows:, :block])
    mine = jnp.where(local, *tiles)
    tails = [tile[last : last + 1] for tile in (mine, jnp.where(local, tiles[1], tiles[0]), tiles[0])]
    lane = lax.broadcasted_iota(jnp.int32, (1, block), 1)
    row = lax.broadcasted_iota(jnp.int32, (rows, block), 0)
    halo_row = lax.broadcasted_iota(jnp.int32, (2 * block, block), 0)
    for number in range(edge_blocks):
        live = lane < tails[0][:, 2 + number : 3 + number]
        sender = jnp.where(live, mine[number : number + 1], -1)
        receiver = jnp.where(live, mine[edge_blocks + number : edge_blocks + number + 1], -1)
        outside = sender - rows
        turned = jnp.where(outside < block, outside + block, outside - block)
        outside = jnp.where(outside >= 0, jnp.where(first_core, turned, outside), -1)
        here = slice(number * block, (number + 1) * block)
        received = slice(edges + number * block, edges + (number + 1) * block)
        for index, at, table, table_t in (
            (sender, here, gown, gown_t),
            (receiver, received, gown, gown_t),
            (outside, here, ghalo, ghalo_t),
        ):
            hot = (index == (halo_row if table is ghalo else row)).astype(F32)
            table_t[:, at] = hot.astype(BF16)
            table[at, :] = hot.T.astype(BF16)

    def whole(tail, place):
        return jnp.broadcast_to(tail[:1, place : place + 1], (1, block))

    to_next, to_prev = whole(tails[0], 0), whole(tails[0], 1)
    lists[0:1, :] = jnp.where(first_core, to_next, to_prev)
    lists[1:2, :] = jnp.where(first_core, to_prev, to_next)
    mate[...] = jnp.where(first_core, whole(tails[1], 1), whole(tails[1], 0))
    to_next, to_prev = whole(tails[2], 0), whole(tails[2], 1)
    home_first = lax.axis_index("dom") % 2 == 0
    home_lists[0:1, :] = jnp.where(home_first, to_next, to_prev)
    home_lists[1:2, :] = jnp.where(home_first, to_prev, to_next)


def entry_kernel(mate, here, there, hidden, inner):
    block = inner.shape[0]

    @pl.when(is_local())
    def _():
        hidden[...] = here[...]
        inner[...] = listed(mate[:, :1], there[: hidden.shape[0], :], block)

    @pl.when(jnp.logical_not(is_local()))
    def _():
        hidden[...] = there[: hidden.shape[0], :]
        inner[...] = listed(mate[:, :1], here[...], block)


def forward_own_kernel(take, h, gown, *refs):
    w_send, w_recv, w_node, _ = quarters(take[0])
    a_out, u_out = refs[-2:]
    edges = gown.shape[0] // 2
    own = mul(gown[...], h[...]).astype(BF16)
    a_out[...] = mul(own[:edges], w_send[...]) + mul(own[edges:], w_recv[...])
    u_out[...] = mul(h[...], w_node[...])


def forward_kernel(take, lists, h, a_own, u_own, inner, outer, ghalo, gown_t, h_out, a_out, u_out, *to):
    packed, gain = take
    w_send, _, _, w_fold = quarters(packed)
    edges = ghalo.shape[0]
    block = inner.shape[0]
    halo = (mul(ghalo[:, :block], inner[...]) + mul(ghalo[:, block:], outer[...])).astype(BF16)
    a = a_own[...] + mul(halo, w_send[...])
    a_out[...] = a
    q = (a * jax.nn.sigmoid(a)).astype(BF16)
    u = u_own[...] + mul(mul(gown_t[:, edges:], q).astype(BF16), w_fold[...])
    u_out[...] = u
    t, _ = normalize(u * jax.nn.sigmoid(u))
    out = (h[...].astype(F32) + t * gain[...]).astype(BF16)
    h_out[...] = out
    for side, ref in zip((OUTER, INNER), reversed(to)):
        ref[...] = listed(lists[side : side + 1, :1], out, block)


def inner_kernel(lists, h, out):
    out[...] = listed(lists[INNER : INNER + 1, :1], h[...], out.shape[0])


def save_kernel(plane, parity, a, u, h, *refs):
    t_out, r_out, s_out, h_out = refs[-4:]
    rows, edges = h.shape[0], a.shape[0]
    at = slice(parity * rows, (parity + 1) * rows)

    @pl.when(here_is(plane))
    def _():
        s_out[parity * edges : (parity + 1) * edges, :] = slope(a[...]).astype(BF16)
        u_value = u[...]
        t, inverse = normalize(u_value * jax.nn.sigmoid(u_value))
        t_out[at, :] = t.astype(BF16)
        r_out[at, :] = (inverse * slope(u_value)).astype(BF16)
        h_out[at, :] = h[...]


def backward_kernel(sides, finish, parity, kept, take, *refs):
    packed, gain = take
    w_send, _, _, w_fold = quarters(packed)
    lists, upstream, *refs = refs[kept:]
    arrived, refs = refs[: len(sides)], refs[len(sides) :]
    t_in, r_in, s_in, gown, ghalo_t, c_out, du_out, da_out, es_out, *done, to_inner, to_outer = refs
    edges = gown.shape[0] // 2
    rows = upstream.shape[0]
    block = to_inner.shape[0]
    at = slice(parity * rows, (parity + 1) * rows)
    at_edges = slice(parity * edges, (parity + 1) * edges)
    c_out[...] = upstream[...].astype(F32)
    for side, ref in zip(sides, arrived):
        add_listed(lists[side : side + 1, :1], c_out, ref[...].astype(F32), block)
    if finish:
        done[0][...] = c_out[...].astype(BF16)
    g = c_out[...] * gain[...]
    t = t_in[at, :].astype(F32)
    centre = jnp.mean(g, axis=-1, keepdims=True)
    along = jnp.mean(g * t, axis=-1, keepdims=True)
    du = ((g - centre - t * along) * r_in[at, :].astype(F32)).astype(BF16)
    du_out[...] = du
    spread = mul(gown[edges:, :], du).astype(BF16)
    da = (mul_t(spread, w_fold[...]) * s_in[at_edges, :].astype(F32)).astype(BF16)
    da_out[...] = da
    es = mul_t(da, w_send[...]).astype(BF16)
    es_out[...] = es
    halo = mul(ghalo_t[...], es).astype(BF16)
    to_inner[...] = halo[:block]
    to_outer[...] = halo[block:]


def backward_own_kernel(add_inner, last, take, *refs):
    _, w_recv, w_node, _ = quarters(take[0])
    if last:
        _, _, other, *refs = refs
    if add_inner:
        lists, inner, *refs = refs
    refs, out = (refs[:-2], refs[-2:]) if last else (refs[:-1], refs[-1:])
    *_, c, du, da, es, gown_t = refs
    er = mul_t(da[...], w_recv[...]).astype(BF16)
    both = jnp.concatenate([es[...], er], axis=0)
    total = c[...] + mul_t(du[...], w_node[...]) + mul(gown_t[...], both)
    if add_inner:
        block = inner.shape[0]
        at = lists[INNER : INNER + 1, :1]
        value = inner[...].astype(F32)
        total = total + jnp.concatenate(
            [jnp.where(at == number, value, 0.0) for number in range(total.shape[0] // block)], axis=0
        )
    if last:
        order(total.astype(BF16), other[...], *out)
    else:
        out[0][...] = total.astype(out[0].dtype)


def order(even, odd, first, second):
    zero = lax.axis_index("dom") % 2 == 0

    @pl.when(zero)
    def _():
        first[...] = even
        second[...] = odd

    @pl.when(jnp.logical_not(zero))
    def _():
        first[...] = odd
        second[...] = even


def order_kernel(both, first, second):
    rows = first.shape[0]
    order(both[:rows, :], both[rows:, :], first, second)


def add_kernel(lists, value, outer, other, first, second, total):
    @pl.when(here_is(1))
    def _():
        total[...] = value[...].astype(F32)
        add_listed(lists[OUTER : OUTER + 1, :1], total, outer[...].astype(F32), outer.shape[0])
        order(total[...].astype(BF16), other[...], first, second)


def place_kernel(lists, outer, flipped, first, second):
    block = outer.shape[0]
    at = lists[OUTER : OUTER + 1, :1]
    for value, out in ((outer, first), (flipped, second)):
        for number in range(out.shape[0] // block):
            covered = jnp.broadcast_to(at == number, value.shape) & here_is(0, 0)
            out[number * block : (number + 1) * block, :] = jnp.where(covered, value[...].astype(F32), 0.0).astype(BF16)


def sum_kernel(*refs):
    ends, placed, totals = (refs[2 * k : 2 * k + 2] for k in range(3))
    for k in range(2):
        totals[k][...] = (ends[k][...].astype(F32) + placed[k][...].astype(F32)).astype(BF16)


def write_kernel(*refs):
    first_home, second_home, totals = (refs[2 * k : 2 * k + 2] for k in range(3))
    out_home, out_grads, sems = refs[6:]
    core = lax.axis_index("pipe") % 2
    slots = core, 1 - core

    def outputs(source):
        return [pltpu.make_async_copy(source[k], out_home.at[0, slots[k]], sems.at[k]) for k in range(2)]

    copies = [pltpu.make_async_copy(totals[k], out_grads.at[0, slots[k]], sems.at[2 + k]) for k in range(2)]
    for copy in copies:
        copy.start()

    @pl.when(here_is(0))
    def _():
        for copy in outputs(first_home):
            copy.start()

    @pl.when(jnp.logical_not(here_is(0)))
    def _():
        for copy in outputs(second_home):
            copy.start()

    for copy in copies + outputs(first_home):
        copy.wait()


def run(kernel, operands, outs, spaces=(), aliases=None, out_spaces=(), scratch=(), cost=1, vmem=12):
    spaces = tuple(spaces) + (pltpu.VMEM,) * (len(operands) - len(spaces))
    out_spaces = tuple(out_spaces) + (pltpu.VMEM,) * (len(outs) - len(out_spaces))
    return pl.pallas_call(
        kernel,
        out_shape=[jax.ShapeDtypeStruct(s, t) for s, t in outs],
        in_specs=[pl.BlockSpec(memory_space=space) for space in spaces],
        out_specs=[pl.BlockSpec(memory_space=space) for space in out_spaces],
        scratch_shapes=list(scratch),
        input_output_aliases=aliases or {},
        compiler_params=pltpu.CompilerParams(vmem_limit_bytes=vmem * 2**20),
        cost_estimate=pl.CostEstimate(flops=cost, bytes_accessed=1, transcendentals=0),
    )(*operands)


def run_section(body, plane, matrices, operands, outs, elsewhere=None, cost=1):
    elsewhere = elsewhere or {}

    def kernel(*refs):
        take, rest = refs[: len(matrices)], refs[len(matrices) :]

        @pl.when(here_is(plane))
        def _():
            body(take, *rest)

        if elsewhere:

            @pl.when(jnp.logical_not(here_is(plane)))
            def _():
                for source, target in elsewhere.items():
                    rest[target][...] = rest[source][...]

    return run(kernel, tuple(matrices) + tuple(operands), outs, cost=cost)


def shards(
    inputs,
    cotangent,
    w_send,
    w_recv,
    w_message,
    w_node,
    w_aggregate,
    gains,
    edge_send,
    edge_recv,
    edge_count,
    halo_send,
):
    sections = lax.axis_size("pipe")
    pairs_total = lax.axis_size("dom") // 2
    phase = lax.axis_index("pipe")
    y = lax.rem(lax.axis_index("dom"), 2)
    plane_here = phase // 2
    rows, latent = inputs.shape[1:]
    edge_blocks, block = edge_send.shape
    edges = edge_blocks * block

    def send(value, rule):
        table = []
        for z in range(pairs_total):
            for which in range(2):
                for x in range(sections // 2):
                    for c in range(2):
                        if (target := rule(z, which, x, c)) is None:
                            continue
                        tz, ty, tx, tc = target
                        target = (2 * (tz % pairs_total) + ty) * sections + 2 * (tx % (sections // 2)) + tc
                        table.append(((2 * z + which) * sections + 2 * x + c, target))
        return lax.ppermute(value, AXES, table)

    def flip_y(value):
        return send(value, lambda z, y, x, c: (z, 1 - y, x, c))

    def flip_core(value):
        return send(value, lambda z, y, x, c: (z, y, x, 1 - c))

    def go_home(first, second, plane=None):
        return (
            send(first, lambda z, y, x, c: (z, c, x, y) if plane in (None, x) else None),
            send(second, lambda z, y, x, c: (z, c, x, 1 - y) if plane in (None, x) else None),
        )

    def towards(value, side, step):
        if side == INNER:
            return send(value, lambda z, y, x, c: (z, y, x + step, 1 - c))
        return send(value, lambda z, y, x, c: (z + 2 * c - 1, y, x + step, 1 - c))

    wide = (rows, latent)
    edge_wide = (edges, latent)
    narrow = (block, latent)
    unit = 2 * rows * latent * latent
    dma = pltpu.SemaphoreType.DMA

    here, there, boundary, packed = run(
        prepare_kernel,
        (edge_count, jnp.swapaxes(halo_send, 1, 2), inputs, cotangent, edge_send, edge_recv),
        [(wide, BF16), ((rows + 16, latent), BF16), (narrow, BF16), ((16, block), BF16)],
        spaces=(pltpu.HBM,) * 6,
        out_spaces=(pltpu.HBM,) * 3,
        scratch=[
            pltpu.SMEM((edge_blocks,), jnp.int32),
            pltpu.SMEM((1, 1, 2), jnp.int32),
            pltpu.VMEM(wide, BF16),
            pltpu.VMEM((rows + 16, latent), BF16),
            pltpu.VMEM(narrow, BF16),
            pltpu.VMEM((2, 8, block), jnp.int32),
            dma((7,)),
            dma((3,)),
        ],
        vmem=56,
    )
    there = flip_y(there)
    outer = send(boundary, lambda z, y, x, c: (z + 2 * y - 1, c, x, 1 - y))
    gown, gown_t, ghalo, ghalo_t, lists, mate, home_lists = run(
        functools.partial(graph_kernel, edge_blocks),
        (packed, there),
        [
            ((2 * edges, rows), BF16),
            ((rows, 2 * edges), BF16),
            ((edges, 2 * block), BF16),
            ((2 * block, edges), BF16),
            ((2, block), jnp.int32),
            ((1, block), jnp.int32),
            ((2, block), jnp.int32),
        ],
    )
    hidden, inner = run(entry_kernel, (mate, here, there), [(wide, BF16), (narrow, BF16)], cost=LONG)

    [weights] = run(
        weights_kernel,
        (w_send[0], w_recv[0], w_node[0], w_message[0], w_aggregate[0]),
        [((4 * latent, latent), BF16)],
        spaces=(pltpu.HBM,) * 5,
        scratch=[pltpu.VMEM((2, latent, latent), BF16), dma((5,))],
        vmem=56,
    )
    even, odd = run(arrange_kernel, (weights, flip_core(weights), hidden), [((4 * latent, latent), BF16)] * 2)
    gain_even, gain_odd = run(arrange_kernel, (gains, flip_core(gains), hidden), [((1, latent), F32)] * 2)
    matrices = ((even, gain_even), (odd, gain_odd))
    upstream = hidden

    saved = ()
    arrived = ()
    for tick in range(sections):
        plane, parity = tick // 2, tick % 2
        packed, gain = matrices[parity]
        a_own, u_own = run_section(
            forward_own_kernel, plane, (packed,), (hidden, gown) + arrived, [(edge_wide, F32), (wide, F32)], cost=BESIDE
        )
        step = (tick + 1) // 2 - plane if tick < sections - 1 else None
        to_send = [(narrow, BF16)] * {0: 2, 1: 1, None: 0}[step]
        hidden, a, u, *to = run_section(
            forward_kernel,
            plane,
            (packed, gain),
            (lists, hidden, a_own, u_own, inner, outer, ghalo, gown_t),
            [(wide, BF16), (edge_wide, F32), (wide, F32)] + to_send,
        )
        produced = hidden
        if to:
            outer = towards(to[-1], OUTER, step)
        if step == 0:
            inner = towards(to[0], INNER, step)
            arrived = (inner,)
        elif step:
            hidden = send(hidden, lambda z, y, x, c: (z, y, x + 1, c))
            inner = towards(*run(inner_kernel, (lists, hidden), [(narrow, BF16)]), INNER, 0)
            arrived = ()
        saved = run(
            functools.partial(save_kernel, plane, parity),
            (a, u, produced) + tuple(saved),
            [((2 * rows, latent), BF16), ((2 * rows, latent), BF16), ((2 * edges, latent), BF16), ((2 * rows, latent), BF16)],
            aliases={3 + k: k for k in range(4)} if saved else None,
            cost=BESIDE,
        )

    *states, both = saved
    halos = {}
    finished = {}
    for tick in range(sections - 1, -1, -1):
        plane, parity = tick // 2, tick % 2
        packed, gain = matrices[parity]
        step = (tick - 1) // 2 - plane if tick else 0
        finish = bool(halos) and tick % 2 == 0
        outs = [(wide, F32), (wide, BF16), (edge_wide, BF16), (edge_wide, BF16)]
        outs += [(wide, BF16)] if finish else []
        outs += [(narrow, BF16)] * 2
        kept = (to_outer,) if tick == 1 else ()
        c, du, da, es, *done, to_inner, to_outer = run_section(
            functools.partial(backward_kernel, tuple(halos), finish, parity, len(kept)),
            plane,
            (packed, gain),
            kept + (lists, upstream) + tuple(halos.values()) + tuple(states) + (gown, ghalo_t),
            outs,
            elsewhere={0: -1} if tick == 1 else {},
            cost=BESIDE // 2 if tick == sections - 2 else 1,
        )
        if done:
            finished[tick + 1] = done[0]
        inner = towards(to_inner, INNER, 0)
        halos = {OUTER: towards(to_outer, OUTER, step)} if tick else {}
        add_inner = tick == 0 or step != 0
        last = tuple(ends) + (finished[1],) if tick == 0 else ()
        beside = (lists, inner) if add_inner else (inner,)
        upstream, *rest = run_section(
            functools.partial(backward_own_kernel, add_inner, bool(last)),
            plane,
            (packed,),
            last + beside + (tuple(first_home) if step else ()) + (c, du, da, es, gown_t),
            [(wide, BF16)] * 2 if last else [(wide, BF16 if step else F32)],
            elsewhere={0: -2, 1: -1} if last else {},
            cost=BESIDE if tick else 1,
        )
        if not add_inner:
            halos = {INNER: inner, **halos}
        if tick == sections - 1:
            outputs, upstream = lax.optimization_barrier((both, upstream))
            first_home = go_home(*run(order_kernel, (outputs,), [(wide, BF16)] * 2), plane=0)
        if step:
            own = upstream
            upstream = send(upstream, lambda z, y, x, c: (z, y, x + 1, c))
        elif tick == 1:
            outputs, upstream = lax.optimization_barrier((both, upstream))
            second_home = go_home(*run(order_kernel, (outputs,), [(wide, BF16)] * 2), plane=1)
            ends = run(
                add_kernel,
                (lists, own, halos[OUTER], finished[3]),
                [(wide, BF16)] * 2,
                scratch=[pltpu.VMEM(wide, F32)],
            )

    final_outer = send(to_outer, lambda z, y, x, c: (z + 2 * c - 1, 1 - c, x, y))
    ends = go_home(upstream, *rest)
    placed = run(
        place_kernel, (home_lists, final_outer, flip_core(final_outer)), [(wide, BF16)] * 2
    )
    totals = run(sum_kernel, tuple(ends) + tuple(placed), [(wide, BF16)] * 2, cost=LONG)
    return tuple(
        run(
            write_kernel,
            tuple(first_home) + tuple(second_home) + tuple(totals),
            [((1, 2) + wide, BF16)] * 2,
            out_spaces=(pltpu.HBM,) * 2,
            scratch=[dma((4,))],
        )
    )


def solution(mesh):
    in_specs = (
        P(None, "dom", None),
        P(None, "dom", None),
        P("pipe", None, None),
        P("pipe", None, None),
        P("pipe", None, None),
        P("pipe", None, None),
        P("pipe", None, None),
        P("pipe", None),
        P("dom", None),
        P("dom", None),
        P("dom"),
        P("dom", None, None),
    )
    out_specs = (P("pipe", None, "dom", None), P("pipe", None, "dom", None))
    return jax.shard_map(shards, mesh=mesh, in_specs=in_specs, out_specs=out_specs, check_vma=False)
```

```python
import functools

import jax
import jax.numpy as jnp
from jax import lax
from jax.experimental import pallas as pl
from jax.experimental.pallas import tpu as pltpu
from jax.sharding import PartitionSpec as P

EPSILON = 1e-05
F32 = jnp.float32
BF16 = jnp.bfloat16
AXES = ("dom", "pipe")
INNER, OUTER = 0, 1
BESIDE = 4 * 10**9
LONG = 2 * 10**10


def mul(a, b):
    return jnp.dot(a, b, preferred_element_type=F32)


def mul_t(a, b):
    return lax.dot_general(a, b, (((1,), (1,)), ((), ())), preferred_element_type=F32)


def slope(v):
    s = jax.nn.sigmoid(v)
    return s * (1.0 + v * (1.0 - s))


def normalize(z):
    centred = z - jnp.mean(z, axis=-1, keepdims=True)
    inverse = lax.rsqrt(jnp.mean(centred * centred, axis=-1, keepdims=True) + EPSILON)
    return centred * inverse, inverse


def quarters(packed):
    depth = packed.shape[0] // 4
    return [packed.at[pl.ds(number * depth, depth), :] for number in range(4)]


def here_is(plane=None, parity=None):
    pipe = lax.axis_index("pipe")
    wanted = jnp.bool_(True)
    if plane is not None:
        wanted = pipe // 2 == plane
    if parity is not None:
        wanted = wanted & (pipe % 2 == parity)
    return wanted


def is_local():
    return lax.axis_index("pipe") % 2 == lax.axis_index("dom") % 2


def listed(at, value, block):
    picked = value[:block]
    for number in range(1, value.shape[0] // block):
        picked = jnp.where(at == number, value[number * block : (number + 1) * block], picked)
    return picked


def add_listed(at, target, value, block):
    for number in range(target.shape[0] // block):
        rows = slice(number * block, (number + 1) * block)
        target[rows, :] = target[rows, :] + jnp.where(at == number, value, 0.0)


def encode(values):
    high = lax.shift_right_logical(values, 4)
    low = values - high * 16
    return jnp.concatenate([high.astype(F32), low.astype(F32)], axis=0).astype(BF16)


def decode(tile):
    half = tile.shape[0] // 2
    tile = tile.astype(F32)
    return (tile[:half] * 16.0 + tile[half:]).astype(jnp.int32)


def prepare_kernel(
    count_in,
    halo_in,
    inputs,
    cotangent,
    send_in,
    recv_in,
    here,
    there,
    boundary,
    packed,
    count,
    halo,
    here_rows,
    there_rows,
    boundary_rows,
    edges,
    sems,
    out_sems,
):
    micro = lax.axis_index("dom") % 2
    block = boundary.shape[0]
    edge_blocks = send_in.shape[0]
    rows = here.shape[0]
    lists = [
        pltpu.make_async_copy(halo_in, halo, sems.at[0]),
        pltpu.make_async_copy(count_in, count, sems.at[1]),
    ]
    ids = [
        pltpu.make_async_copy(ref, edges.at[k, pl.ds(0, edge_blocks), :], sems.at[2 + k])
        for k, ref in enumerate((send_in, recv_in))
    ]
    def fetch(source):
        return [
            pltpu.make_async_copy(source.at[1 - micro], there_rows.at[pl.ds(0, rows), :], sems.at[4]),
            pltpu.make_async_copy(source.at[micro], here_rows, sems.at[5]),
        ]

    blocks = pltpu.make_async_copy(inputs.at[lax.axis_index("pipe") % 2], boundary_rows, sems.at[6])

    for copy in lists + ids:
        copy.start()

    @pl.when(here_is(0))
    def _():
        for copy in fetch(inputs):
            copy.start()

    @pl.when(jnp.logical_not(here_is(0)))
    def _():
        for copy in fetch(cotangent):
            copy.start()

    blocks.start()
    for copy in lists:
        copy.wait()
    number = jnp.where(micro == 1, halo[0, 0, 0], halo[0, 0, 1])
    for copy in ids:
        copy.wait()
    lane = lax.broadcasted_iota(jnp.int32, (1, block), 1)
    tail = jnp.where(lane == 0, halo[0, 0, 0], jnp.where(lane == 1, halo[0, 0, 1], 0))
    for place in range(edge_blocks):
        tail = jnp.where(lane == 2 + place, count[place], tail)
    spare = jnp.zeros((7 - 2 * edge_blocks, block), jnp.int32)
    tile = encode(jnp.concatenate([edges[0, :edge_blocks, :], edges[1, :edge_blocks, :], tail, spare], axis=0))
    packed[...] = tile
    there_rows[rows:, :] = jnp.zeros((there_rows.shape[0] - rows, there_rows.shape[1]), BF16)
    there_rows[rows:, :block] = tile
    fetched = fetch(inputs)
    leaving = [
        pltpu.make_async_copy(there_rows, there, out_sems.at[0]),
        pltpu.make_async_copy(here_rows, here, out_sems.at[1]),
        pltpu.make_async_copy(
            boundary_rows.at[pl.ds(pl.multiple_of(number * block, block), block), :], boundary, out_sems.at[2]
        ),
    ]
    fetched[0].wait()
    leaving[0].start()
    fetched[1].wait()
    leaving[1].start()
    blocks.wait()
    leaving[2].start()
    for copy in leaving:
        copy.wait()


def weights_kernel(w_send, w_recv, w_node, w_message, w_aggregate, out, factors, sems):
    depth = w_send.shape[0]
    copies = [pltpu.make_async_copy(ref, factors.at[k], sems.at[k]) for k, ref in enumerate((w_message, w_aggregate))]
    copies += [
        pltpu.make_async_copy(ref, out.at[pl.ds(k * depth, depth), :], sems.at[2 + k])
        for k, ref in enumerate((w_send, w_recv, w_node))
    ]
    for copy in copies:
        copy.start()
    for copy in copies[:2]:
        copy.wait()
    out[3 * depth :, :] = mul(factors[0], factors[1]).astype(BF16)
    for copy in copies[2:]:
        copy.wait()


def place_mine_kernel(mine, even, odd):
    @pl.when(here_is(parity=0))
    def _():
        even[...] = mine[...]

    @pl.when(here_is(parity=1))
    def _():
        odd[...] = mine[...]


def place_swapped_kernel(swapped, _, even_in, odd_in, even, odd):
    del even_in, odd_in

    @pl.when(here_is(parity=0))
    def _():
        odd[...] = swapped[...]

    @pl.when(here_is(parity=1))
    def _():
        even[...] = swapped[...]


def graph_kernel(edge_blocks, packed, there, gown, gown_t, ghalo, ghalo_t, lists, mate, home_lists):
    block = packed.shape[1]
    rows = gown_t.shape[0]
    edges = edge_blocks * block
    local = is_local()
    first_core = lax.axis_index("pipe") % 2 == 0
    last = 2 * edge_blocks
    tiles = decode(packed[...]), decode(there[rows:, :block])
    mine = jnp.where(local, *tiles)
    tails = [tile[last : last + 1] for tile in (mine, jnp.where(local, tiles[1], tiles[0]), tiles[0])]
    lane = lax.broadcasted_iota(jnp.int32, (1, block), 1)
    row = lax.broadcasted_iota(jnp.int32, (rows, block), 0)
    halo_row = lax.broadcasted_iota(jnp.int32, (2 * block, block), 0)
    for number in range(edge_blocks):
        live = lane < tails[0][:, 2 + number : 3 + number]
        sender = jnp.where(live, mine[number : number + 1], -1)
        receiver = jnp.where(live, mine[edge_blocks + number : edge_blocks + number + 1], -1)
        outside = sender - rows
        turned = jnp.where(outside < block, outside + block, outside - block)
        outside = jnp.where(outside >= 0, jnp.where(first_core, turned, outside), -1)
        here = slice(number * block, (number + 1) * block)
        received = slice(edges + number * block, edges + (number + 1) * block)
        for index, at, table, table_t in (
            (sender, here, gown, gown_t),
            (receiver, received, gown, gown_t),
            (outside, here, ghalo, ghalo_t),
        ):
            hot = (index == (halo_row if table is ghalo else row)).astype(F32)
            table_t[:, at] = hot.astype(BF16)
            table[at, :] = hot.T.astype(BF16)

    def whole(tail, place):
        return jnp.broadcast_to(tail[:1, place : place + 1], (1, block))

    to_next, to_prev = whole(tails[0], 0), whole(tails[0], 1)
    lists[0:1, :] = jnp.where(first_core, to_next, to_prev)
    lists[1:2, :] = jnp.where(first_core, to_prev, to_next)
    mate[...] = jnp.where(first_core, whole(tails[1], 1), whole(tails[1], 0))
    to_next, to_prev = whole(tails[2], 0), whole(tails[2], 1)
    home_first = lax.axis_index("dom") % 2 == 0
    home_lists[0:1, :] = jnp.where(home_first, to_next, to_prev)
    home_lists[1:2, :] = jnp.where(home_first, to_prev, to_next)


def entry_kernel(mate, here, there, _, hidden, inner):
    block = inner.shape[0]

    @pl.when(is_local())
    def _():
        hidden[...] = here[...]
        inner[...] = listed(mate[:, :1], there[: hidden.shape[0], :], block)

    @pl.when(jnp.logical_not(is_local()))
    def _():
        hidden[...] = there[: hidden.shape[0], :]
        inner[...] = listed(mate[:, :1], here[...], block)


def forward_own_kernel(take, h, gown, *refs):
    w_send, w_recv, w_node, _ = quarters(take[0])
    a_out, u_out = refs[-2:]
    edges = gown.shape[0] // 2
    own = mul(gown[...], h[...]).astype(BF16)
    a_out[...] = mul(own[:edges], w_send[...]) + mul(own[edges:], w_recv[...])
    u_out[...] = mul(h[...], w_node[...])


def forward_kernel(parity, take, lists, h, a_own, u_own, inner, outer, ghalo, gown_t, h_out, a_out, u_out, *to):
    packed, *gains = take
    w_send, _, _, w_fold = quarters(packed)
    gain = jnp.where(here_is(parity=parity), gains[0][...], gains[1][...])
    edges = ghalo.shape[0]
    block = inner.shape[0]
    halo = (mul(ghalo[:, :block], inner[...]) + mul(ghalo[:, block:], outer[...])).astype(BF16)
    a = a_own[...] + mul(halo, w_send[...])
    a_out[...] = a
    q = (a * jax.nn.sigmoid(a)).astype(BF16)
    u = u_own[...] + mul(mul(gown_t[:, edges:], q).astype(BF16), w_fold[...])
    u_out[...] = u
    t, _ = normalize(u * jax.nn.sigmoid(u))
    out = (h[...].astype(F32) + t * gain).astype(BF16)
    h_out[...] = out
    for side, ref in zip((OUTER, INNER), reversed(to)):
        ref[...] = listed(lists[side : side + 1, :1], out, block)


def inner_kernel(lists, h, out):
    out[...] = listed(lists[INNER : INNER + 1, :1], h[...], out.shape[0])


def save_kernel(plane, parity, a, u, h, *refs):
    t_out, r_out, s_out, h_out = refs[-4:]
    rows, edges = h.shape[0], a.shape[0]
    at = slice(parity * rows, (parity + 1) * rows)

    @pl.when(here_is(plane))
    def _():
        s_out[parity * edges : (parity + 1) * edges, :] = slope(a[...]).astype(BF16)
        u_value = u[...]
        t, inverse = normalize(u_value * jax.nn.sigmoid(u_value))
        t_out[at, :] = t.astype(BF16)
        r_out[at, :] = (inverse * slope(u_value)).astype(BF16)
        h_out[at, :] = h[...]


def backward_kernel(sides, finish, parity, kept, take, *refs):
    packed, *gains = take
    w_send, _, _, w_fold = quarters(packed)
    gain = jnp.where(here_is(parity=parity), gains[0][...], gains[1][...])
    lists, upstream, *refs = refs[kept:]
    arrived, refs = refs[: len(sides)], refs[len(sides) :]
    t_in, r_in, s_in, gown, ghalo_t, c_out, du_out, da_out, es_out, *done, to_inner, to_outer = refs
    edges = gown.shape[0] // 2
    rows = upstream.shape[0]
    block = to_inner.shape[0]
    at = slice(parity * rows, (parity + 1) * rows)
    at_edges = slice(parity * edges, (parity + 1) * edges)
    c_out[...] = upstream[...].astype(F32)
    for side, ref in zip(sides, arrived):
        if ref.shape == c_out.shape:
            c_out[...] = c_out[...] + ref[...]
        else:
            add_listed(lists[side : side + 1, :1], c_out, ref[...].astype(F32), block)
    if finish:
        done[0][...] = c_out[...].astype(BF16)
    g = c_out[...] * gain
    t = t_in[at, :].astype(F32)
    centre = jnp.mean(g, axis=-1, keepdims=True)
    along = jnp.mean(g * t, axis=-1, keepdims=True)
    du = ((g - centre - t * along) * r_in[at, :].astype(F32)).astype(BF16)
    du_out[...] = du
    spread = mul(gown[edges:, :], du).astype(BF16)
    da = (mul_t(spread, w_fold[...]) * s_in[at_edges, :].astype(F32)).astype(BF16)
    da_out[...] = da
    es = mul_t(da, w_send[...]).astype(BF16)
    es_out[...] = es
    halo = mul(ghalo_t[...], es).astype(BF16)
    to_inner[...] = halo[:block]
    to_outer[...] = halo[block:]


def backward_own_kernel(add_inner, last, take, *refs):
    _, w_recv, w_node, _ = quarters(take[0])
    if last:
        _, _, other, *refs = refs
    if add_inner:
        lists, inner, *refs = refs
    refs, out = (refs[:-2], refs[-2:]) if last else (refs[:-1], refs[-1:])
    *_, c, du, da, es, gown_t = refs
    er = mul_t(da[...], w_recv[...]).astype(BF16)
    both = jnp.concatenate([es[...], er], axis=0)
    total = c[...] + mul_t(du[...], w_node[...]) + mul(gown_t[...], both)
    if add_inner:
        block = inner.shape[0]
        at = lists[INNER : INNER + 1, :1]
        value = inner[...].astype(F32)
        total = total + jnp.concatenate(
            [jnp.where(at == number, value, 0.0) for number in range(total.shape[0] // block)], axis=0
        )
    if last:
        order(total.astype(BF16), other[...], *out)
    else:
        out[0][...] = total.astype(out[0].dtype)


def order(even, odd, first, second):
    zero = lax.axis_index("dom") % 2 == 0

    @pl.when(zero)
    def _():
        first[...] = even
        second[...] = odd

    @pl.when(jnp.logical_not(zero))
    def _():
        first[...] = odd
        second[...] = even


def order_kernel(both, first, second):
    rows = first.shape[0]
    order(both[:rows, :], both[rows:, :], first, second)


def add_kernel(lists, value, outer, other, first, second, total):
    @pl.when(here_is(1))
    def _():
        total[...] = value[...].astype(F32)
        add_listed(lists[OUTER : OUTER + 1, :1], total, outer[...].astype(F32), outer.shape[0])
        order(total[...].astype(BF16), other[...], first, second)


def spread_kernel(lists, outer, out):
    block = outer.shape[0]
    at = lists[OUTER : OUTER + 1, :1]
    value = outer[...].astype(F32)
    for number in range(out.shape[0] // block):
        out[number * block : (number + 1) * block, :] = jnp.where(at == number, value, 0.0)


def place_kernel(lists, outer, flipped, first, second):
    block = outer.shape[0]
    at = lists[OUTER : OUTER + 1, :1]
    for value, out in ((outer, first), (flipped, second)):
        for number in range(out.shape[0] // block):
            covered = jnp.broadcast_to(at == number, value.shape) & here_is(0, 0)
            out[number * block : (number + 1) * block, :] = jnp.where(covered, value[...].astype(F32), 0.0).astype(BF16)


def sum_kernel(*refs):
    ends, placed, totals = (refs[2 * k : 2 * k + 2] for k in range(3))
    for k in range(2):
        totals[k][...] = (ends[k][...].astype(F32) + placed[k][...].astype(F32)).astype(BF16)


def write_kernel(*refs):
    first_home, second_home, totals = (refs[2 * k : 2 * k + 2] for k in range(3))
    out_home, out_grads, sems = refs[6:]
    core = lax.axis_index("pipe") % 2
    slots = core, 1 - core

    def outputs(source):
        return [pltpu.make_async_copy(source[k], out_home.at[0, slots[k]], sems.at[k]) for k in range(2)]

    copies = [pltpu.make_async_copy(totals[k], out_grads.at[0, slots[k]], sems.at[2 + k]) for k in range(2)]
    for copy in copies:
        copy.start()

    @pl.when(here_is(0))
    def _():
        for copy in outputs(first_home):
            copy.start()

    @pl.when(jnp.logical_not(here_is(0)))
    def _():
        for copy in outputs(second_home):
            copy.start()

    for copy in copies + outputs(first_home):
        copy.wait()


def run(kernel, operands, outs, spaces=(), aliases=None, out_spaces=(), scratch=(), cost=1, vmem=12):
    spaces = tuple(spaces) + (pltpu.VMEM,) * (len(operands) - len(spaces))
    out_spaces = tuple(out_spaces) + (pltpu.VMEM,) * (len(outs) - len(out_spaces))
    return pl.pallas_call(
        kernel,
        out_shape=[jax.ShapeDtypeStruct(s, t) for s, t in outs],
        in_specs=[pl.BlockSpec(memory_space=space) for space in spaces],
        out_specs=[pl.BlockSpec(memory_space=space) for space in out_spaces],
        scratch_shapes=list(scratch),
        input_output_aliases=aliases or {},
        compiler_params=pltpu.CompilerParams(vmem_limit_bytes=vmem * 2**20),
        cost_estimate=pl.CostEstimate(flops=cost, bytes_accessed=1, transcendentals=0),
    )(*operands)


def run_section(body, plane, matrices, operands, outs, elsewhere=None, cost=1):
    elsewhere = elsewhere or {}

    def kernel(*refs):
        take, rest = refs[: len(matrices)], refs[len(matrices) :]

        @pl.when(here_is(plane))
        def _():
            body(take, *rest)

        if elsewhere:

            @pl.when(jnp.logical_not(here_is(plane)))
            def _():
                for source, target in elsewhere.items():
                    rest[target][...] = rest[source][...]

    return run(kernel, tuple(matrices) + tuple(operands), outs, cost=cost)


def shards(
    inputs,
    cotangent,
    w_send,
    w_recv,
    w_message,
    w_node,
    w_aggregate,
    gains,
    edge_send,
    edge_recv,
    edge_count,
    halo_send,
):
    sections = lax.axis_size("pipe")
    pairs_total = lax.axis_size("dom") // 2
    phase = lax.axis_index("pipe")
    y = lax.rem(lax.axis_index("dom"), 2)
    plane_here = phase // 2
    rows, latent = inputs.shape[1:]
    edge_blocks, block = edge_send.shape
    edges = edge_blocks * block

    def send(value, rule):
        table = []
        for z in range(pairs_total):
            for which in range(2):
                for x in range(sections // 2):
                    for c in range(2):
                        if (target := rule(z, which, x, c)) is None:
                            continue
                        tz, ty, tx, tc = target
                        target = (2 * (tz % pairs_total) + ty) * sections + 2 * (tx % (sections // 2)) + tc
                        table.append(((2 * z + which) * sections + 2 * x + c, target))
        return lax.ppermute(value, AXES, table)

    def flip_y(value):
        return send(value, lambda z, y, x, c: (z, 1 - y, x, c))

    def flip_core(value):
        return send(value, lambda z, y, x, c: (z, y, x, 1 - c))

    def go_home(first, second, plane=None):
        return (
            send(first, lambda z, y, x, c: (z, c, x, y) if plane in (None, x) else None),
            send(second, lambda z, y, x, c: (z, c, x, 1 - y) if plane in (None, x) else None),
        )

    def towards(value, side, step):
        if side == INNER:
            return send(value, lambda z, y, x, c: (z, y, x, 1 - c))
        return send(value, lambda z, y, x, c: (z + 2 * c - 1, y, x + step, 1 - c) if crosses(x, step) else None)

    def crosses(x, step):
        return step == 0 or 0 <= x + step < sections // 2

    def across(value, step):
        return send(value, lambda z, y, x, c: (z, y, x + step, c) if crosses(x, step) else None)

    wide = (rows, latent)
    edge_wide = (edges, latent)
    narrow = (block, latent)
    unit = 2 * rows * latent * latent
    dma = pltpu.SemaphoreType.DMA

    here, there, boundary, packed = run(
        prepare_kernel,
        (edge_count, jnp.swapaxes(halo_send, 1, 2), inputs, cotangent, edge_send, edge_recv),
        [(wide, BF16), ((rows + 16, latent), BF16), (narrow, BF16), ((16, block), BF16)],
        spaces=(pltpu.HBM,) * 6,
        out_spaces=(pltpu.HBM,) * 3,
        scratch=[
            pltpu.SMEM((edge_blocks,), jnp.int32),
            pltpu.SMEM((1, 1, 2), jnp.int32),
            pltpu.VMEM(wide, BF16),
            pltpu.VMEM((rows + 16, latent), BF16),
            pltpu.VMEM(wide, BF16),
            pltpu.VMEM((2, 8, block), jnp.int32),
            dma((7,)),
            dma((3,)),
        ],
        vmem=56,
    )
    there = flip_y(there)
    outer = send(boundary, lambda z, y, x, c: (z + 2 * y - 1, c, x, 1 - y))
    gown, gown_t, ghalo, ghalo_t, lists, mate, home_lists = run(
        functools.partial(graph_kernel, edge_blocks),
        (packed, there),
        [
            ((2 * edges, rows), BF16),
            ((rows, 2 * edges), BF16),
            ((edges, 2 * block), BF16),
            ((2 * block, edges), BF16),
            ((2, block), jnp.int32),
            ((1, block), jnp.int32),
            ((2, block), jnp.int32),
        ],
    )
    hidden, inner = run(entry_kernel, (mate, here, there, outer), [(wide, BF16), (narrow, BF16)], cost=LONG)

    [weights] = run(
        weights_kernel,
        (w_send[0], w_recv[0], w_node[0], w_message[0], w_aggregate[0]),
        [((4 * latent, latent), BF16)],
        spaces=(pltpu.HBM,) * 5,
        scratch=[pltpu.VMEM((2, latent, latent), BF16), dma((5,))],
        vmem=56,
    )
    pair = run(place_mine_kernel, (weights,), [((4 * latent, latent), BF16)] * 2)
    matrices = run(
        place_swapped_kernel, (flip_core(weights), hidden, *pair), [((4 * latent, latent), BF16)] * 2, aliases={2: 0, 3: 1}
    )
    both_gains = (gains, flip_core(gains))
    upstream = hidden

    saved = ()
    arrived = ()
    for tick in range(sections):
        plane, parity = tick // 2, tick % 2
        packed = matrices[parity]
        a_own, u_own = run_section(
            forward_own_kernel, plane, (packed,), (hidden, gown) + arrived, [(edge_wide, F32), (wide, F32)], cost=BESIDE
        )
        if tick == sections - 1:
            outputs, a_own = lax.optimization_barrier((saved[3], a_own))
            first_home = go_home(*run(order_kernel, (outputs,), [(wide, BF16)] * 2), plane=0)
        step = (tick + 1) // 2 - plane if tick < sections - 1 else None
        to_send = [(narrow, BF16)] * {0: 2, 1: 1, None: 0}[step]
        hidden, a, u, *to = run_section(
            functools.partial(forward_kernel, parity),
            plane,
            (packed, *both_gains),
            (lists, hidden, a_own, u_own, inner, outer, ghalo, gown_t),
            [(wide, BF16), (edge_wide, F32), (wide, F32)] + to_send,
            cost=1 if to_send else BESIDE // 2,
        )
        produced = hidden
        if to:
            outer = towards(to[-1], OUTER, step)
        if step == 0:
            inner = towards(to[0], INNER, step)
            arrived = (inner,)
        elif step:
            hidden = across(hidden, step)
            inner = towards(*run(inner_kernel, (lists, hidden), [(narrow, BF16)]), INNER, 0)
            arrived = ()
        saved = run(
            functools.partial(save_kernel, plane, parity),
            (a, u, produced) + tuple(saved),
            [((2 * rows, latent), BF16), ((2 * rows, latent), BF16), ((2 * edges, latent), BF16), ((2 * rows, latent), BF16)],
            aliases={3 + k: k for k in range(4)} if saved else None,
            cost=BESIDE,
        )

    *states, both = saved
    halos = {}
    finished = {}
    for tick in range(sections - 1, -1, -1):
        plane, parity = tick // 2, tick % 2
        packed = matrices[parity]
        step = (tick - 1) // 2 - plane if tick else 0
        finish = bool(halos) and tick % 2 == 0
        outs = [(wide, F32), (wide, BF16), (edge_wide, BF16), (edge_wide, BF16)]
        outs += [(wide, BF16)] if finish else []
        outs += [(narrow, BF16)] * 2
        kept = (to_outer,) if tick == 1 else ()
        c, du, da, es, *done, to_inner, to_outer = run_section(
            functools.partial(backward_kernel, tuple(halos), finish, parity, len(kept)),
            plane,
            (packed, *both_gains),
            kept + (lists, upstream) + tuple(halos.values()) + tuple(states) + (gown, ghalo_t),
            outs,
            elsewhere={0: -1} if tick == 1 else {},
        )
        if done:
            finished[tick + 1] = done[0]
        inner = towards(to_inner, INNER, 0)
        halos = {OUTER: towards(to_outer, OUTER, step)} if tick else {}
        add_inner = tick == 0 or step != 0
        last = tuple(ends) + (finished[1],) if tick == 0 else ()
        beside = (lists, inner) if add_inner else (inner,)
        upstream, *rest = run_section(
            functools.partial(backward_own_kernel, add_inner, bool(last)),
            plane,
            (packed,),
            last + beside + (tuple(first_home) if tick == sections - 1 else ()) + (c, du, da, es, gown_t),
            [(wide, BF16)] * 2 if last else [(wide, BF16 if step else F32)],
            elsewhere={0: -2, 1: -1} if last else {},
            cost=BESIDE if tick else 1,
        )
        if not add_inner:
            halos = {INNER: inner, **halos}
        if step:
            own = upstream
            upstream = across(upstream, step)
            halos = {OUTER: run(spread_kernel, (lists, halos[OUTER]), [(wide, F32)], cost=LONG)[0]}
        elif tick == 1:
            outputs, upstream = lax.optimization_barrier((both, upstream))
            second_home = go_home(*run(order_kernel, (outputs,), [(wide, BF16)] * 2), plane=1)
            ends = run(
                add_kernel,
                (lists, own, halos[OUTER], finished[3]),
                [(wide, BF16)] * 2,
                scratch=[pltpu.VMEM(wide, F32)],
            )

    final_outer = send(to_outer, lambda z, y, x, c: (z + 2 * c - 1, 1 - c, x, y))
    ends = go_home(upstream, *rest)
    placed = run(
        place_kernel, (home_lists, final_outer, flip_core(final_outer)), [(wide, BF16)] * 2
    )
    totals = run(sum_kernel, tuple(ends) + tuple(placed), [(wide, BF16)] * 2, cost=LONG)
    return tuple(
        run(
            write_kernel,
            tuple(first_home) + tuple(second_home) + tuple(totals),
            [((1, 2) + wide, BF16)] * 2,
            out_spaces=(pltpu.HBM,) * 2,
            scratch=[dma((4,))],
        )
    )


def solution(mesh):
    in_specs = (
        P(None, "dom", None),
        P(None, "dom", None),
        P("pipe", None, None),
        P("pipe", None, None),
        P("pipe", None, None),
        P("pipe", None, None),
        P("pipe", None, None),
        P("pipe", None),
        P("dom", None),
        P("dom", None),
        P("dom"),
        P("dom", None, None),
    )
    out_specs = (P("pipe", None, "dom", None), P("pipe", None, "dom", None))
    return jax.shard_map(shards, mesh=mesh, in_specs=in_specs, out_specs=out_specs, check_vma=False)
```

```python
import functools

import jax
import jax.numpy as jnp
from jax import lax
from jax.experimental import pallas as pl
from jax.experimental.pallas import tpu as pltpu
from jax.sharding import PartitionSpec as P

EPSILON = 1e-05
F32 = jnp.float32
BF16 = jnp.bfloat16
AXES = ("dom", "pipe")
INNER, OUTER = 0, 1
BESIDE = 4 * 10**9
LONG = 2 * 10**10


def mul(a, b):
    return jnp.dot(a, b, preferred_element_type=F32)


def mul_t(a, b):
    return lax.dot_general(a, b, (((1,), (1,)), ((), ())), preferred_element_type=F32)


def slope(v):
    s = jax.nn.sigmoid(v)
    return s * (1.0 + v * (1.0 - s))


def normalize(z):
    centred = z - jnp.mean(z, axis=-1, keepdims=True)
    inverse = lax.rsqrt(jnp.mean(centred * centred, axis=-1, keepdims=True) + EPSILON)
    return centred * inverse, inverse


def quarters(packed):
    depth = packed.shape[0] // 4
    return [packed.at[pl.ds(number * depth, depth), :] for number in range(4)]


def here_is(plane=None, parity=None):
    pipe = lax.axis_index("pipe")
    wanted = jnp.bool_(True)
    if plane is not None:
        wanted = pipe // 2 == plane
    if parity is not None:
        wanted = wanted & (pipe % 2 == parity)
    return wanted


def is_local():
    return lax.axis_index("pipe") % 2 == lax.axis_index("dom") % 2


def listed(at, value, block):
    picked = value[:block]
    for number in range(1, value.shape[0] // block):
        picked = jnp.where(at == number, value[number * block : (number + 1) * block], picked)
    return picked


def add_listed(at, target, value, block):
    for number in range(target.shape[0] // block):
        rows = slice(number * block, (number + 1) * block)
        target[rows, :] = target[rows, :] + jnp.where(at == number, value, 0.0)


def encode(values):
    high = lax.shift_right_logical(values, 4)
    low = values - high * 16
    return jnp.concatenate([high.astype(F32), low.astype(F32)], axis=0).astype(BF16)


def decode(tile):
    half = tile.shape[0] // 2
    tile = tile.astype(F32)
    return (tile[:half] * 16.0 + tile[half:]).astype(jnp.int32)


def prepare_kernel(
    count_in,
    halo_in,
    inputs,
    cotangent,
    send_in,
    recv_in,
    here,
    there,
    boundary,
    packed,
    count,
    halo,
    blocks,
    edges,
    sems,
):
    micro = lax.axis_index("dom") % 2
    block = boundary.shape[0]
    edge_blocks = send_in.shape[0]
    rows = here.shape[0]
    lists = [
        pltpu.make_async_copy(halo_in, halo, sems.at[0]),
        pltpu.make_async_copy(count_in, count, sems.at[1]),
    ]
    ids = [
        pltpu.make_async_copy(ref, edges.at[k, pl.ds(0, edge_blocks), :], sems.at[2 + k])
        for k, ref in enumerate((send_in, recv_in))
    ]
    def fetch(source):
        return [
            pltpu.make_async_copy(source.at[1 - micro], there.at[pl.ds(0, rows), :], sems.at[4]),
            pltpu.make_async_copy(source.at[micro], here, sems.at[5]),
        ]

    whole = pltpu.make_async_copy(inputs.at[lax.axis_index("pipe") % 2], blocks, sems.at[6])

    for copy in lists + ids:
        copy.start()

    @pl.when(here_is(0))
    def _():
        for copy in fetch(inputs):
            copy.start()

    @pl.when(jnp.logical_not(here_is(0)))
    def _():
        for copy in fetch(cotangent):
            copy.start()

    whole.start()
    for copy in lists:
        copy.wait()
    number = jnp.where(micro == 1, halo[0, 0, 0], halo[0, 0, 1])
    for copy in ids:
        copy.wait()
    lane = lax.broadcasted_iota(jnp.int32, (1, block), 1)
    tail = jnp.where(lane == 0, halo[0, 0, 0], jnp.where(lane == 1, halo[0, 0, 1], 0))
    for place in range(edge_blocks):
        tail = jnp.where(lane == 2 + place, count[place], tail)
    spare = jnp.zeros((7 - 2 * edge_blocks, block), jnp.int32)
    tile = encode(jnp.concatenate([edges[0, :edge_blocks, :], edges[1, :edge_blocks, :], tail, spare], axis=0))
    packed[...] = tile
    there[rows:, :] = jnp.zeros((there.shape[0] - rows, there.shape[1]), BF16)
    there[rows:, :block] = tile
    for copy in fetch(inputs):
        copy.wait()
    whole.wait()
    boundary[...] = blocks[pl.ds(pl.multiple_of(number * block, block), block), :]


def weights_kernel(w_send, w_recv, w_node, w_message, w_aggregate, out, factors, sems):
    depth = w_send.shape[0]
    copies = [pltpu.make_async_copy(ref, factors.at[k], sems.at[k]) for k, ref in enumerate((w_message, w_aggregate))]
    copies += [
        pltpu.make_async_copy(ref, out.at[pl.ds(k * depth, depth), :], sems.at[2 + k])
        for k, ref in enumerate((w_send, w_recv, w_node))
    ]
    for copy in copies:
        copy.start()
    for copy in copies[:2]:
        copy.wait()
    out[3 * depth :, :] = mul(factors[0], factors[1]).astype(BF16)
    for copy in copies[2:]:
        copy.wait()


def place_mine_kernel(mine, even, odd):
    @pl.when(here_is(parity=0))
    def _():
        even[...] = mine[...]

    @pl.when(here_is(parity=1))
    def _():
        odd[...] = mine[...]


def place_swapped_kernel(swapped, _, even_in, odd_in, even, odd):
    del even_in, odd_in

    @pl.when(here_is(parity=0))
    def _():
        odd[...] = swapped[...]

    @pl.when(here_is(parity=1))
    def _():
        even[...] = swapped[...]


def graph_kernel(edge_blocks, packed, there, gown, gown_t, ghalo, ghalo_t, lists, mate, home_lists):
    block = packed.shape[1]
    rows = gown_t.shape[0]
    edges = edge_blocks * block
    local = is_local()
    first_core = lax.axis_index("pipe") % 2 == 0
    last = 2 * edge_blocks
    tiles = decode(packed[...]), decode(there[rows:, :block])
    mine = jnp.where(local, *tiles)
    tails = [tile[last : last + 1] for tile in (mine, jnp.where(local, tiles[1], tiles[0]), tiles[0])]
    lane = lax.broadcasted_iota(jnp.int32, (1, block), 1)
    row = lax.broadcasted_iota(jnp.int32, (rows, block), 0)
    halo_row = lax.broadcasted_iota(jnp.int32, (2 * block, block), 0)
    for number in range(edge_blocks):
        live = lane < tails[0][:, 2 + number : 3 + number]
        sender = jnp.where(live, mine[number : number + 1], -1)
        receiver = jnp.where(live, mine[edge_blocks + number : edge_blocks + number + 1], -1)
        outside = sender - rows
        turned = jnp.where(outside < block, outside + block, outside - block)
        outside = jnp.where(outside >= 0, jnp.where(first_core, turned, outside), -1)
        here = slice(number * block, (number + 1) * block)
        received = slice(edges + number * block, edges + (number + 1) * block)
        for index, at, table, table_t in (
            (sender, here, gown, gown_t),
            (receiver, received, gown, gown_t),
            (outside, here, ghalo, ghalo_t),
        ):
            hot = (index == (halo_row if table is ghalo else row)).astype(F32)
            table_t[:, at] = hot.astype(BF16)
            table[at, :] = hot.T.astype(BF16)

    def whole(tail, place):
        return jnp.broadcast_to(tail[:1, place : place + 1], (1, block))

    to_next, to_prev = whole(tails[0], 0), whole(tails[0], 1)
    lists[0:1, :] = jnp.where(first_core, to_next, to_prev)
    lists[1:2, :] = jnp.where(first_core, to_prev, to_next)
    mate[...] = jnp.where(first_core, whole(tails[1], 1), whole(tails[1], 0))
    to_next, to_prev = whole(tails[2], 0), whole(tails[2], 1)
    home_first = lax.axis_index("dom") % 2 == 0
    home_lists[0:1, :] = jnp.where(home_first, to_next, to_prev)
    home_lists[1:2, :] = jnp.where(home_first, to_prev, to_next)


def entry_kernel(mate, here, there, _, hidden, inner):
    block = inner.shape[0]

    @pl.when(is_local())
    def _():
        hidden[...] = here[...]
        inner[...] = listed(mate[:, :1], there[: hidden.shape[0], :], block)

    @pl.when(jnp.logical_not(is_local()))
    def _():
        hidden[...] = there[: hidden.shape[0], :]
        inner[...] = listed(mate[:, :1], here[...], block)


def forward_own_kernel(take, h, gown, *refs):
    w_send, w_recv, w_node, _ = quarters(take[0])
    a_out, u_out = refs[-2:]
    edges = gown.shape[0] // 2
    own = mul(gown[...], h[...]).astype(BF16)
    a_out[...] = mul(own[:edges], w_send[...]) + mul(own[edges:], w_recv[...])
    u_out[...] = mul(h[...], w_node[...])


def forward_kernel(parity, take, lists, h, a_own, u_own, inner, outer, ghalo, gown_t, h_out, a_out, u_out, *to):
    packed, *gains = take
    w_send, _, _, w_fold = quarters(packed)
    gain = jnp.where(here_is(parity=parity), gains[0][...], gains[1][...])
    edges = ghalo.shape[0]
    block = inner.shape[0]
    halo = (mul(ghalo[:, :block], inner[...]) + mul(ghalo[:, block:], outer[...])).astype(BF16)
    a = a_own[...] + mul(halo, w_send[...])
    a_out[...] = a
    q = (a * jax.nn.sigmoid(a)).astype(BF16)
    u = u_own[...] + mul(mul(gown_t[:, edges:], q).astype(BF16), w_fold[...])
    u_out[...] = u
    t, _ = normalize(u * jax.nn.sigmoid(u))
    out = (h[...].astype(F32) + t * gain).astype(BF16)
    h_out[...] = out
    for side, ref in zip((OUTER, INNER), reversed(to)):
        ref[...] = listed(lists[side : side + 1, :1], out, block)


def inner_kernel(lists, h, out):
    out[...] = listed(lists[INNER : INNER + 1, :1], h[...], out.shape[0])


def save_kernel(plane, parity, a, u, h, *refs):
    t_out, r_out, s_out, h_out = refs[-4:]
    rows, edges = h.shape[0], a.shape[0]
    at = slice(parity * rows, (parity + 1) * rows)

    @pl.when(here_is(plane))
    def _():
        s_out[parity * edges : (parity + 1) * edges, :] = slope(a[...]).astype(BF16)
        u_value = u[...]
        t, inverse = normalize(u_value * jax.nn.sigmoid(u_value))
        t_out[at, :] = t.astype(BF16)
        r_out[at, :] = (inverse * slope(u_value)).astype(BF16)
        h_out[at, :] = h[...]


def backward_kernel(sides, finish, parity, kept, take, *refs):
    packed, *gains = take
    w_send, _, _, w_fold = quarters(packed)
    gain = jnp.where(here_is(parity=parity), gains[0][...], gains[1][...])
    lists, upstream, *refs = refs[kept:]
    arrived, refs = refs[: len(sides)], refs[len(sides) :]
    t_in, r_in, s_in, gown, ghalo_t, c_out, du_out, da_out, es_out, *done, to_inner, to_outer = refs
    edges = gown.shape[0] // 2
    rows = upstream.shape[0]
    block = to_inner.shape[0]
    at = slice(parity * rows, (parity + 1) * rows)
    at_edges = slice(parity * edges, (parity + 1) * edges)
    c_out[...] = upstream[...].astype(F32)
    for side, ref in zip(sides, arrived):
        if ref.shape == c_out.shape:
            c_out[...] = c_out[...] + ref[...]
        else:
            add_listed(lists[side : side + 1, :1], c_out, ref[...].astype(F32), block)
    if finish:
        done[0][...] = c_out[...].astype(BF16)
    g = c_out[...] * gain
    t = t_in[at, :].astype(F32)
    centre = jnp.mean(g, axis=-1, keepdims=True)
    along = jnp.mean(g * t, axis=-1, keepdims=True)
    du = ((g - centre - t * along) * r_in[at, :].astype(F32)).astype(BF16)
    du_out[...] = du
    spread = mul(gown[edges:, :], du).astype(BF16)
    da = (mul_t(spread, w_fold[...]) * s_in[at_edges, :].astype(F32)).astype(BF16)
    da_out[...] = da
    es = mul_t(da, w_send[...]).astype(BF16)
    es_out[...] = es
    halo = mul(ghalo_t[...], es).astype(BF16)
    to_inner[...] = halo[:block]
    to_outer[...] = halo[block:]


def backward_own_kernel(add_inner, last, take, *refs):
    _, w_recv, w_node, _ = quarters(take[0])
    if last:
        _, _, other, *refs = refs
    if add_inner:
        lists, inner, *refs = refs
    refs, out = (refs[:-2], refs[-2:]) if last else (refs[:-1], refs[-1:])
    *_, c, du, da, es, gown_t = refs
    er = mul_t(da[...], w_recv[...]).astype(BF16)
    both = jnp.concatenate([es[...], er], axis=0)
    total = c[...] + mul_t(du[...], w_node[...]) + mul(gown_t[...], both)
    if add_inner:
        block = inner.shape[0]
        at = lists[INNER : INNER + 1, :1]
        value = inner[...].astype(F32)
        total = total + jnp.concatenate(
            [jnp.where(at == number, value, 0.0) for number in range(total.shape[0] // block)], axis=0
        )
    if last:
        order(total.astype(BF16), other[...], *out)
    else:
        out[0][...] = total.astype(out[0].dtype)


def order(even, odd, first, second):
    zero = lax.axis_index("dom") % 2 == 0

    @pl.when(zero)
    def _():
        first[...] = even
        second[...] = odd

    @pl.when(jnp.logical_not(zero))
    def _():
        first[...] = odd
        second[...] = even


def order_kernel(both, first, second):
    rows = first.shape[0]
    order(both[:rows, :], both[rows:, :], first, second)


def add_kernel(lists, value, outer, other, first, second, total):
    @pl.when(here_is(1))
    def _():
        total[...] = value[...].astype(F32)
        add_listed(lists[OUTER : OUTER + 1, :1], total, outer[...].astype(F32), outer.shape[0])
        order(total[...].astype(BF16), other[...], first, second)


def spread_kernel(lists, outer, out):
    block = outer.shape[0]
    at = lists[OUTER : OUTER + 1, :1]
    value = outer[...].astype(F32)
    for number in range(out.shape[0] // block):
        out[number * block : (number + 1) * block, :] = jnp.where(at == number, value, 0.0)


def place_kernel(lists, outer, flipped, first, second):
    block = outer.shape[0]
    at = lists[OUTER : OUTER + 1, :1]
    for value, out in ((outer, first), (flipped, second)):
        for number in range(out.shape[0] // block):
            covered = jnp.broadcast_to(at == number, value.shape) & here_is(0, 0)
            out[number * block : (number + 1) * block, :] = jnp.where(covered, value[...].astype(F32), 0.0).astype(BF16)


def sum_kernel(*refs):
    ends, placed, totals = (refs[2 * k : 2 * k + 2] for k in range(3))
    for k in range(2):
        totals[k][...] = (ends[k][...].astype(F32) + placed[k][...].astype(F32)).astype(BF16)


def write_kernel(*refs):
    first_home, second_home, totals = (refs[2 * k : 2 * k + 2] for k in range(3))
    out_home, out_grads, sems = refs[6:]
    core = lax.axis_index("pipe") % 2
    slots = core, 1 - core

    def outputs(source):
        return [pltpu.make_async_copy(source[k], out_home.at[0, slots[k]], sems.at[k]) for k in range(2)]

    copies = [pltpu.make_async_copy(totals[k], out_grads.at[0, slots[k]], sems.at[2 + k]) for k in range(2)]
    for copy in copies:
        copy.start()

    @pl.when(here_is(0))
    def _():
        for copy in outputs(first_home):
            copy.start()

    @pl.when(jnp.logical_not(here_is(0)))
    def _():
        for copy in outputs(second_home):
            copy.start()

    for copy in copies + outputs(first_home):
        copy.wait()


def run(kernel, operands, outs, spaces=(), aliases=None, out_spaces=(), scratch=(), cost=1, vmem=12):
    spaces = tuple(spaces) + (pltpu.VMEM,) * (len(operands) - len(spaces))
    operands = [
        pltpu.with_memory_space_constraint(operand, space) if space == pltpu.HBM else operand
        for operand, space in zip(operands, spaces)
    ]
    out_spaces = tuple(out_spaces) + (pltpu.VMEM,) * (len(outs) - len(out_spaces))
    return pl.pallas_call(
        kernel,
        out_shape=[jax.ShapeDtypeStruct(s, t) for s, t in outs],
        in_specs=[pl.BlockSpec(memory_space=space) for space in spaces],
        out_specs=[pl.BlockSpec(memory_space=space) for space in out_spaces],
        scratch_shapes=list(scratch),
        input_output_aliases=aliases or {},
        compiler_params=pltpu.CompilerParams(vmem_limit_bytes=vmem * 2**20),
        cost_estimate=pl.CostEstimate(flops=cost, bytes_accessed=1, transcendentals=0),
    )(*operands)


def run_section(body, plane, matrices, operands, outs, elsewhere=None, cost=1):
    elsewhere = elsewhere or {}

    def kernel(*refs):
        take, rest = refs[: len(matrices)], refs[len(matrices) :]

        @pl.when(here_is(plane))
        def _():
            body(take, *rest)

        if elsewhere:

            @pl.when(jnp.logical_not(here_is(plane)))
            def _():
                for source, target in elsewhere.items():
                    rest[target][...] = rest[source][...]

    return run(kernel, tuple(matrices) + tuple(operands), outs, cost=cost)


def shards(
    inputs,
    cotangent,
    w_send,
    w_recv,
    w_message,
    w_node,
    w_aggregate,
    gains,
    edge_send,
    edge_recv,
    edge_count,
    halo_send,
):
    sections = lax.axis_size("pipe")
    pairs_total = lax.axis_size("dom") // 2
    phase = lax.axis_index("pipe")
    y = lax.rem(lax.axis_index("dom"), 2)
    plane_here = phase // 2
    rows, latent = inputs.shape[1:]
    edge_blocks, block = edge_send.shape
    edges = edge_blocks * block

    def send(value, rule):
        table = []
        for z in range(pairs_total):
            for which in range(2):
                for x in range(sections // 2):
                    for c in range(2):
                        if (target := rule(z, which, x, c)) is None:
                            continue
                        tz, ty, tx, tc = target
                        target = (2 * (tz % pairs_total) + ty) * sections + 2 * (tx % (sections // 2)) + tc
                        table.append(((2 * z + which) * sections + 2 * x + c, target))
        return lax.ppermute(value, AXES, table)

    def flip_y(value):
        return send(value, lambda z, y, x, c: (z, 1 - y, x, c))

    def flip_core(value):
        return send(value, lambda z, y, x, c: (z, y, x, 1 - c))

    def go_home(first, second, plane=None):
        return (
            send(first, lambda z, y, x, c: (z, c, x, y) if plane in (None, x) else None),
            send(second, lambda z, y, x, c: (z, c, x, 1 - y) if plane in (None, x) else None),
        )

    def towards(value, side, step):
        if side == INNER:
            return send(value, lambda z, y, x, c: (z, y, x, 1 - c))
        return send(value, lambda z, y, x, c: (z + 2 * c - 1, y, x + step, 1 - c) if crosses(x, step) else None)

    def crosses(x, step):
        return step == 0 or 0 <= x + step < sections // 2

    def across(value, step):
        return send(value, lambda z, y, x, c: (z, y, x + step, c) if crosses(x, step) else None)

    wide = (rows, latent)
    edge_wide = (edges, latent)
    narrow = (block, latent)
    unit = 2 * rows * latent * latent
    dma = pltpu.SemaphoreType.DMA

    here, there, boundary, packed = run(
        prepare_kernel,
        (edge_count, jnp.swapaxes(halo_send, 1, 2), inputs, cotangent, edge_send, edge_recv),
        [(wide, BF16), ((rows + 16, latent), BF16), (narrow, BF16), ((16, block), BF16)],
        spaces=(pltpu.HBM,) * 6,
        scratch=[
            pltpu.SMEM((edge_blocks,), jnp.int32),
            pltpu.SMEM((1, 1, 2), jnp.int32),
            pltpu.VMEM(wide, BF16),
            pltpu.VMEM((2, 8, block), jnp.int32),
            dma((7,)),
        ],
    )
    there = flip_y(there)
    outer = send(boundary, lambda z, y, x, c: (z + 2 * y - 1, c, x, 1 - y))
    gown, gown_t, ghalo, ghalo_t, lists, mate, home_lists = run(
        functools.partial(graph_kernel, edge_blocks),
        (packed, there),
        [
            ((2 * edges, rows), BF16),
            ((rows, 2 * edges), BF16),
            ((edges, 2 * block), BF16),
            ((2 * block, edges), BF16),
            ((2, block), jnp.int32),
            ((1, block), jnp.int32),
            ((2, block), jnp.int32),
        ],
    )
    hidden, inner = run(entry_kernel, (mate, here, there, outer), [(wide, BF16), (narrow, BF16)], cost=LONG)

    [weights] = run(
        weights_kernel,
        (w_send[0], w_recv[0], w_node[0], w_message[0], w_aggregate[0]),
        [((4 * latent, latent), BF16)],
        spaces=(pltpu.HBM,) * 5,
        scratch=[pltpu.VMEM((2, latent, latent), BF16), dma((5,))],
    )
    pair = run(place_mine_kernel, (weights,), [((4 * latent, latent), BF16)] * 2)
    matrices = run(
        place_swapped_kernel, (flip_core(weights), hidden, *pair), [((4 * latent, latent), BF16)] * 2, aliases={2: 0, 3: 1}
    )
    both_gains = (gains, flip_core(gains))
    upstream = hidden

    saved = ()
    arrived = ()
    for tick in range(sections):
        plane, parity = tick // 2, tick % 2
        packed = matrices[parity]
        a_own, u_own = run_section(
            forward_own_kernel, plane, (packed,), (hidden, gown) + arrived, [(edge_wide, F32), (wide, F32)], cost=BESIDE
        )
        if tick == sections - 1:
            outputs, a_own = lax.optimization_barrier((saved[3], a_own))
            first_home = go_home(*run(order_kernel, (outputs,), [(wide, BF16)] * 2), plane=0)
        step = (tick + 1) // 2 - plane if tick < sections - 1 else None
        to_send = [(narrow, BF16)] * {0: 2, 1: 1, None: 0}[step]
        hidden, a, u, *to = run_section(
            functools.partial(forward_kernel, parity),
            plane,
            (packed, *both_gains),
            (lists, hidden, a_own, u_own, inner, outer, ghalo, gown_t),
            [(wide, BF16), (edge_wide, F32), (wide, F32)] + to_send,
            cost=1 if to_send else BESIDE // 2,
        )
        produced = hidden
        if to:
            outer = towards(to[-1], OUTER, step)
        if step == 0:
            inner = towards(to[0], INNER, step)
            arrived = (inner,)
        elif step:
            hidden = across(hidden, step)
            inner = towards(*run(inner_kernel, (lists, hidden), [(narrow, BF16)]), INNER, 0)
            arrived = ()
        saved = run(
            functools.partial(save_kernel, plane, parity),
            (a, u, produced) + tuple(saved),
            [((2 * rows, latent), BF16), ((2 * rows, latent), BF16), ((2 * edges, latent), BF16), ((2 * rows, latent), BF16)],
            aliases={3 + k: k for k in range(4)} if saved else None,
            cost=BESIDE,
        )

    *states, both = saved
    halos = {}
    finished = {}
    for tick in range(sections - 1, -1, -1):
        plane, parity = tick // 2, tick % 2
        packed = matrices[parity]
        step = (tick - 1) // 2 - plane if tick else 0
        finish = bool(halos) and tick % 2 == 0
        outs = [(wide, F32), (wide, BF16), (edge_wide, BF16), (edge_wide, BF16)]
        outs += [(wide, BF16)] if finish else []
        outs += [(narrow, BF16)] * 2
        kept = (to_outer,) if tick == 1 else ()
        c, du, da, es, *done, to_inner, to_outer = run_section(
            functools.partial(backward_kernel, tuple(halos), finish, parity, len(kept)),
            plane,
            (packed, *both_gains),
            kept + (lists, upstream) + tuple(halos.values()) + tuple(states) + (gown, ghalo_t),
            outs,
            elsewhere={0: -1} if tick == 1 else {},
        )
        if done:
            finished[tick + 1] = done[0]
        inner = towards(to_inner, INNER, 0)
        halos = {OUTER: towards(to_outer, OUTER, step)} if tick else {}
        add_inner = tick == 0 or step != 0
        last = tuple(ends) + (finished[1],) if tick == 0 else ()
        beside = (lists, inner) if add_inner else (inner,)
        upstream, *rest = run_section(
            functools.partial(backward_own_kernel, add_inner, bool(last)),
            plane,
            (packed,),
            last + beside + (tuple(first_home) if tick == sections - 1 else ()) + (c, du, da, es, gown_t),
            [(wide, BF16)] * 2 if last else [(wide, BF16 if step else F32)],
            elsewhere={0: -2, 1: -1} if last else {},
            cost=BESIDE if tick else 1,
        )
        if not add_inner:
            halos = {INNER: inner, **halos}
        if step:
            own = upstream
            upstream = across(upstream, step)
            halos = {OUTER: run(spread_kernel, (lists, halos[OUTER]), [(wide, F32)], cost=LONG)[0]}
        elif tick == 1:
            outputs, upstream = lax.optimization_barrier((both, upstream))
            second_home = go_home(*run(order_kernel, (outputs,), [(wide, BF16)] * 2), plane=1)
            ends = run(
                add_kernel,
                (lists, own, halos[OUTER], finished[3]),
                [(wide, BF16)] * 2,
                scratch=[pltpu.VMEM(wide, F32)],
            )

    final_outer = send(to_outer, lambda z, y, x, c: (z + 2 * c - 1, 1 - c, x, y))
    ends = go_home(upstream, *rest)
    placed = run(
        place_kernel, (home_lists, final_outer, flip_core(final_outer)), [(wide, BF16)] * 2
    )
    totals = run(sum_kernel, tuple(ends) + tuple(placed), [(wide, BF16)] * 2, cost=LONG)
    return tuple(
        run(
            write_kernel,
            tuple(first_home) + tuple(second_home) + tuple(totals),
            [((1, 2) + wide, BF16)] * 2,
            out_spaces=(pltpu.HBM,) * 2,
            scratch=[dma((4,))],
        )
    )


def solution(mesh):
    in_specs = (
        P(None, "dom", None),
        P(None, "dom", None),
        P("pipe", None, None),
        P("pipe", None, None),
        P("pipe", None, None),
        P("pipe", None, None),
        P("pipe", None, None),
        P("pipe", None),
        P("dom", None),
        P("dom", None),
        P("dom"),
        P("dom", None, None),
    )
    out_specs = (P("pipe", None, "dom", None), P("pipe", None, "dom", None))
    return jax.shard_map(shards, mesh=mesh, in_specs=in_specs, out_specs=out_specs, check_vma=False)
```

```python
import functools

import jax
import jax.numpy as jnp
from jax import lax
from jax.experimental import pallas as pl
from jax.experimental.pallas import tpu as pltpu
from jax.sharding import PartitionSpec as P

EPSILON = 1e-05
F32 = jnp.float32
BF16 = jnp.bfloat16
AXES = ("dom", "pipe")
INNER, OUTER = 0, 1
BESIDE = 4 * 10**9
LONG = 2 * 10**10


def mul(a, b):
    return jnp.dot(a, b, preferred_element_type=F32)


def mul_t(a, b):
    return lax.dot_general(a, b, (((1,), (1,)), ((), ())), preferred_element_type=F32)


def slope(v):
    s = jax.nn.sigmoid(v)
    return s * (1.0 + v * (1.0 - s))


def normalize(z):
    centred = z - jnp.mean(z, axis=-1, keepdims=True)
    inverse = lax.rsqrt(jnp.mean(centred * centred, axis=-1, keepdims=True) + EPSILON)
    return centred * inverse, inverse


def quarters(packed):
    depth = packed.shape[0] // 4
    return [packed.at[pl.ds(number * depth, depth), :] for number in range(4)]


def here_is(plane=None, parity=None):
    pipe = lax.axis_index("pipe")
    wanted = jnp.bool_(True)
    if plane is not None:
        wanted = pipe // 2 == plane
    if parity is not None:
        wanted = wanted & (pipe % 2 == parity)
    return wanted


def is_local():
    return lax.axis_index("pipe") % 2 == lax.axis_index("dom") % 2


def listed(at, value, block):
    picked = value[:block]
    for number in range(1, value.shape[0] // block):
        picked = jnp.where(at == number, value[number * block : (number + 1) * block], picked)
    return picked


def add_listed(at, target, value, block):
    for number in range(target.shape[0] // block):
        rows = slice(number * block, (number + 1) * block)
        target[rows, :] = target[rows, :] + jnp.where(at == number, value, 0.0)


def encode(values):
    high = lax.shift_right_logical(values, 4)
    low = values - high * 16
    return jnp.concatenate([high.astype(F32), low.astype(F32)], axis=0).astype(BF16)


def decode(tile):
    half = tile.shape[0] // 2
    tile = tile.astype(F32)
    return (tile[:half] * 16.0 + tile[half:]).astype(jnp.int32)


def prepare_kernel(
    count_in,
    halo_in,
    inputs,
    cotangent,
    send_in,
    recv_in,
    here,
    there,
    boundary,
    packed,
    count,
    halo,
    blocks,
    edges,
    sems,
):
    micro = lax.axis_index("dom") % 2
    block = boundary.shape[0]
    edge_blocks = send_in.shape[0]
    rows = here.shape[0]
    lists = [
        pltpu.make_async_copy(halo_in, halo, sems.at[0]),
        pltpu.make_async_copy(count_in, count, sems.at[1]),
    ]
    ids = [
        pltpu.make_async_copy(ref, edges.at[k, pl.ds(0, edge_blocks), :], sems.at[2 + k])
        for k, ref in enumerate((send_in, recv_in))
    ]
    def fetch(source):
        return [
            pltpu.make_async_copy(source.at[1 - micro], there.at[pl.ds(0, rows), :], sems.at[4]),
            pltpu.make_async_copy(source.at[micro], here, sems.at[5]),
        ]

    whole = pltpu.make_async_copy(inputs.at[lax.axis_index("pipe") % 2], blocks, sems.at[6])

    for copy in lists + ids:
        copy.start()

    @pl.when(here_is(0))
    def _():
        for copy in fetch(inputs):
            copy.start()

    @pl.when(jnp.logical_not(here_is(0)))
    def _():
        for copy in fetch(cotangent):
            copy.start()

    whole.start()
    for copy in lists:
        copy.wait()
    number = jnp.where(micro == 1, halo[0, 0, 0], halo[0, 0, 1])
    for copy in ids:
        copy.wait()
    lane = lax.broadcasted_iota(jnp.int32, (1, block), 1)
    tail = jnp.where(lane == 0, halo[0, 0, 0], jnp.where(lane == 1, halo[0, 0, 1], 0))
    for place in range(edge_blocks):
        tail = jnp.where(lane == 2 + place, count[place], tail)
    spare = jnp.zeros((7 - 2 * edge_blocks, block), jnp.int32)
    tile = encode(jnp.concatenate([edges[0, :edge_blocks, :], edges[1, :edge_blocks, :], tail, spare], axis=0))
    packed[...] = tile
    there[rows:, :] = jnp.zeros((there.shape[0] - rows, there.shape[1]), BF16)
    there[rows:, :block] = tile
    for copy in fetch(inputs):
        copy.wait()
    whole.wait()
    boundary[...] = blocks[pl.ds(pl.multiple_of(number * block, block), block), :]


def weights_kernel(w_send, w_recv, w_node, w_message, w_aggregate, out, factors, sems):
    depth = w_send.shape[0]
    copies = [pltpu.make_async_copy(ref, factors.at[k], sems.at[k]) for k, ref in enumerate((w_message, w_aggregate))]
    copies += [
        pltpu.make_async_copy(ref, out.at[pl.ds(k * depth, depth), :], sems.at[2 + k])
        for k, ref in enumerate((w_send, w_recv, w_node))
    ]
    for copy in copies:
        copy.start()
    for copy in copies[:2]:
        copy.wait()
    out[3 * depth :, :] = mul(factors[0], factors[1]).astype(BF16)
    for copy in copies[2:]:
        copy.wait()


def place_mine_kernel(mine, even, odd):
    @pl.when(here_is(parity=0))
    def _():
        even[...] = mine[...]

    @pl.when(here_is(parity=1))
    def _():
        odd[...] = mine[...]


def place_swapped_kernel(swapped, _, even_in, odd_in, even, odd):
    del even_in, odd_in

    @pl.when(here_is(parity=0))
    def _():
        odd[...] = swapped[...]

    @pl.when(here_is(parity=1))
    def _():
        even[...] = swapped[...]


def graph_kernel(edge_blocks, packed, there, gown, gown_t, ghalo, ghalo_t, lists, home_lists):
    block = packed.shape[1]
    rows = gown_t.shape[0]
    edges = edge_blocks * block
    local = is_local()
    first_core = lax.axis_index("pipe") % 2 == 0
    last = 2 * edge_blocks
    tiles = decode(packed[...]), decode(there[rows:, :block])
    mine = jnp.where(local, *tiles)
    tails = [tile[last : last + 1] for tile in (mine, tiles[0])]
    lane = lax.broadcasted_iota(jnp.int32, (1, block), 1)
    row = lax.broadcasted_iota(jnp.int32, (rows, block), 0)
    halo_row = lax.broadcasted_iota(jnp.int32, (2 * block, block), 0)
    for number in range(edge_blocks):
        live = lane < tails[0][:, 2 + number : 3 + number]
        sender = jnp.where(live, mine[number : number + 1], -1)
        receiver = jnp.where(live, mine[edge_blocks + number : edge_blocks + number + 1], -1)
        outside = sender - rows
        turned = jnp.where(outside < block, outside + block, outside - block)
        outside = jnp.where(outside >= 0, jnp.where(first_core, turned, outside), -1)
        here = slice(number * block, (number + 1) * block)
        received = slice(edges + number * block, edges + (number + 1) * block)
        for index, at, table, table_t in (
            (sender, here, gown, gown_t),
            (receiver, received, gown, gown_t),
            (outside, here, ghalo, ghalo_t),
        ):
            hot = (index == (halo_row if table is ghalo else row)).astype(F32)
            table_t[:, at] = hot.astype(BF16)
            table[at, :] = hot.T.astype(BF16)

    def whole(tail, place):
        return jnp.broadcast_to(tail[:1, place : place + 1], (1, block))

    to_next, to_prev = whole(tails[0], 0), whole(tails[0], 1)
    lists[0:1, :] = jnp.where(first_core, to_next, to_prev)
    lists[1:2, :] = jnp.where(first_core, to_prev, to_next)
    to_next, to_prev = whole(tails[1], 0), whole(tails[1], 1)
    home_first = lax.axis_index("dom") % 2 == 0
    home_lists[0:1, :] = jnp.where(home_first, to_next, to_prev)
    home_lists[1:2, :] = jnp.where(home_first, to_prev, to_next)


def entry_kernel(here, there, _, lists, hidden, to_inner):
    @pl.when(is_local())
    def _():
        hidden[...] = here[...]

    @pl.when(jnp.logical_not(is_local()))
    def _():
        hidden[...] = there[: hidden.shape[0], :]

    to_inner[...] = listed(lists[INNER : INNER + 1, :1], hidden[...], to_inner.shape[0])


def forward_own_kernel(take, h, gown, *refs):
    w_send, w_recv, w_node, _ = quarters(take[0])
    a_out, u_out = refs[-2:]
    edges = gown.shape[0] // 2
    own = mul(gown[...], h[...]).astype(BF16)
    a_out[...] = mul(own[:edges], w_send[...]) + mul(own[edges:], w_recv[...])
    u_out[...] = mul(h[...], w_node[...])


def forward_kernel(parity, take, lists, h, a_own, u_own, inner, outer, ghalo, gown_t, h_out, a_out, u_out, *to):
    packed, *gains = take
    w_send, _, _, w_fold = quarters(packed)
    gain = jnp.where(here_is(parity=parity), gains[0][...], gains[1][...])
    edges = ghalo.shape[0]
    block = inner.shape[0]
    halo = (mul(ghalo[:, :block], inner[...]) + mul(ghalo[:, block:], outer[...])).astype(BF16)
    a = a_own[...] + mul(halo, w_send[...])
    a_out[...] = a
    q = (a * jax.nn.sigmoid(a)).astype(BF16)
    u = u_own[...] + mul(mul(gown_t[:, edges:], q).astype(BF16), w_fold[...])
    u_out[...] = u
    t, _ = normalize(u * jax.nn.sigmoid(u))
    out = (h[...].astype(F32) + t * gain).astype(BF16)
    h_out[...] = out
    for side, ref in zip((OUTER, INNER), reversed(to)):
        ref[...] = listed(lists[side : side + 1, :1], out, block)


def inner_kernel(lists, h, out):
    out[...] = listed(lists[INNER : INNER + 1, :1], h[...], out.shape[0])


def save_kernel(plane, parity, a, u, h, *refs):
    t_out, r_out, s_out, h_out = refs[-4:]
    rows, edges = h.shape[0], a.shape[0]
    at = slice(parity * rows, (parity + 1) * rows)

    @pl.when(here_is(plane))
    def _():
        s_out[parity * edges : (parity + 1) * edges, :] = slope(a[...]).astype(BF16)
        u_value = u[...]
        t, inverse = normalize(u_value * jax.nn.sigmoid(u_value))
        t_out[at, :] = t.astype(BF16)
        r_out[at, :] = (inverse * slope(u_value)).astype(BF16)
        h_out[at, :] = h[...]


def backward_kernel(sides, finish, parity, kept, take, *refs):
    packed, *gains = take
    w_send, _, _, w_fold = quarters(packed)
    gain = jnp.where(here_is(parity=parity), gains[0][...], gains[1][...])
    lists, upstream, *refs = refs[kept:]
    arrived, refs = refs[: len(sides)], refs[len(sides) :]
    t_in, r_in, s_in, gown, ghalo_t, c_out, du_out, da_out, es_out, *done, to_inner, to_outer = refs
    edges = gown.shape[0] // 2
    rows = upstream.shape[0]
    block = to_inner.shape[0]
    at = slice(parity * rows, (parity + 1) * rows)
    at_edges = slice(parity * edges, (parity + 1) * edges)
    c_out[...] = upstream[...].astype(F32)
    for side, ref in zip(sides, arrived):
        if ref.shape == c_out.shape:
            c_out[...] = c_out[...] + ref[...]
        else:
            add_listed(lists[side : side + 1, :1], c_out, ref[...].astype(F32), block)
    if finish:
        done[0][...] = c_out[...].astype(BF16)
    g = c_out[...] * gain
    t = t_in[at, :].astype(F32)
    centre = jnp.mean(g, axis=-1, keepdims=True)
    along = jnp.mean(g * t, axis=-1, keepdims=True)
    du = ((g - centre - t * along) * r_in[at, :].astype(F32)).astype(BF16)
    du_out[...] = du
    spread = mul(gown[edges:, :], du).astype(BF16)
    da = (mul_t(spread, w_fold[...]) * s_in[at_edges, :].astype(F32)).astype(BF16)
    da_out[...] = da
    es = mul_t(da, w_send[...]).astype(BF16)
    es_out[...] = es
    halo = mul(ghalo_t[...], es).astype(BF16)
    to_inner[...] = halo[:block]
    to_outer[...] = halo[block:]


def backward_own_kernel(add_inner, last, take, *refs):
    _, w_recv, w_node, _ = quarters(take[0])
    if last:
        _, _, other, *refs = refs
    if add_inner:
        lists, inner, *refs = refs
    refs, out = (refs[:-2], refs[-2:]) if last else (refs[:-1], refs[-1:])
    *_, c, du, da, es, gown_t = refs
    er = mul_t(da[...], w_recv[...]).astype(BF16)
    both = jnp.concatenate([es[...], er], axis=0)
    total = c[...] + mul_t(du[...], w_node[...]) + mul(gown_t[...], both)
    if add_inner:
        block = inner.shape[0]
        at = lists[INNER : INNER + 1, :1]
        value = inner[...].astype(F32)
        total = total + jnp.concatenate(
            [jnp.where(at == number, value, 0.0) for number in range(total.shape[0] // block)], axis=0
        )
    if last:
        order(total.astype(BF16), other[...], *out)
    else:
        out[0][...] = total.astype(out[0].dtype)


def order(even, odd, first, second):
    zero = lax.axis_index("dom") % 2 == 0

    @pl.when(zero)
    def _():
        first[...] = even
        second[...] = odd

    @pl.when(jnp.logical_not(zero))
    def _():
        first[...] = odd
        second[...] = even


def order_kernel(both, first, second):
    rows = first.shape[0]
    order(both[:rows, :], both[rows:, :], first, second)


def add_kernel(lists, value, outer, other, first, second, total):
    @pl.when(here_is(1))
    def _():
        total[...] = value[...].astype(F32)
        add_listed(lists[OUTER : OUTER + 1, :1], total, outer[...].astype(F32), outer.shape[0])
        order(total[...].astype(BF16), other[...], first, second)


def spread_kernel(lists, outer, out):
    block = outer.shape[0]
    at = lists[OUTER : OUTER + 1, :1]
    value = outer[...].astype(F32)
    for number in range(out.shape[0] // block):
        out[number * block : (number + 1) * block, :] = jnp.where(at == number, value, 0.0)


def place_kernel(lists, outer, flipped, first, second):
    block = outer.shape[0]
    at = lists[OUTER : OUTER + 1, :1]
    for value, out in ((outer, first), (flipped, second)):
        for number in range(out.shape[0] // block):
            covered = jnp.broadcast_to(at == number, value.shape) & here_is(0, 0)
            out[number * block : (number + 1) * block, :] = jnp.where(covered, value[...].astype(F32), 0.0).astype(BF16)


def sum_kernel(*refs):
    ends, placed, totals = (refs[2 * k : 2 * k + 2] for k in range(3))
    for k in range(2):
        totals[k][...] = (ends[k][...].astype(F32) + placed[k][...].astype(F32)).astype(BF16)


def write_kernel(*refs):
    first_home, second_home, totals = (refs[2 * k : 2 * k + 2] for k in range(3))
    out_home, out_grads, sems = refs[6:]
    core = lax.axis_index("pipe") % 2
    slots = core, 1 - core

    def outputs(source):
        return [pltpu.make_async_copy(source[k], out_home.at[0, slots[k]], sems.at[k]) for k in range(2)]

    copies = [pltpu.make_async_copy(totals[k], out_grads.at[0, slots[k]], sems.at[2 + k]) for k in range(2)]
    for copy in copies:
        copy.start()

    @pl.when(here_is(0))
    def _():
        for copy in outputs(first_home):
            copy.start()

    @pl.when(jnp.logical_not(here_is(0)))
    def _():
        for copy in outputs(second_home):
            copy.start()

    for copy in copies + outputs(first_home):
        copy.wait()


def run(kernel, operands, outs, spaces=(), aliases=None, out_spaces=(), scratch=(), cost=1, vmem=12):
    spaces = tuple(spaces) + (pltpu.VMEM,) * (len(operands) - len(spaces))
    operands = [
        pltpu.with_memory_space_constraint(operand, space) if space == pltpu.HBM else operand
        for operand, space in zip(operands, spaces)
    ]
    out_spaces = tuple(out_spaces) + (pltpu.VMEM,) * (len(outs) - len(out_spaces))
    return pl.pallas_call(
        kernel,
        out_shape=[jax.ShapeDtypeStruct(s, t) for s, t in outs],
        in_specs=[pl.BlockSpec(memory_space=space) for space in spaces],
        out_specs=[pl.BlockSpec(memory_space=space) for space in out_spaces],
        scratch_shapes=list(scratch),
        input_output_aliases=aliases or {},
        compiler_params=pltpu.CompilerParams(vmem_limit_bytes=vmem * 2**20),
        cost_estimate=pl.CostEstimate(flops=cost, bytes_accessed=1, transcendentals=0),
    )(*operands)


def run_section(body, plane, matrices, operands, outs, elsewhere=None, cost=1):
    elsewhere = elsewhere or {}

    def kernel(*refs):
        take, rest = refs[: len(matrices)], refs[len(matrices) :]

        @pl.when(here_is(plane))
        def _():
            body(take, *rest)

        if elsewhere:

            @pl.when(jnp.logical_not(here_is(plane)))
            def _():
                for source, target in elsewhere.items():
                    rest[target][...] = rest[source][...]

    return run(kernel, tuple(matrices) + tuple(operands), outs, cost=cost)


def shards(
    inputs,
    cotangent,
    w_send,
    w_recv,
    w_message,
    w_node,
    w_aggregate,
    gains,
    edge_send,
    edge_recv,
    edge_count,
    halo_send,
):
    sections = lax.axis_size("pipe")
    pairs_total = lax.axis_size("dom") // 2
    phase = lax.axis_index("pipe")
    y = lax.rem(lax.axis_index("dom"), 2)
    plane_here = phase // 2
    rows, latent = inputs.shape[1:]
    edge_blocks, block = edge_send.shape
    edges = edge_blocks * block

    def send(value, rule):
        table = []
        for z in range(pairs_total):
            for which in range(2):
                for x in range(sections // 2):
                    for c in range(2):
                        if (target := rule(z, which, x, c)) is None:
                            continue
                        tz, ty, tx, tc = target
                        target = (2 * (tz % pairs_total) + ty) * sections + 2 * (tx % (sections // 2)) + tc
                        table.append(((2 * z + which) * sections + 2 * x + c, target))
        return lax.ppermute(value, AXES, table)

    def flip_y(value):
        return send(value, lambda z, y, x, c: (z, 1 - y, x, c))

    def flip_core(value):
        return send(value, lambda z, y, x, c: (z, y, x, 1 - c))

    def go_home(first, second, plane=None):
        return (
            send(first, lambda z, y, x, c: (z, c, x, y) if plane in (None, x) else None),
            send(second, lambda z, y, x, c: (z, c, x, 1 - y) if plane in (None, x) else None),
        )

    def towards(value, side, step):
        if side == INNER:
            return send(value, lambda z, y, x, c: (z, y, x, 1 - c))
        return send(value, lambda z, y, x, c: (z + 2 * c - 1, y, x + step, 1 - c) if crosses(x, step) else None)

    def crosses(x, step):
        return step == 0 or 0 <= x + step < sections // 2

    def across(value, step):
        return send(value, lambda z, y, x, c: (z, y, x + step, c) if crosses(x, step) else None)

    wide = (rows, latent)
    edge_wide = (edges, latent)
    narrow = (block, latent)
    unit = 2 * rows * latent * latent
    dma = pltpu.SemaphoreType.DMA

    here, there, boundary, packed = run(
        prepare_kernel,
        (edge_count, jnp.swapaxes(halo_send, 1, 2), inputs, cotangent, edge_send, edge_recv),
        [(wide, BF16), ((rows + 16, latent), BF16), (narrow, BF16), ((16, block), BF16)],
        spaces=(pltpu.HBM,) * 6,
        scratch=[
            pltpu.SMEM((edge_blocks,), jnp.int32),
            pltpu.SMEM((1, 1, 2), jnp.int32),
            pltpu.VMEM(wide, BF16),
            pltpu.VMEM((2, 8, block), jnp.int32),
            dma((7,)),
        ],
    )
    there = send(there, lambda z, y, x, c: (z, 1 - y, x, c) if c == y else (z, y, x, 1 - c))
    outer = send(boundary, lambda z, y, x, c: (z + 2 * y - 1, c, x, 1 - y))
    gown, gown_t, ghalo, ghalo_t, lists, home_lists = run(
        functools.partial(graph_kernel, edge_blocks),
        (packed, there),
        [
            ((2 * edges, rows), BF16),
            ((rows, 2 * edges), BF16),
            ((edges, 2 * block), BF16),
            ((2 * block, edges), BF16),
            ((2, block), jnp.int32),
            ((2, block), jnp.int32),
        ],
    )
    hidden, inner = run(entry_kernel, (here, there, outer, lists), [(wide, BF16), (narrow, BF16)], cost=LONG * 3 // 2)
    inner = towards(inner, INNER, 0)

    [weights] = run(
        weights_kernel,
        (w_send[0], w_recv[0], w_node[0], w_message[0], w_aggregate[0]),
        [((4 * latent, latent), BF16)],
        spaces=(pltpu.HBM,) * 5,
        scratch=[pltpu.VMEM((2, latent, latent), BF16), dma((5,))],
    )
    pair = run(place_mine_kernel, (weights,), [((4 * latent, latent), BF16)] * 2)
    matrices = run(
        place_swapped_kernel, (flip_core(weights), hidden, *pair), [((4 * latent, latent), BF16)] * 2, aliases={2: 0, 3: 1}
    )
    both_gains = (gains, flip_core(gains))
    upstream = hidden

    saved = ()
    arrived = ()
    for tick in range(sections):
        plane, parity = tick // 2, tick % 2
        packed = matrices[parity]
        a_own, u_own = run_section(
            forward_own_kernel, plane, (packed,), (hidden, gown) + arrived, [(edge_wide, F32), (wide, F32)], cost=BESIDE
        )
        if tick == sections - 1:
            outputs, a_own = lax.optimization_barrier((saved[3], a_own))
            first_home = go_home(*run(order_kernel, (outputs,), [(wide, BF16)] * 2), plane=0)
        step = (tick + 1) // 2 - plane if tick < sections - 1 else None
        to_send = [(narrow, BF16)] * {0: 2, 1: 1, None: 0}[step]
        hidden, a, u, *to = run_section(
            functools.partial(forward_kernel, parity),
            plane,
            (packed, *both_gains),
            (lists, hidden, a_own, u_own, inner, outer, ghalo, gown_t),
            [(wide, BF16), (edge_wide, F32), (wide, F32)] + to_send,
            cost=1 if to_send else BESIDE // 2,
        )
        produced = hidden
        if to:
            outer = towards(to[-1], OUTER, step)
        if step == 0:
            inner = towards(to[0], INNER, step)
            arrived = (inner,)
        elif step:
            hidden = across(hidden, step)
            inner = towards(*run(inner_kernel, (lists, hidden), [(narrow, BF16)]), INNER, 0)
            arrived = ()
        saved = run(
            functools.partial(save_kernel, plane, parity),
            (a, u, produced) + tuple(saved),
            [((2 * rows, latent), BF16), ((2 * rows, latent), BF16), ((2 * edges, latent), BF16), ((2 * rows, latent), BF16)],
            aliases={3 + k: k for k in range(4)} if saved else None,
            cost=BESIDE,
        )

    *states, both = saved
    halos = {}
    finished = {}
    second_home = ()
    for tick in range(sections - 1, -1, -1):
        plane, parity = tick // 2, tick % 2
        packed = matrices[parity]
        step = (tick - 1) // 2 - plane if tick else 0
        finish = bool(halos) and tick % 2 == 0
        outs = [(wide, F32), (wide, BF16), (edge_wide, BF16), (edge_wide, BF16)]
        outs += [(wide, BF16)] if finish else []
        outs += [(narrow, BF16)] * 2
        kept = (to_outer,) if tick == 1 else ()
        c, du, da, es, *done, to_inner, to_outer = run_section(
            functools.partial(backward_kernel, tuple(halos), finish, parity, len(kept)),
            plane,
            (packed, *both_gains),
            kept + (lists, upstream) + tuple(halos.values()) + tuple(states) + (gown, ghalo_t),
            outs,
            elsewhere={0: -1} if tick == 1 else {},
            cost=1 if tick else BESIDE // 2,
        )
        if done:
            finished[tick + 1] = done[0]
        inner = towards(to_inner, INNER, 0)
        halos = {OUTER: towards(to_outer, OUTER, step)} if tick else {}
        add_inner = tick == 0 or step != 0
        last = tuple(ends) + (finished[1],) if tick == 0 else ()
        beside = (lists, inner) if add_inner else (inner,)
        upstream, *rest = run_section(
            functools.partial(backward_own_kernel, add_inner, bool(last)),
            plane,
            (packed,),
            last + beside + tuple({sections - 1: first_home, 0: second_home}.get(tick, ())) + (c, du, da, es, gown_t),
            [(wide, BF16)] * 2 if last else [(wide, BF16 if step else F32)],
            elsewhere={0: -2, 1: -1} if last else {},
            cost=BESIDE if tick else 1,
        )
        if not add_inner:
            halos = {INNER: inner, **halos}
        if step:
            own = upstream
            upstream = across(upstream, step)
            halos = {OUTER: run(spread_kernel, (lists, halos[OUTER]), [(wide, F32)], cost=LONG)[0]}
        elif tick == 1:
            outputs, upstream = lax.optimization_barrier((both, upstream))
            second_home = go_home(*run(order_kernel, (outputs,), [(wide, BF16)] * 2), plane=1)
            ends = run(
                add_kernel,
                (lists, own, halos[OUTER], finished[3]),
                [(wide, BF16)] * 2,
                scratch=[pltpu.VMEM(wide, F32)],
            )

    final_outer = send(to_outer, lambda z, y, x, c: (z + 2 * c - 1, 1 - c, x, y))
    ends = go_home(upstream, *rest)
    placed = run(
        place_kernel, (home_lists, final_outer, flip_core(final_outer)), [(wide, BF16)] * 2
    )
    totals = run(sum_kernel, tuple(ends) + tuple(placed), [(wide, BF16)] * 2, cost=LONG)
    return tuple(
        run(
            write_kernel,
            tuple(first_home) + tuple(second_home) + tuple(totals),
            [((1, 2) + wide, BF16)] * 2,
            out_spaces=(pltpu.HBM,) * 2,
            scratch=[dma((4,))],
        )
    )


def solution(mesh):
    in_specs = (
        P(None, "dom", None),
        P(None, "dom", None),
        P("pipe", None, None),
        P("pipe", None, None),
        P("pipe", None, None),
        P("pipe", None, None),
        P("pipe", None, None),
        P("pipe", None),
        P("dom", None),
        P("dom", None),
        P("dom"),
        P("dom", None, None),
    )
    out_specs = (P("pipe", None, "dom", None), P("pipe", None, "dom", None))
    return jax.shard_map(shards, mesh=mesh, in_specs=in_specs, out_specs=out_specs, check_vma=False)
```

```python
import functools

import jax
import jax.numpy as jnp
from jax import lax
from jax.experimental import pallas as pl
from jax.experimental.pallas import tpu as pltpu
from jax.sharding import PartitionSpec as P

EPSILON = 1e-05
F32 = jnp.float32
BF16 = jnp.bfloat16
AXES = ("dom", "pipe")
INNER, OUTER = 0, 1
BESIDE = 4 * 10**9
LONG = 2 * 10**10


def mul(a, b):
    return jnp.dot(a, b, preferred_element_type=F32)


def mul_t(a, b):
    return lax.dot_general(a, b, (((1,), (1,)), ((), ())), preferred_element_type=F32)


def slope(v):
    s = jax.nn.sigmoid(v)
    return s * (1.0 + v * (1.0 - s))


def normalize(z):
    centred = z - jnp.mean(z, axis=-1, keepdims=True)
    inverse = lax.rsqrt(jnp.mean(centred * centred, axis=-1, keepdims=True) + EPSILON)
    return centred * inverse, inverse


def quarters(packed):
    depth = packed.shape[0] // 4
    return [packed.at[pl.ds(number * depth, depth), :] for number in range(4)]


def here_is(plane=None, parity=None):
    pipe = lax.axis_index("pipe")
    wanted = jnp.bool_(True)
    if plane is not None:
        wanted = pipe // 2 == plane
    if parity is not None:
        wanted = wanted & (pipe % 2 == parity)
    return wanted


def is_local():
    return lax.axis_index("pipe") % 2 == lax.axis_index("dom") % 2


def listed(at, value, block):
    picked = value[:block]
    for number in range(1, value.shape[0] // block):
        picked = jnp.where(at == number, value[number * block : (number + 1) * block], picked)
    return picked


def add_listed(at, target, value, block):
    for number in range(target.shape[0] // block):
        rows = slice(number * block, (number + 1) * block)
        target[rows, :] = target[rows, :] + jnp.where(at == number, value, 0.0)


def encode(values):
    high = lax.shift_right_logical(values, 4)
    low = values - high * 16
    return jnp.concatenate([high.astype(F32), low.astype(F32)], axis=0).astype(BF16)


def decode(tile):
    half = tile.shape[0] // 2
    tile = tile.astype(F32)
    return (tile[:half] * 16.0 + tile[half:]).astype(jnp.int32)


def prepare_kernel(
    count_in,
    halo_in,
    inputs,
    cotangent,
    send_in,
    recv_in,
    here,
    there,
    boundary,
    packed,
    count,
    halo,
    blocks,
    edges,
    sems,
):
    micro = lax.axis_index("dom") % 2
    block = boundary.shape[0]
    edge_blocks = send_in.shape[0]
    rows = here.shape[0]
    lists = [
        pltpu.make_async_copy(halo_in, halo, sems.at[0]),
        pltpu.make_async_copy(count_in, count, sems.at[1]),
    ]
    ids = [
        pltpu.make_async_copy(ref, edges.at[k, pl.ds(0, edge_blocks), :], sems.at[2 + k])
        for k, ref in enumerate((send_in, recv_in))
    ]
    def fetch(source):
        return [
            pltpu.make_async_copy(source.at[1 - micro], there.at[pl.ds(0, rows), :], sems.at[4]),
            pltpu.make_async_copy(source.at[micro], here, sems.at[5]),
        ]

    whole = pltpu.make_async_copy(inputs.at[lax.axis_index("pipe") % 2], blocks, sems.at[6])

    for copy in lists + ids:
        copy.start()

    @pl.when(here_is(0))
    def _():
        for copy in fetch(inputs):
            copy.start()

    @pl.when(jnp.logical_not(here_is(0)))
    def _():
        for copy in fetch(cotangent):
            copy.start()

    whole.start()
    for copy in lists:
        copy.wait()
    number = jnp.where(micro == 1, halo[0, 0, 0], halo[0, 0, 1])
    for copy in ids:
        copy.wait()
    lane = lax.broadcasted_iota(jnp.int32, (1, block), 1)
    tail = jnp.where(lane == 0, halo[0, 0, 0], jnp.where(lane == 1, halo[0, 0, 1], 0))
    for place in range(edge_blocks):
        tail = jnp.where(lane == 2 + place, count[place], tail)
    spare = jnp.zeros((7 - 2 * edge_blocks, block), jnp.int32)
    tile = encode(jnp.concatenate([edges[0, :edge_blocks, :], edges[1, :edge_blocks, :], tail, spare], axis=0))
    packed[...] = tile
    there[rows:, :] = jnp.zeros((there.shape[0] - rows, there.shape[1]), BF16)
    there[rows:, :block] = tile
    for copy in fetch(inputs):
        copy.wait()
    whole.wait()
    boundary[...] = blocks[pl.ds(pl.multiple_of(number * block, block), block), :]


def weights_kernel(w_send, w_recv, w_node, w_message, w_aggregate, out, factors, sems):
    depth = w_send.shape[0]
    copies = [pltpu.make_async_copy(ref, factors.at[k], sems.at[k]) for k, ref in enumerate((w_message, w_aggregate))]
    copies += [
        pltpu.make_async_copy(ref, out.at[pl.ds(k * depth, depth), :], sems.at[2 + k])
        for k, ref in enumerate((w_send, w_recv, w_node))
    ]
    for copy in copies:
        copy.start()
    for copy in copies[:2]:
        copy.wait()
    out[3 * depth :, :] = mul(factors[0], factors[1]).astype(BF16)
    for copy in copies[2:]:
        copy.wait()


def place_mine_kernel(mine, even, odd):
    @pl.when(here_is(parity=0))
    def _():
        even[...] = mine[...]

    @pl.when(here_is(parity=1))
    def _():
        odd[...] = mine[...]


def place_swapped_kernel(swapped, _, even_in, odd_in, even, odd):
    del even_in, odd_in

    @pl.when(here_is(parity=0))
    def _():
        odd[...] = swapped[...]

    @pl.when(here_is(parity=1))
    def _():
        even[...] = swapped[...]


def graph_kernel(edge_blocks, packed, there, gown, gown_t, ghalo, ghalo_t, lists, home_lists):
    block = packed.shape[1]
    rows = gown_t.shape[0]
    edges = edge_blocks * block
    local = is_local()
    first_core = lax.axis_index("pipe") % 2 == 0
    last = 2 * edge_blocks
    tiles = decode(packed[...]), decode(there[rows:, :block])
    mine = jnp.where(local, *tiles)
    tails = [tile[last : last + 1] for tile in (mine, tiles[0])]
    lane = lax.broadcasted_iota(jnp.int32, (1, block), 1)
    row = lax.broadcasted_iota(jnp.int32, (rows, block), 0)
    halo_row = lax.broadcasted_iota(jnp.int32, (2 * block, block), 0)
    for number in range(edge_blocks):
        live = lane < tails[0][:, 2 + number : 3 + number]
        sender = jnp.where(live, mine[number : number + 1], -1)
        receiver = jnp.where(live, mine[edge_blocks + number : edge_blocks + number + 1], -1)
        outside = sender - rows
        turned = jnp.where(outside < block, outside + block, outside - block)
        outside = jnp.where(outside >= 0, jnp.where(first_core, turned, outside), -1)
        here = slice(number * block, (number + 1) * block)
        received = slice(edges + number * block, edges + (number + 1) * block)
        for index, at, table, table_t in (
            (sender, here, gown, gown_t),
            (receiver, received, gown, gown_t),
            (outside, here, ghalo, ghalo_t),
        ):
            hot = (index == (halo_row if table is ghalo else row)).astype(F32)
            table_t[:, at] = hot.astype(BF16)
            table[at, :] = hot.T.astype(BF16)

    def whole(tail, place):
        return jnp.broadcast_to(tail[:1, place : place + 1], (1, block))

    to_next, to_prev = whole(tails[0], 0), whole(tails[0], 1)
    lists[0:1, :] = jnp.where(first_core, to_next, to_prev)
    lists[1:2, :] = jnp.where(first_core, to_prev, to_next)
    to_next, to_prev = whole(tails[1], 0), whole(tails[1], 1)
    home_first = lax.axis_index("dom") % 2 == 0
    home_lists[0:1, :] = jnp.where(home_first, to_next, to_prev)
    home_lists[1:2, :] = jnp.where(home_first, to_prev, to_next)


def entry_kernel(here, there, _, lists, hidden, to_inner):
    @pl.when(is_local())
    def _():
        hidden[...] = here[...]

    @pl.when(jnp.logical_not(is_local()))
    def _():
        hidden[...] = there[: hidden.shape[0], :]

    to_inner[...] = listed(lists[INNER : INNER + 1, :1], hidden[...], to_inner.shape[0])


def forward_own_kernel(take, h, gown, *refs):
    w_send, w_recv, w_node, _ = quarters(take[0])
    a_out, u_out = refs[-2:]
    edges = gown.shape[0] // 2
    own = mul(gown[...], h[...]).astype(BF16)
    a_out[...] = mul(own[:edges], w_send[...]) + mul(own[edges:], w_recv[...])
    u_out[...] = mul(h[...], w_node[...])


def forward_kernel(parity, take, lists, h, a_own, u_own, inner, outer, ghalo, gown_t, h_out, a_out, u_out, *to):
    packed, *gains = take
    w_send, _, _, w_fold = quarters(packed)
    gain = jnp.where(here_is(parity=parity), gains[0][...], gains[1][...])
    edges = ghalo.shape[0]
    block = inner.shape[0]
    halo = (mul(ghalo[:, :block], inner[...]) + mul(ghalo[:, block:], outer[...])).astype(BF16)
    a = a_own[...] + mul(halo, w_send[...])
    a_out[...] = a
    q = (a * jax.nn.sigmoid(a)).astype(BF16)
    u = u_own[...] + mul(mul(gown_t[:, edges:], q).astype(BF16), w_fold[...])
    u_out[...] = u
    t, _ = normalize(u * jax.nn.sigmoid(u))
    out = (h[...].astype(F32) + t * gain).astype(BF16)
    h_out[...] = out
    for side, ref in zip((OUTER, INNER), reversed(to)):
        ref[...] = listed(lists[side : side + 1, :1], out, block)


def inner_kernel(lists, h, out):
    out[...] = listed(lists[INNER : INNER + 1, :1], h[...], out.shape[0])


def save_kernel(plane, parity, a, u, h, *refs):
    t_out, r_out, s_out, h_out = refs[-4:]
    rows, edges = h.shape[0], a.shape[0]
    at = slice(parity * rows, (parity + 1) * rows)

    @pl.when(here_is(plane))
    def _():
        s_out[parity * edges : (parity + 1) * edges, :] = slope(a[...]).astype(BF16)
        u_value = u[...]
        t, inverse = normalize(u_value * jax.nn.sigmoid(u_value))
        t_out[at, :] = t.astype(BF16)
        r_out[at, :] = (inverse * slope(u_value)).astype(BF16)
        h_out[at, :] = h[...]


def backward_kernel(sides, finish, parity, kept, take, *refs):
    packed, *gains = take
    w_send, _, _, w_fold = quarters(packed)
    gain = jnp.where(here_is(parity=parity), gains[0][...], gains[1][...])
    lists, upstream, *refs = refs[kept:]
    arrived, refs = refs[: len(sides)], refs[len(sides) :]
    t_in, r_in, s_in, gown, ghalo_t, c_out, du_out, da_out, es_out, *done, to_inner, to_outer = refs
    edges = gown.shape[0] // 2
    rows = upstream.shape[0]
    block = to_inner.shape[0]
    at = slice(parity * rows, (parity + 1) * rows)
    at_edges = slice(parity * edges, (parity + 1) * edges)
    c_out[...] = upstream[...].astype(F32)
    for side, ref in zip(sides, arrived):
        if ref.shape == c_out.shape:
            c_out[...] = c_out[...] + ref[...]
        else:
            add_listed(lists[side : side + 1, :1], c_out, ref[...].astype(F32), block)
    if finish:
        done[0][...] = c_out[...].astype(BF16)
    g = c_out[...] * gain
    t = t_in[at, :].astype(F32)
    centre = jnp.mean(g, axis=-1, keepdims=True)
    along = jnp.mean(g * t, axis=-1, keepdims=True)
    du = ((g - centre - t * along) * r_in[at, :].astype(F32)).astype(BF16)
    du_out[...] = du
    spread = mul(gown[edges:, :], du).astype(BF16)
    da = (mul_t(spread, w_fold[...]) * s_in[at_edges, :].astype(F32)).astype(BF16)
    da_out[...] = da
    es = mul_t(da, w_send[...]).astype(BF16)
    es_out[...] = es
    halo = mul(ghalo_t[...], es).astype(BF16)
    to_inner[...] = halo[:block]
    to_outer[...] = halo[block:]


def backward_own_kernel(add_inner, last, take, *refs):
    _, w_recv, w_node, _ = quarters(take[0])
    if last:
        _, _, other, *refs = refs
    if add_inner:
        lists, inner, *refs = refs
    refs, out = (refs[:-2], refs[-2:]) if last else (refs[:-1], refs[-1:])
    *_, c, du, da, es, gown_t = refs
    er = mul_t(da[...], w_recv[...]).astype(BF16)
    both = jnp.concatenate([es[...], er], axis=0)
    total = c[...] + mul_t(du[...], w_node[...]) + mul(gown_t[...], both)
    if add_inner:
        block = inner.shape[0]
        at = lists[INNER : INNER + 1, :1]
        value = inner[...].astype(F32)
        total = total + jnp.concatenate(
            [jnp.where(at == number, value, 0.0) for number in range(total.shape[0] // block)], axis=0
        )
    if last:
        order(total.astype(BF16), other[...], *out)
    else:
        out[0][...] = total.astype(out[0].dtype)


def order(even, odd, first, second):
    zero = lax.axis_index("dom") % 2 == 0

    @pl.when(zero)
    def _():
        first[...] = even
        second[...] = odd

    @pl.when(jnp.logical_not(zero))
    def _():
        first[...] = odd
        second[...] = even


def order_kernel(both, first, second):
    rows = first.shape[0]
    order(both[:rows, :], both[rows:, :], first, second)


def add_kernel(lists, value, outer, other, first, second, total):
    @pl.when(here_is(1))
    def _():
        total[...] = value[...].astype(F32)
        add_listed(lists[OUTER : OUTER + 1, :1], total, outer[...].astype(F32), outer.shape[0])
        order(total[...].astype(BF16), other[...], first, second)


def spread_kernel(lists, outer, out):
    block = outer.shape[0]
    at = lists[OUTER : OUTER + 1, :1]
    value = outer[...].astype(F32)
    for number in range(out.shape[0] // block):
        out[number * block : (number + 1) * block, :] = jnp.where(at == number, value, 0.0)


def place_kernel(lists, outer, flipped, first, second):
    block = outer.shape[0]
    at = lists[OUTER : OUTER + 1, :1]
    for value, out in ((outer, first), (flipped, second)):
        for number in range(out.shape[0] // block):
            covered = jnp.broadcast_to(at == number, value.shape) & here_is(0, 0)
            out[number * block : (number + 1) * block, :] = jnp.where(covered, value[...].astype(F32), 0.0).astype(BF16)


def sum_kernel(*refs):
    ends, placed, totals = (refs[2 * k : 2 * k + 2] for k in range(3))
    for k in range(2):
        totals[k][...] = (ends[k][...].astype(F32) + placed[k][...].astype(F32)).astype(BF16)


def write_kernel(*refs):
    first_home, second_home, totals = (refs[2 * k : 2 * k + 2] for k in range(3))
    out_home, out_grads, sems = refs[6:]
    core = lax.axis_index("pipe") % 2
    slots = core, 1 - core

    def outputs(source):
        return [pltpu.make_async_copy(source[k], out_home.at[0, slots[k]], sems.at[k]) for k in range(2)]

    copies = [pltpu.make_async_copy(totals[k], out_grads.at[0, slots[k]], sems.at[2 + k]) for k in range(2)]
    for copy in copies:
        copy.start()

    @pl.when(here_is(0))
    def _():
        for copy in outputs(first_home):
            copy.start()

    @pl.when(jnp.logical_not(here_is(0)))
    def _():
        for copy in outputs(second_home):
            copy.start()

    for copy in copies + outputs(first_home):
        copy.wait()


def run(kernel, operands, outs, spaces=(), aliases=None, out_spaces=(), scratch=(), cost=1, vmem=12):
    spaces = tuple(spaces) + (pltpu.VMEM,) * (len(operands) - len(spaces))
    operands = [
        pltpu.with_memory_space_constraint(operand, space) if space == pltpu.HBM else operand
        for operand, space in zip(operands, spaces)
    ]
    out_spaces = tuple(out_spaces) + (pltpu.VMEM,) * (len(outs) - len(out_spaces))
    return pl.pallas_call(
        kernel,
        out_shape=[jax.ShapeDtypeStruct(s, t) for s, t in outs],
        in_specs=[pl.BlockSpec(memory_space=space) for space in spaces],
        out_specs=[pl.BlockSpec(memory_space=space) for space in out_spaces],
        scratch_shapes=list(scratch),
        input_output_aliases=aliases or {},
        compiler_params=pltpu.CompilerParams(vmem_limit_bytes=vmem * 2**20),
        cost_estimate=pl.CostEstimate(flops=cost, bytes_accessed=1, transcendentals=0),
    )(*operands)


def run_section(body, plane, matrices, operands, outs, elsewhere=None, cost=1):
    elsewhere = elsewhere or {}

    def kernel(*refs):
        take, rest = refs[: len(matrices)], refs[len(matrices) :]

        @pl.when(here_is(plane))
        def _():
            body(take, *rest)

        if elsewhere:

            @pl.when(jnp.logical_not(here_is(plane)))
            def _():
                for source, target in elsewhere.items():
                    rest[target][...] = rest[source][...]

    return run(kernel, tuple(matrices) + tuple(operands), outs, cost=cost)


def shards(
    inputs,
    cotangent,
    w_send,
    w_recv,
    w_message,
    w_node,
    w_aggregate,
    gains,
    edge_send,
    edge_recv,
    edge_count,
    halo_send,
):
    sections = lax.axis_size("pipe")
    pairs_total = lax.axis_size("dom") // 2
    phase = lax.axis_index("pipe")
    y = lax.rem(lax.axis_index("dom"), 2)
    plane_here = phase // 2
    rows, latent = inputs.shape[1:]
    edge_blocks, block = edge_send.shape
    edges = edge_blocks * block

    def send(value, rule):
        table = []
        for z in range(pairs_total):
            for which in range(2):
                for x in range(sections // 2):
                    for c in range(2):
                        if (target := rule(z, which, x, c)) is None:
                            continue
                        tz, ty, tx, tc = target
                        target = (2 * (tz % pairs_total) + ty) * sections + 2 * (tx % (sections // 2)) + tc
                        table.append(((2 * z + which) * sections + 2 * x + c, target))
        return lax.ppermute(value, AXES, table)

    def flip_y(value):
        return send(value, lambda z, y, x, c: (z, 1 - y, x, c))

    def flip_core(value):
        return send(value, lambda z, y, x, c: (z, y, x, 1 - c))

    def go_home(first, second, plane=None):
        return (
            send(first, lambda z, y, x, c: (z, c, x, y) if plane in (None, x) else None),
            send(second, lambda z, y, x, c: (z, c, x, 1 - y) if plane in (None, x) else None),
        )

    def towards(value, side, step):
        if side == INNER:
            return send(value, lambda z, y, x, c: (z, y, x, 1 - c))
        return send(value, lambda z, y, x, c: (z + 2 * c - 1, y, x + step, 1 - c) if x + min(step, 0) >= 0 else None)

    def across(value):
        return send(value, lambda z, y, x, c: (z, y, x + 1, c))

    wide = (rows, latent)
    edge_wide = (edges, latent)
    narrow = (block, latent)
    unit = 2 * rows * latent * latent
    dma = pltpu.SemaphoreType.DMA

    here, there, boundary, packed = run(
        prepare_kernel,
        (edge_count, jnp.swapaxes(halo_send, 1, 2), inputs, cotangent, edge_send, edge_recv),
        [(wide, BF16), ((rows + 16, latent), BF16), (narrow, BF16), ((16, block), BF16)],
        spaces=(pltpu.HBM,) * 6,
        scratch=[
            pltpu.SMEM((edge_blocks,), jnp.int32),
            pltpu.SMEM((1, 1, 2), jnp.int32),
            pltpu.VMEM(wide, BF16),
            pltpu.VMEM((2, 8, block), jnp.int32),
            dma((7,)),
        ],
    )
    there = send(there, lambda z, y, x, c: (z, 1 - y, x, c) if c == y else (z, y, x, 1 - c))
    outer = send(boundary, lambda z, y, x, c: (z + 2 * y - 1, c, x, 1 - y))
    gown, gown_t, ghalo, ghalo_t, lists, home_lists = run(
        functools.partial(graph_kernel, edge_blocks),
        (packed, there),
        [
            ((2 * edges, rows), BF16),
            ((rows, 2 * edges), BF16),
            ((edges, 2 * block), BF16),
            ((2 * block, edges), BF16),
            ((2, block), jnp.int32),
            ((2, block), jnp.int32),
        ],
    )
    hidden, inner = run(entry_kernel, (here, there, outer, lists), [(wide, BF16), (narrow, BF16)], cost=LONG * 3 // 2)
    inner = towards(inner, INNER, 0)

    [weights] = run(
        weights_kernel,
        (w_send[0], w_recv[0], w_node[0], w_message[0], w_aggregate[0]),
        [((4 * latent, latent), BF16)],
        spaces=(pltpu.HBM,) * 5,
        scratch=[pltpu.VMEM((2, latent, latent), BF16), dma((5,))],
    )
    pair = run(place_mine_kernel, (weights,), [((4 * latent, latent), BF16)] * 2)
    matrices = run(
        place_swapped_kernel, (flip_core(weights), hidden, *pair), [((4 * latent, latent), BF16)] * 2, aliases={2: 0, 3: 1}
    )
    both_gains = (gains, flip_core(gains))
    upstream = hidden

    saved = ()
    arrived = ()
    for tick in range(sections):
        plane, parity = tick // 2, tick % 2
        packed = matrices[parity]
        a_own, u_own = run_section(
            forward_own_kernel, plane, (packed,), (hidden, gown) + arrived, [(edge_wide, F32), (wide, F32)], cost=BESIDE
        )
        if tick == sections - 1:
            outputs, a_own = lax.optimization_barrier((saved[3], a_own))
            first_home = go_home(*run(order_kernel, (outputs,), [(wide, BF16)] * 2), plane=0)
        step = (tick + 1) // 2 - plane if tick < sections - 1 else None
        to_send = [(narrow, BF16)] * {0: 2, 1: 1, None: 0}[step]
        hidden, a, u, *to = run_section(
            functools.partial(forward_kernel, parity),
            plane,
            (packed, *both_gains),
            (lists, hidden, a_own, u_own, inner, outer, ghalo, gown_t),
            [(wide, BF16), (edge_wide, F32), (wide, F32)] + to_send,
            cost=1 if to_send else BESIDE // 2,
        )
        produced = hidden
        if to:
            outer = towards(to[-1], OUTER, step)
        if step == 0:
            inner = towards(to[0], INNER, step)
            arrived = (inner,)
        elif step:
            hidden = across(hidden)
            inner = towards(*run(inner_kernel, (lists, hidden), [(narrow, BF16)]), INNER, 0)
            arrived = ()
        saved = run(
            functools.partial(save_kernel, plane, parity),
            (a, u, produced) + tuple(saved),
            [((2 * rows, latent), BF16), ((2 * rows, latent), BF16), ((2 * edges, latent), BF16), ((2 * rows, latent), BF16)],
            aliases={3 + k: k for k in range(4)} if saved else None,
            cost=BESIDE,
        )

    *states, both = saved
    halos = {}
    finished = {}
    second_home = ()
    for tick in range(sections - 1, -1, -1):
        plane, parity = tick // 2, tick % 2
        packed = matrices[parity]
        step = (tick - 1) // 2 - plane if tick else 0
        finish = bool(halos) and tick % 2 == 0
        outs = [(wide, F32), (wide, BF16), (edge_wide, BF16), (edge_wide, BF16)]
        outs += [(wide, BF16)] if finish else []
        outs += [(narrow, BF16)] * 2
        kept = (to_outer,) if tick == 1 else ()
        c, du, da, es, *done, to_inner, to_outer = run_section(
            functools.partial(backward_kernel, tuple(halos), finish, parity, len(kept)),
            plane,
            (packed, *both_gains),
            kept + (lists, upstream) + tuple(halos.values()) + tuple(states) + (gown, ghalo_t),
            outs,
            elsewhere={0: -1} if tick == 1 else {},
            cost=1 if tick else BESIDE // 2,
        )
        if done:
            finished[tick + 1] = done[0]
        inner = towards(to_inner, INNER, 0)
        halos = {OUTER: towards(to_outer, OUTER, step)} if tick else {}
        add_inner = tick == 0 or step != 0
        last = tuple(ends) + (finished[1],) if tick == 0 else ()
        beside = (lists, inner) if add_inner else (inner,)
        upstream, *rest = run_section(
            functools.partial(backward_own_kernel, add_inner, bool(last)),
            plane,
            (packed,),
            last + beside + tuple({sections - 1: first_home, 0: second_home}.get(tick, ())) + (c, du, da, es, gown_t),
            [(wide, BF16)] * 2 if last else [(wide, BF16 if step else F32)],
            elsewhere={0: -2, 1: -1} if last else {},
            cost=BESIDE if tick else 1,
        )
        if not add_inner:
            halos = {INNER: inner, **halos}
        if step:
            own = upstream
            upstream = across(upstream)
            halos = {OUTER: run(spread_kernel, (lists, halos[OUTER]), [(wide, F32)], cost=LONG)[0]}
        elif tick == 1:
            outputs, upstream = lax.optimization_barrier((both, upstream))
            second_home = go_home(*run(order_kernel, (outputs,), [(wide, BF16)] * 2), plane=1)
            ends = run(
                add_kernel,
                (lists, own, halos[OUTER], finished[3]),
                [(wide, BF16)] * 2,
                scratch=[pltpu.VMEM(wide, F32)],
            )

    final_outer = send(to_outer, lambda z, y, x, c: (z + 2 * c - 1, 1 - c, x, y))
    ends = go_home(upstream, *rest)
    placed = run(
        place_kernel, (home_lists, final_outer, flip_core(final_outer)), [(wide, BF16)] * 2
    )
    totals = run(sum_kernel, tuple(ends) + tuple(placed), [(wide, BF16)] * 2, cost=LONG)
    return tuple(
        run(
            write_kernel,
            tuple(first_home) + tuple(second_home) + tuple(totals),
            [((1, 2) + wide, BF16)] * 2,
            out_spaces=(pltpu.HBM,) * 2,
            scratch=[dma((4,))],
        )
    )


def solution(mesh):
    in_specs = (
        P(None, "dom", None),
        P(None, "dom", None),
        P("pipe", None, None),
        P("pipe", None, None),
        P("pipe", None, None),
        P("pipe", None, None),
        P("pipe", None, None),
        P("pipe", None),
        P("dom", None),
        P("dom", None),
        P("dom"),
        P("dom", None, None),
    )
    out_specs = (P("pipe", None, "dom", None), P("pipe", None, "dom", None))
    return jax.shard_map(shards, mesh=mesh, in_specs=in_specs, out_specs=out_specs, check_vma=False)
```

```python
import functools

import jax
import jax.numpy as jnp
from jax import lax
from jax.experimental import pallas as pl
from jax.experimental.pallas import tpu as pltpu
from jax.sharding import PartitionSpec as P

EPSILON = 1e-05
F32 = jnp.float32
BF16 = jnp.bfloat16
AXES = ("dom", "pipe")
INNER, OUTER = 0, 1
BESIDE = 4 * 10**9
LONG = 2 * 10**10


def mul(a, b):
    return jnp.dot(a, b, preferred_element_type=F32)


def mul_t(a, b):
    return lax.dot_general(a, b, (((1,), (1,)), ((), ())), preferred_element_type=F32)


def slope(v):
    s = jax.nn.sigmoid(v)
    return s * (1.0 + v * (1.0 - s))


def normalize(z):
    centred = z - jnp.mean(z, axis=-1, keepdims=True)
    inverse = lax.rsqrt(jnp.mean(centred * centred, axis=-1, keepdims=True) + EPSILON)
    return centred * inverse, inverse


def quarters(packed):
    depth = packed.shape[0] // 4
    return [packed.at[pl.ds(number * depth, depth), :] for number in range(4)]


def here_is(plane=None, parity=None):
    pipe = lax.axis_index("pipe")
    wanted = jnp.bool_(True)
    if plane is not None:
        wanted = pipe // 2 == plane
    if parity is not None:
        wanted = wanted & (pipe % 2 == parity)
    return wanted


def is_local():
    return lax.axis_index("pipe") % 2 == lax.axis_index("dom") % 2


def listed(at, value, block):
    picked = value[:block]
    for number in range(1, value.shape[0] // block):
        picked = jnp.where(at == number, value[number * block : (number + 1) * block], picked)
    return picked


def add_listed(at, target, value, block):
    for number in range(target.shape[0] // block):
        rows = slice(number * block, (number + 1) * block)
        target[rows, :] = target[rows, :] + jnp.where(at == number, value, 0.0)


def encode(values):
    high = lax.shift_right_logical(values, 4)
    low = values - high * 16
    return jnp.concatenate([high.astype(F32), low.astype(F32)], axis=0).astype(BF16)


def decode(tile):
    half = tile.shape[0] // 2
    tile = tile.astype(F32)
    return (tile[:half] * 16.0 + tile[half:]).astype(jnp.int32)


def prepare_kernel(
    count_in,
    halo_in,
    inputs,
    cotangent,
    send_in,
    recv_in,
    here,
    there,
    boundary,
    packed,
    count,
    halo,
    blocks,
    edges,
    sems,
):
    micro = lax.axis_index("dom") % 2
    block = boundary.shape[0]
    edge_blocks = send_in.shape[0]
    rows = here.shape[0]
    lists = [
        pltpu.make_async_copy(halo_in, halo, sems.at[0]),
        pltpu.make_async_copy(count_in, count, sems.at[1]),
    ]
    ids = [
        pltpu.make_async_copy(ref, edges.at[k, pl.ds(0, edge_blocks), :], sems.at[2 + k])
        for k, ref in enumerate((send_in, recv_in))
    ]
    def fetch(source):
        return [
            pltpu.make_async_copy(source.at[1 - micro], there.at[pl.ds(0, rows), :], sems.at[4]),
            pltpu.make_async_copy(source.at[micro], here, sems.at[5]),
        ]

    whole = pltpu.make_async_copy(inputs.at[lax.axis_index("pipe") % 2], blocks, sems.at[6])

    for copy in lists + ids:
        copy.start()

    @pl.when(here_is(0))
    def _():
        for copy in fetch(inputs):
            copy.start()

    @pl.when(jnp.logical_not(here_is(0)))
    def _():
        for copy in fetch(cotangent):
            copy.start()

    whole.start()
    for copy in lists:
        copy.wait()
    number = jnp.where(micro == 1, halo[0, 0, 0], halo[0, 0, 1])
    for copy in ids:
        copy.wait()
    lane = lax.broadcasted_iota(jnp.int32, (1, block), 1)
    tail = jnp.where(lane == 0, halo[0, 0, 0], jnp.where(lane == 1, halo[0, 0, 1], 0))
    for place in range(edge_blocks):
        tail = jnp.where(lane == 2 + place, count[place], tail)
    spare = jnp.zeros((7 - 2 * edge_blocks, block), jnp.int32)
    tile = encode(jnp.concatenate([edges[0, :edge_blocks, :], edges[1, :edge_blocks, :], tail, spare], axis=0))
    packed[...] = tile
    there[rows:, :] = jnp.zeros((there.shape[0] - rows, there.shape[1]), BF16)
    there[rows:, :block] = tile
    for copy in fetch(inputs):
        copy.wait()
    whole.wait()
    boundary[...] = blocks[pl.ds(pl.multiple_of(number * block, block), block), :]


def weights_kernel(w_send, w_recv, w_node, w_message, w_aggregate, out, factors, sems):
    depth = w_send.shape[0]
    copies = [pltpu.make_async_copy(ref, factors.at[k], sems.at[k]) for k, ref in enumerate((w_message, w_aggregate))]
    copies += [
        pltpu.make_async_copy(ref, out.at[pl.ds(k * depth, depth), :], sems.at[2 + k])
        for k, ref in enumerate((w_send, w_recv, w_node))
    ]
    for copy in copies:
        copy.start()
    for copy in copies[:2]:
        copy.wait()
    out[3 * depth :, :] = mul(factors[0], factors[1]).astype(BF16)
    for copy in copies[2:]:
        copy.wait()


def place_mine_kernel(mine, even, odd):
    @pl.when(here_is(parity=0))
    def _():
        even[...] = mine[...]

    @pl.when(here_is(parity=1))
    def _():
        odd[...] = mine[...]


def place_swapped_kernel(swapped, _, even_in, odd_in, even, odd):
    del even_in, odd_in

    @pl.when(here_is(parity=0))
    def _():
        odd[...] = swapped[...]

    @pl.when(here_is(parity=1))
    def _():
        even[...] = swapped[...]


def graph_kernel(edge_blocks, packed, there, gown, gown_t, ghalo, ghalo_t, lists, home_lists):
    block = packed.shape[1]
    rows = gown_t.shape[0]
    edges = edge_blocks * block
    local = is_local()
    first_core = lax.axis_index("pipe") % 2 == 0
    last = 2 * edge_blocks
    tiles = decode(packed[...]), decode(there[rows:, :block])
    mine = jnp.where(local, *tiles)
    tails = [tile[last : last + 1] for tile in (mine, tiles[0])]
    lane = lax.broadcasted_iota(jnp.int32, (1, block), 1)
    row = lax.broadcasted_iota(jnp.int32, (rows, block), 0)
    halo_row = lax.broadcasted_iota(jnp.int32, (2 * block, block), 0)
    for number in range(edge_blocks):
        live = lane < tails[0][:, 2 + number : 3 + number]
        sender = jnp.where(live, mine[number : number + 1], -1)
        receiver = jnp.where(live, mine[edge_blocks + number : edge_blocks + number + 1], -1)
        outside = sender - rows
        turned = jnp.where(outside < block, outside + block, outside - block)
        outside = jnp.where(outside >= 0, jnp.where(first_core, turned, outside), -1)
        here = slice(number * block, (number + 1) * block)
        received = slice(edges + number * block, edges + (number + 1) * block)
        for index, at, table, table_t in (
            (sender, here, gown, gown_t),
            (receiver, received, gown, gown_t),
            (outside, here, ghalo, ghalo_t),
        ):
            hot = (index == (halo_row if table is ghalo else row)).astype(F32)
            table_t[:, at] = hot.astype(BF16)
            table[at, :] = hot.T.astype(BF16)

    def whole(tail, place):
        return jnp.broadcast_to(tail[:1, place : place + 1], (1, block))

    to_next, to_prev = whole(tails[0], 0), whole(tails[0], 1)
    lists[0:1, :] = jnp.where(first_core, to_next, to_prev)
    lists[1:2, :] = jnp.where(first_core, to_prev, to_next)
    to_next, to_prev = whole(tails[1], 0), whole(tails[1], 1)
    home_first = lax.axis_index("dom") % 2 == 0
    home_lists[0:1, :] = jnp.where(home_first, to_next, to_prev)
    home_lists[1:2, :] = jnp.where(home_first, to_prev, to_next)


def entry_kernel(here, there, _, lists, hidden, to_inner):
    @pl.when(is_local())
    def _():
        hidden[...] = here[...]

    @pl.when(jnp.logical_not(is_local()))
    def _():
        hidden[...] = there[: hidden.shape[0], :]

    to_inner[...] = listed(lists[INNER : INNER + 1, :1], hidden[...], to_inner.shape[0])


def forward_own_kernel(take, h, gown, *refs):
    w_send, w_recv, w_node, _ = quarters(take[0])
    a_out, u_out = refs[-2:]
    edges = gown.shape[0] // 2
    own = mul(gown[...], h[...]).astype(BF16)
    a_out[...] = mul(own[:edges], w_send[...]) + mul(own[edges:], w_recv[...])
    u_out[...] = mul(h[...], w_node[...])


def forward_kernel(parity, last, take, lists, h, a_own, u_own, inner, outer, ghalo, gown_t, *refs):
    packed, *gains = take
    w_send, _, _, w_fold = quarters(packed)
    gain = jnp.where(here_is(parity=parity), gains[0][...], gains[1][...])
    edges = ghalo.shape[0]
    block = inner.shape[0]
    halo = mul(ghalo[...], jnp.concatenate([inner[...], outer[...]], axis=0)).astype(BF16)
    a = a_own[...] + mul(halo, w_send[...])
    q = (a * jax.nn.sigmoid(a)).astype(BF16)
    u = u_own[...] + mul(mul(gown_t[:, edges:], q).astype(BF16), w_fold[...])
    t, inverse = normalize(u * jax.nn.sigmoid(u))
    out = (h[...].astype(F32) + t * gain).astype(BF16)
    if last:
        keep(parity, a, u, t, inverse, out, *refs[-4:])
        return
    h_out, a_out, u_out, *to = refs
    a_out[...] = a
    u_out[...] = u
    h_out[...] = out
    for side, ref in zip((OUTER, INNER), reversed(to)):
        ref[...] = listed(lists[side : side + 1, :1], out, block)


def inner_kernel(lists, h, out):
    out[...] = listed(lists[INNER : INNER + 1, :1], h[...], out.shape[0])


def keep(parity, a, u, t, inverse, h, t_out, r_out, s_out, h_out):
    rows, edges = h.shape[0], a.shape[0]
    at = slice(parity * rows, (parity + 1) * rows)
    s_out[parity * edges : (parity + 1) * edges, :] = slope(a).astype(BF16)
    t_out[at, :] = t.astype(BF16)
    r_out[at, :] = (inverse * slope(u)).astype(BF16)
    h_out[at, :] = h


def save_kernel(plane, parity, a, u, h, *refs):
    @pl.when(here_is(plane))
    def _():
        u_value = u[...]
        t, inverse = normalize(u_value * jax.nn.sigmoid(u_value))
        keep(parity, a[...], u_value, t, inverse, h[...], *refs[-4:])


def backward_kernel(sides, finish, parity, kept, take, *refs):
    packed, *gains = take
    w_send, _, _, w_fold = quarters(packed)
    gain = jnp.where(here_is(parity=parity), gains[0][...], gains[1][...])
    lists, upstream, *refs = refs[kept:]
    arrived, refs = refs[: len(sides)], refs[len(sides) :]
    t_in, r_in, s_in, gown, ghalo_t, c_out, du_out, da_out, es_out, *done, to_inner, to_outer = refs
    edges = gown.shape[0] // 2
    rows = upstream.shape[0]
    block = to_inner.shape[0]
    at = slice(parity * rows, (parity + 1) * rows)
    at_edges = slice(parity * edges, (parity + 1) * edges)
    c_out[...] = upstream[...].astype(F32)
    for side, ref in zip(sides, arrived):
        if ref.shape == c_out.shape:
            c_out[...] = c_out[...] + ref[...]
        else:
            add_listed(lists[side : side + 1, :1], c_out, ref[...].astype(F32), block)
    if finish:
        done[0][...] = c_out[...].astype(BF16)
    g = c_out[...] * gain
    t = t_in[at, :].astype(F32)
    centre = jnp.mean(g, axis=-1, keepdims=True)
    along = jnp.mean(g * t, axis=-1, keepdims=True)
    du = ((g - centre - t * along) * r_in[at, :].astype(F32)).astype(BF16)
    du_out[...] = du
    spread = mul(gown[edges:, :], du).astype(BF16)
    da = (mul_t(spread, w_fold[...]) * s_in[at_edges, :].astype(F32)).astype(BF16)
    da_out[...] = da
    es = mul_t(da, w_send[...]).astype(BF16)
    es_out[...] = es
    halo = mul(ghalo_t[...], es).astype(BF16)
    to_inner[...] = halo[:block]
    to_outer[...] = halo[block:]


def backward_own_kernel(add_inner, last, take, *refs):
    _, w_recv, w_node, _ = quarters(take[0])
    if last:
        _, _, other, *refs = refs
    if add_inner:
        lists, inner, *refs = refs
    refs, out = (refs[:-2], refs[-2:]) if last else (refs[:-1], refs[-1:])
    *_, c, du, da, es, gown_t = refs
    er = mul_t(da[...], w_recv[...]).astype(BF16)
    both = jnp.concatenate([es[...], er], axis=0)
    total = c[...] + mul_t(du[...], w_node[...]) + mul(gown_t[...], both)
    if add_inner:
        block = inner.shape[0]
        at = lists[INNER : INNER + 1, :1]
        value = inner[...].astype(F32)
        total = total + jnp.concatenate(
            [jnp.where(at == number, value, 0.0) for number in range(total.shape[0] // block)], axis=0
        )
    if last:
        order(total.astype(BF16), other[...], *out)
    else:
        out[0][...] = total.astype(out[0].dtype)


def order(even, odd, first, second):
    zero = lax.axis_index("dom") % 2 == 0

    @pl.when(zero)
    def _():
        first[...] = even
        second[...] = odd

    @pl.when(jnp.logical_not(zero))
    def _():
        first[...] = odd
        second[...] = even


def order_kernel(both, first, second):
    rows = first.shape[0]
    order(both[:rows, :], both[rows:, :], first, second)


def add_kernel(lists, value, outer, other, first, second, total):
    @pl.when(here_is(1))
    def _():
        total[...] = value[...].astype(F32)
        add_listed(lists[OUTER : OUTER + 1, :1], total, outer[...].astype(F32), outer.shape[0])
        order(total[...].astype(BF16), other[...], first, second)


def spread_kernel(lists, outer, out):
    block = outer.shape[0]
    at = lists[OUTER : OUTER + 1, :1]
    value = outer[...].astype(F32)
    for number in range(out.shape[0] // block):
        out[number * block : (number + 1) * block, :] = jnp.where(at == number, value, 0.0)


def place_kernel(lists, outer, flipped, first, second):
    block = outer.shape[0]
    at = lists[OUTER : OUTER + 1, :1]
    for value, out in ((outer, first), (flipped, second)):
        for number in range(out.shape[0] // block):
            covered = jnp.broadcast_to(at == number, value.shape) & here_is(0, 0)
            out[number * block : (number + 1) * block, :] = jnp.where(covered, value[...].astype(F32), 0.0).astype(BF16)


def sum_kernel(*refs):
    ends, placed, totals = (refs[2 * k : 2 * k + 2] for k in range(3))
    for k in range(2):
        totals[k][...] = (ends[k][...].astype(F32) + placed[k][...].astype(F32)).astype(BF16)


def write_kernel(*refs):
    first_home, second_home, totals = (refs[2 * k : 2 * k + 2] for k in range(3))
    out_home, out_grads, sems = refs[6:]
    core = lax.axis_index("pipe") % 2
    slots = core, 1 - core

    def outputs(source):
        return [pltpu.make_async_copy(source[k], out_home.at[0, slots[k]], sems.at[k]) for k in range(2)]

    copies = [pltpu.make_async_copy(totals[k], out_grads.at[0, slots[k]], sems.at[2 + k]) for k in range(2)]
    for copy in copies:
        copy.start()

    @pl.when(here_is(0))
    def _():
        for copy in outputs(first_home):
            copy.start()

    @pl.when(jnp.logical_not(here_is(0)))
    def _():
        for copy in outputs(second_home):
            copy.start()

    for copy in copies + outputs(first_home):
        copy.wait()


def run(kernel, operands, outs, spaces=(), aliases=None, out_spaces=(), scratch=(), cost=1, vmem=12):
    spaces = tuple(spaces) + (pltpu.VMEM,) * (len(operands) - len(spaces))
    operands = [
        pltpu.with_memory_space_constraint(operand, space) if space == pltpu.HBM else operand
        for operand, space in zip(operands, spaces)
    ]
    out_spaces = tuple(out_spaces) + (pltpu.VMEM,) * (len(outs) - len(out_spaces))
    return pl.pallas_call(
        kernel,
        out_shape=[jax.ShapeDtypeStruct(s, t) for s, t in outs],
        in_specs=[pl.BlockSpec(memory_space=space) for space in spaces],
        out_specs=[pl.BlockSpec(memory_space=space) for space in out_spaces],
        scratch_shapes=list(scratch),
        input_output_aliases=aliases or {},
        compiler_params=pltpu.CompilerParams(vmem_limit_bytes=vmem * 2**20),
        cost_estimate=pl.CostEstimate(flops=cost, bytes_accessed=1, transcendentals=0),
    )(*operands)


def run_section(body, plane, matrices, operands, outs, elsewhere=None, aliases=None, cost=1):
    elsewhere = elsewhere or {}

    def kernel(*refs):
        take, rest = refs[: len(matrices)], refs[len(matrices) :]

        @pl.when(here_is(plane))
        def _():
            body(take, *rest)

        if elsewhere:

            @pl.when(jnp.logical_not(here_is(plane)))
            def _():
                for source, target in elsewhere.items():
                    rest[target][...] = rest[source][...]

    aliases = {len(matrices) + source: target for source, target in (aliases or {}).items()}
    return run(kernel, tuple(matrices) + tuple(operands), outs, aliases=aliases, cost=cost)


def shards(
    inputs,
    cotangent,
    w_send,
    w_recv,
    w_message,
    w_node,
    w_aggregate,
    gains,
    edge_send,
    edge_recv,
    edge_count,
    halo_send,
):
    sections = lax.axis_size("pipe")
    pairs_total = lax.axis_size("dom") // 2
    phase = lax.axis_index("pipe")
    y = lax.rem(lax.axis_index("dom"), 2)
    plane_here = phase // 2
    rows, latent = inputs.shape[1:]
    edge_blocks, block = edge_send.shape
    edges = edge_blocks * block

    def send(value, rule):
        table = []
        for z in range(pairs_total):
            for which in range(2):
                for x in range(sections // 2):
                    for c in range(2):
                        if (target := rule(z, which, x, c)) is None:
                            continue
                        tz, ty, tx, tc = target
                        target = (2 * (tz % pairs_total) + ty) * sections + 2 * (tx % (sections // 2)) + tc
                        table.append(((2 * z + which) * sections + 2 * x + c, target))
        return lax.ppermute(value, AXES, table)

    def flip_y(value):
        return send(value, lambda z, y, x, c: (z, 1 - y, x, c))

    def flip_core(value):
        return send(value, lambda z, y, x, c: (z, y, x, 1 - c))

    def go_home(first, second, plane=None):
        return (
            send(first, lambda z, y, x, c: (z, c, x, y) if plane in (None, x) else None),
            send(second, lambda z, y, x, c: (z, c, x, 1 - y) if plane in (None, x) else None),
        )

    def towards(value, side, step):
        if side == INNER:
            return send(value, lambda z, y, x, c: (z, y, x, 1 - c))
        return send(value, lambda z, y, x, c: (z + 2 * c - 1, y, x + step, 1 - c) if x + min(step, 0) >= 0 else None)

    def across(value):
        return send(value, lambda z, y, x, c: (z, y, x + 1, c))

    wide = (rows, latent)
    edge_wide = (edges, latent)
    narrow = (block, latent)
    both_wide = (2 * rows, latent)
    unit = 2 * rows * latent * latent
    dma = pltpu.SemaphoreType.DMA

    here, there, boundary, packed = run(
        prepare_kernel,
        (edge_count, jnp.swapaxes(halo_send, 1, 2), inputs, cotangent, edge_send, edge_recv),
        [(wide, BF16), ((rows + 16, latent), BF16), (narrow, BF16), ((16, block), BF16)],
        spaces=(pltpu.HBM,) * 6,
        scratch=[
            pltpu.SMEM((edge_blocks,), jnp.int32),
            pltpu.SMEM((1, 1, 2), jnp.int32),
            pltpu.VMEM(wide, BF16),
            pltpu.VMEM((2, 8, block), jnp.int32),
            dma((7,)),
        ],
    )
    there = send(there, lambda z, y, x, c: (z, 1 - y, x, c) if c == y else (z, y, x, 1 - c))
    outer = send(boundary, lambda z, y, x, c: (z + 2 * y - 1, c, x, 1 - y))
    gown, gown_t, ghalo, ghalo_t, lists, home_lists = run(
        functools.partial(graph_kernel, edge_blocks),
        (packed, there),
        [
            ((2 * edges, rows), BF16),
            ((rows, 2 * edges), BF16),
            ((edges, 2 * block), BF16),
            ((2 * block, edges), BF16),
            ((2, block), jnp.int32),
            ((2, block), jnp.int32),
        ],
    )
    hidden, inner = run(entry_kernel, (here, there, outer, lists), [(wide, BF16), (narrow, BF16)], cost=LONG * 3 // 2)
    inner = towards(inner, INNER, 0)

    [weights] = run(
        weights_kernel,
        (w_send[0], w_recv[0], w_node[0], w_message[0], w_aggregate[0]),
        [((4 * latent, latent), BF16)],
        spaces=(pltpu.HBM,) * 5,
        scratch=[pltpu.VMEM((2, latent, latent), BF16), dma((5,))],
    )
    pair = run(place_mine_kernel, (weights,), [((4 * latent, latent), BF16)] * 2)
    matrices = run(
        place_swapped_kernel, (flip_core(weights), hidden, *pair), [((4 * latent, latent), BF16)] * 2, aliases={2: 0, 3: 1}
    )
    both_gains = (gains, flip_core(gains))
    upstream = hidden

    saved = ()
    arrived = ()
    for tick in range(sections):
        plane, parity = tick // 2, tick % 2
        packed = matrices[parity]
        a_own, u_own = run_section(
            forward_own_kernel, plane, (packed,), (hidden, gown) + arrived, [(edge_wide, F32), (wide, F32)], cost=BESIDE
        )
        if tick == sections - 1:
            outputs, a_own = lax.optimization_barrier((saved[3], a_own))
            first_home = go_home(*run(order_kernel, (outputs,), [(wide, BF16)] * 2), plane=0)
        step = (tick + 1) // 2 - plane if tick < sections - 1 else None
        to_send = [(narrow, BF16)] * {0: 2, 1: 1, None: 0}[step]
        last = tick == sections - 1
        state = [(both_wide, BF16), (both_wide, BF16), ((2 * edges, latent), BF16), (both_wide, BF16)]
        made = run_section(
            functools.partial(forward_kernel, parity, last),
            plane,
            (packed, *both_gains),
            (lists, hidden, a_own, u_own, inner, outer, ghalo, gown_t) + (tuple(saved) if last else ()),
            state if last else [(wide, BF16), (edge_wide, F32), (wide, F32)] + to_send,
            aliases={8 + k: k for k in range(4)} if last else None,
            cost=BESIDE // 2 if last else 1,
        )
        if last:
            saved = made
            break
        hidden, a, u, *to = made
        produced = hidden
        if to:
            outer = towards(to[-1], OUTER, step)
        if step == 0:
            inner = towards(to[0], INNER, step)
            arrived = (inner,)
        elif step:
            hidden = across(hidden)
            inner = towards(*run(inner_kernel, (lists, hidden), [(narrow, BF16)]), INNER, 0)
            arrived = ()
        saved = run(
            functools.partial(save_kernel, plane, parity),
            (a, u, produced) + tuple(saved),
            state,
            aliases={3 + k: k for k in range(4)} if saved else None,
            cost=BESIDE,
        )

    *states, both = saved
    halos = {}
    finished = {}
    second_home = ()
    for tick in range(sections - 1, -1, -1):
        plane, parity = tick // 2, tick % 2
        packed = matrices[parity]
        step = (tick - 1) // 2 - plane if tick else 0
        finish = bool(halos) and tick % 2 == 0
        outs = [(wide, F32), (wide, BF16), (edge_wide, BF16), (edge_wide, BF16)]
        outs += [(wide, BF16)] if finish else []
        outs += [(narrow, BF16)] * 2
        kept = (to_outer,) if tick == 1 else ()
        c, du, da, es, *done, to_inner, to_outer = run_section(
            functools.partial(backward_kernel, tuple(halos), finish, parity, len(kept)),
            plane,
            (packed, *both_gains),
            kept + (lists, upstream) + tuple(halos.values()) + tuple(states) + (gown, ghalo_t),
            outs,
            elsewhere={0: -1} if tick == 1 else {},
            cost=1 if tick else BESIDE // 2,
        )
        if done:
            finished[tick + 1] = done[0]
        inner = towards(to_inner, INNER, 0)
        halos = {OUTER: towards(to_outer, OUTER, step)} if tick else {}
        add_inner = tick == 0 or step != 0
        last = tuple(ends) + (finished[1],) if tick == 0 else ()
        beside = (lists, inner) if add_inner else (inner,)
        upstream, *rest = run_section(
            functools.partial(backward_own_kernel, add_inner, bool(last)),
            plane,
            (packed,),
            last + beside + tuple({sections - 1: first_home, 0: second_home}.get(tick, ())) + (c, du, da, es, gown_t),
            [(wide, BF16)] * 2 if last else [(wide, BF16 if step else F32)],
            elsewhere={0: -2, 1: -1} if last else {},
            cost=BESIDE if tick else 1,
        )
        if not add_inner:
            halos = {INNER: inner, **halos}
        if step:
            own = upstream
            upstream = across(upstream)
            halos = {OUTER: run(spread_kernel, (lists, halos[OUTER]), [(wide, F32)], cost=LONG)[0]}
        elif tick == 1:
            outputs, upstream = lax.optimization_barrier((both, upstream))
            second_home = go_home(*run(order_kernel, (outputs,), [(wide, BF16)] * 2), plane=1)
            ends = run(
                add_kernel,
                (lists, own, halos[OUTER], finished[3]),
                [(wide, BF16)] * 2,
                scratch=[pltpu.VMEM(wide, F32)],
            )

    final_outer = send(to_outer, lambda z, y, x, c: (z + 2 * c - 1, 1 - c, x, y))
    ends = go_home(upstream, *rest)
    placed = run(
        place_kernel, (home_lists, final_outer, flip_core(final_outer)), [(wide, BF16)] * 2
    )
    totals = run(sum_kernel, tuple(ends) + tuple(placed), [(wide, BF16)] * 2, cost=LONG)
    return tuple(
        run(
            write_kernel,
            tuple(first_home) + tuple(second_home) + tuple(totals),
            [((1, 2) + wide, BF16)] * 2,
            out_spaces=(pltpu.HBM,) * 2,
            scratch=[dma((4,))],
        )
    )


def solution(mesh):
    in_specs = (
        P(None, "dom", None),
        P(None, "dom", None),
        P("pipe", None, None),
        P("pipe", None, None),
        P("pipe", None, None),
        P("pipe", None, None),
        P("pipe", None, None),
        P("pipe", None),
        P("dom", None),
        P("dom", None),
        P("dom"),
        P("dom", None, None),
    )
    out_specs = (P("pipe", None, "dom", None), P("pipe", None, "dom", None))
    return jax.shard_map(shards, mesh=mesh, in_specs=in_specs, out_specs=out_specs, check_vma=False)
```

```python
import functools

import jax
import jax.numpy as jnp
from jax import lax
from jax.experimental import pallas as pl
from jax.experimental.pallas import tpu as pltpu
from jax.sharding import PartitionSpec as P

EPSILON = 1e-05
F32 = jnp.float32
BF16 = jnp.bfloat16
AXES = ("dom", "pipe")
INNER, OUTER = 0, 1
BESIDE = 4 * 10**9
LONG = 2 * 10**10


def mul(a, b):
    return jnp.dot(a, b, preferred_element_type=F32)


def mul_t(a, b):
    return lax.dot_general(a, b, (((1,), (1,)), ((), ())), preferred_element_type=F32)


def slope(v):
    s = jax.nn.sigmoid(v)
    return s * (1.0 + v * (1.0 - s))


def normalize(z):
    centred = z - jnp.mean(z, axis=-1, keepdims=True)
    inverse = lax.rsqrt(jnp.mean(centred * centred, axis=-1, keepdims=True) + EPSILON)
    return centred * inverse, inverse


def quarters(packed):
    depth = packed.shape[0] // 4
    return [packed.at[pl.ds(number * depth, depth), :] for number in range(4)]


def here_is(plane=None, parity=None):
    pipe = lax.axis_index("pipe")
    wanted = jnp.bool_(True)
    if plane is not None:
        wanted = pipe // 2 == plane
    if parity is not None:
        wanted = wanted & (pipe % 2 == parity)
    return wanted


def is_local():
    return lax.axis_index("pipe") % 2 == lax.axis_index("dom") % 2


def listed(at, value, block):
    picked = value[:block]
    for number in range(1, value.shape[0] // block):
        picked = jnp.where(at == number, value[number * block : (number + 1) * block], picked)
    return picked


def add_listed(at, target, value, block):
    for number in range(target.shape[0] // block):
        rows = slice(number * block, (number + 1) * block)
        target[rows, :] = target[rows, :] + jnp.where(at == number, value, 0.0)


def encode(values):
    high = lax.shift_right_logical(values, 4)
    low = values - high * 16
    return jnp.concatenate([high.astype(F32), low.astype(F32)], axis=0).astype(BF16)


def decode(tile):
    half = tile.shape[0] // 2
    tile = tile.astype(F32)
    return (tile[:half] * 16.0 + tile[half:]).astype(jnp.int32)


def prepare_kernel(
    count_in,
    halo_in,
    inputs,
    cotangent,
    send_in,
    recv_in,
    here,
    there,
    boundary,
    packed,
    count,
    halo,
    blocks,
    edges,
    sems,
):
    micro = lax.axis_index("dom") % 2
    block = boundary.shape[0]
    edge_blocks = send_in.shape[0]
    rows = here.shape[0]
    lists = [
        pltpu.make_async_copy(halo_in, halo, sems.at[0]),
        pltpu.make_async_copy(count_in, count, sems.at[1]),
    ]
    ids = [
        pltpu.make_async_copy(ref, edges.at[k, pl.ds(0, edge_blocks), :], sems.at[2 + k])
        for k, ref in enumerate((send_in, recv_in))
    ]
    def fetch(source):
        return [
            pltpu.make_async_copy(source.at[1 - micro], there.at[pl.ds(0, rows), :], sems.at[4]),
            pltpu.make_async_copy(source.at[micro], here, sems.at[5]),
        ]

    whole = pltpu.make_async_copy(inputs.at[lax.axis_index("pipe") % 2], blocks, sems.at[6])

    for copy in lists + ids:
        copy.start()

    @pl.when(here_is(0))
    def _():
        for copy in fetch(inputs):
            copy.start()

    @pl.when(jnp.logical_not(here_is(0)))
    def _():
        for copy in fetch(cotangent):
            copy.start()

    whole.start()
    for copy in lists:
        copy.wait()
    number = jnp.where(micro == 1, halo[0, 0, 0], halo[0, 0, 1])
    for copy in ids:
        copy.wait()
    lane = lax.broadcasted_iota(jnp.int32, (1, block), 1)
    tail = jnp.where(lane == 0, halo[0, 0, 0], jnp.where(lane == 1, halo[0, 0, 1], 0))
    for place in range(edge_blocks):
        tail = jnp.where(lane == 2 + place, count[place], tail)
    spare = jnp.zeros((7 - 2 * edge_blocks, block), jnp.int32)
    tile = encode(jnp.concatenate([edges[0, :edge_blocks, :], edges[1, :edge_blocks, :], tail, spare], axis=0))
    packed[...] = tile
    there[rows:, :] = jnp.zeros((there.shape[0] - rows, there.shape[1]), BF16)
    there[rows:, :block] = tile
    for copy in fetch(inputs):
        copy.wait()
    whole.wait()
    boundary[...] = blocks[pl.ds(pl.multiple_of(number * block, block), block), :]


def weights_kernel(w_send, w_recv, w_node, w_message, w_aggregate, out, factors, sems):
    depth = w_send.shape[0]
    copies = [pltpu.make_async_copy(ref, factors.at[k], sems.at[k]) for k, ref in enumerate((w_message, w_aggregate))]
    copies += [
        pltpu.make_async_copy(ref, out.at[pl.ds(k * depth, depth), :], sems.at[2 + k])
        for k, ref in enumerate((w_send, w_recv, w_node))
    ]
    for copy in copies:
        copy.start()
    for copy in copies[:2]:
        copy.wait()
    out[3 * depth :, :] = mul(factors[0], factors[1]).astype(BF16)
    for copy in copies[2:]:
        copy.wait()


def place_mine_kernel(mine, even, odd):
    @pl.when(here_is(parity=0))
    def _():
        even[...] = mine[...]

    @pl.when(here_is(parity=1))
    def _():
        odd[...] = mine[...]


def place_swapped_kernel(swapped, _, even_in, odd_in, even, odd):
    del even_in, odd_in

    @pl.when(here_is(parity=0))
    def _():
        odd[...] = swapped[...]

    @pl.when(here_is(parity=1))
    def _():
        even[...] = swapped[...]


def graph_kernel(edge_blocks, packed, there, gown, gown_t, ghalo, ghalo_t, lists, home_lists):
    block = packed.shape[1]
    rows = gown_t.shape[0]
    edges = edge_blocks * block
    local = is_local()
    first_core = lax.axis_index("pipe") % 2 == 0
    last = 2 * edge_blocks
    tiles = decode(packed[...]), decode(there[rows:, :block])
    mine = jnp.where(local, *tiles)
    tails = [tile[last : last + 1] for tile in (mine, tiles[0])]
    lane = lax.broadcasted_iota(jnp.int32, (1, block), 1)
    row = lax.broadcasted_iota(jnp.int32, (rows, block), 0)
    halo_row = lax.broadcasted_iota(jnp.int32, (2 * block, block), 0)
    for number in range(edge_blocks):
        live = lane < tails[0][:, 2 + number : 3 + number]
        sender = jnp.where(live, mine[number : number + 1], -1)
        receiver = jnp.where(live, mine[edge_blocks + number : edge_blocks + number + 1], -1)
        outside = sender - rows
        turned = jnp.where(outside < block, outside + block, outside - block)
        outside = jnp.where(outside >= 0, jnp.where(first_core, turned, outside), -1)
        here = slice(number * block, (number + 1) * block)
        received = slice(edges + number * block, edges + (number + 1) * block)
        for index, at, table, table_t in (
            (sender, here, gown, gown_t),
            (receiver, received, gown, gown_t),
            (outside, here, ghalo, ghalo_t),
        ):
            hot = (index == (halo_row if table is ghalo else row)).astype(F32)
            table_t[:, at] = hot.astype(BF16)
            table[at, :] = hot.T.astype(BF16)

    def whole(tail, place):
        return jnp.broadcast_to(tail[:1, place : place + 1], (1, block))

    to_next, to_prev = whole(tails[0], 0), whole(tails[0], 1)
    lists[0:1, :] = jnp.where(first_core, to_next, to_prev)
    lists[1:2, :] = jnp.where(first_core, to_prev, to_next)
    to_next, to_prev = whole(tails[1], 0), whole(tails[1], 1)
    home_first = lax.axis_index("dom") % 2 == 0
    home_lists[0:1, :] = jnp.where(home_first, to_next, to_prev)
    home_lists[1:2, :] = jnp.where(home_first, to_prev, to_next)


def entry_kernel(here, there, _, lists, hidden, to_inner):
    @pl.when(is_local())
    def _():
        hidden[...] = here[...]

    @pl.when(jnp.logical_not(is_local()))
    def _():
        hidden[...] = there[: hidden.shape[0], :]

    to_inner[...] = listed(lists[INNER : INNER + 1, :1], hidden[...], to_inner.shape[0])


def forward_own_kernel(take, h, gown, *refs):
    w_send, w_recv, w_node, _ = quarters(take[0])
    a_out, u_out = refs[-2:]
    edges = gown.shape[0] // 2
    own = mul(gown[...], h[...]).astype(BF16)
    a_out[...] = mul(own[:edges], w_send[...]) + mul(own[edges:], w_recv[...])
    u_out[...] = mul(h[...], w_node[...])


def forward_kernel(parity, last, take, lists, h, a_own, u_own, inner, outer, ghalo, gown_t, *refs):
    packed, *gains = take
    w_send, _, _, w_fold = quarters(packed)
    gain = jnp.where(here_is(parity=parity), gains[0][...], gains[1][...])
    edges = ghalo.shape[0]
    block = inner.shape[0]
    halo = mul(ghalo[...], jnp.concatenate([inner[...], outer[...]], axis=0)).astype(BF16)
    a = a_own[...] + mul(halo, w_send[...])
    q = (a * jax.nn.sigmoid(a)).astype(BF16)
    u = u_own[...] + mul(mul(gown_t[:, edges:], q).astype(BF16), w_fold[...])
    t, inverse = normalize(u * jax.nn.sigmoid(u))
    out = (h[...].astype(F32) + t * gain).astype(BF16)
    if last:
        keep(parity, a, u, t, inverse, out, *refs[-4:])
        return
    h_out, a_out, u_out, *to = refs
    a_out[...] = a
    u_out[...] = u
    h_out[...] = out
    for side, ref in zip((OUTER, INNER), reversed(to)):
        ref[...] = listed(lists[side : side + 1, :1], out, block)


def inner_kernel(lists, h, out):
    out[...] = listed(lists[INNER : INNER + 1, :1], h[...], out.shape[0])


def keep(parity, a, u, t, inverse, h, t_out, r_out, s_out, h_out):
    rows, edges = h.shape[0], a.shape[0]
    at = slice(parity * rows, (parity + 1) * rows)
    s_out[parity * edges : (parity + 1) * edges, :] = slope(a).astype(BF16)
    t_out[at, :] = t.astype(BF16)
    r_out[at, :] = (inverse * slope(u)).astype(BF16)
    h_out[at, :] = h


def save_kernel(plane, parity, a, u, h, *refs):
    @pl.when(here_is(plane))
    def _():
        u_value = u[...]
        t, inverse = normalize(u_value * jax.nn.sigmoid(u_value))
        keep(parity, a[...], u_value, t, inverse, h[...], *refs[-4:])


def backward_kernel(sides, finish, parity, kept, take, *refs):
    packed, *gains = take
    w_send, _, _, w_fold = quarters(packed)
    gain = jnp.where(here_is(parity=parity), gains[0][...], gains[1][...])
    lists, upstream, *refs = refs[kept:]
    arrived, refs = refs[: len(sides)], refs[len(sides) :]
    t_in, r_in, s_in, gown, ghalo_t, c_out, du_out, da_out, es_out, *done, to_inner, to_outer = refs
    edges = gown.shape[0] // 2
    rows = upstream.shape[0]
    block = to_inner.shape[0]
    at = slice(parity * rows, (parity + 1) * rows)
    at_edges = slice(parity * edges, (parity + 1) * edges)
    c_out[...] = upstream[...].astype(F32)
    for side, ref in zip(sides, arrived):
        if ref.shape == c_out.shape:
            c_out[...] = c_out[...] + ref[...]
        else:
            add_listed(lists[side : side + 1, :1], c_out, ref[...].astype(F32), block)
    if finish:
        done[0][...] = c_out[...].astype(BF16)
    g = c_out[...] * gain
    t = t_in[at, :].astype(F32)
    centre = jnp.mean(g, axis=-1, keepdims=True)
    along = jnp.mean(g * t, axis=-1, keepdims=True)
    du = ((g - centre - t * along) * r_in[at, :].astype(F32)).astype(BF16)
    du_out[...] = du
    spread = mul(gown[edges:, :], du).astype(BF16)
    da = (mul_t(spread, w_fold[...]) * s_in[at_edges, :].astype(F32)).astype(BF16)
    da_out[...] = da
    es = mul_t(da, w_send[...]).astype(BF16)
    es_out[...] = es
    halo = mul(ghalo_t[...], es).astype(BF16)
    to_inner[...] = halo[:block]
    to_outer[...] = halo[block:]


def backward_own_kernel(add_inner, last, take, *refs):
    _, w_recv, w_node, _ = quarters(take[0])
    if last:
        _, _, other, *refs = refs
    if add_inner:
        lists, inner, *refs = refs
    refs, out = (refs[:-2], refs[-2:]) if last else (refs[:-1], refs[-1:])
    *_, c, du, da, es, gown_t = refs
    er = mul_t(da[...], w_recv[...]).astype(BF16)
    both = jnp.concatenate([es[...], er], axis=0)
    total = c[...] + mul_t(du[...], w_node[...]) + mul(gown_t[...], both)
    if add_inner:
        block = inner.shape[0]
        at = lists[INNER : INNER + 1, :1]
        value = inner[...].astype(F32)
        total = total + jnp.concatenate(
            [jnp.where(at == number, value, 0.0) for number in range(total.shape[0] // block)], axis=0
        )
    if last:
        order(total.astype(BF16), other[...], *out)
    else:
        out[0][...] = total.astype(out[0].dtype)


def order(even, odd, first, second):
    zero = lax.axis_index("dom") % 2 == 0

    @pl.when(zero)
    def _():
        first[...] = even
        second[...] = odd

    @pl.when(jnp.logical_not(zero))
    def _():
        first[...] = odd
        second[...] = even


def order_kernel(both, first, second):
    rows = first.shape[0]
    order(both[:rows, :], both[rows:, :], first, second)


def add_kernel(lists, value, outer, other, first, second, total):
    @pl.when(here_is(1))
    def _():
        total[...] = value[...].astype(F32)
        add_listed(lists[OUTER : OUTER + 1, :1], total, outer[...].astype(F32), outer.shape[0])
        order(total[...].astype(BF16), other[...], first, second)


def spread_kernel(lists, outer, out):
    block = outer.shape[0]
    at = lists[OUTER : OUTER + 1, :1]
    value = outer[...].astype(F32)
    for number in range(out.shape[0] // block):
        out[number * block : (number + 1) * block, :] = jnp.where(at == number, value, 0.0)


def place_kernel(lists, outer, flipped, first, second):
    block = outer.shape[0]
    at = lists[OUTER : OUTER + 1, :1]
    for value, out in ((outer, first), (flipped, second)):
        for number in range(out.shape[0] // block):
            covered = jnp.broadcast_to(at == number, value.shape) & here_is(0, 0)
            out[number * block : (number + 1) * block, :] = jnp.where(covered, value[...].astype(F32), 0.0).astype(BF16)


def sum_kernel(*refs):
    ends, placed, totals = (refs[2 * k : 2 * k + 2] for k in range(3))
    for k in range(2):
        totals[k][...] = (ends[k][...].astype(F32) + placed[k][...].astype(F32)).astype(BF16)


def write_kernel(*refs):
    first_home, second_home, totals = (refs[2 * k : 2 * k + 2] for k in range(3))
    out_home, out_grads, sems = refs[6:]
    core = lax.axis_index("pipe") % 2
    slots = core, 1 - core

    def outputs(source):
        return [pltpu.make_async_copy(source[k], out_home.at[0, slots[k]], sems.at[k]) for k in range(2)]

    copies = [pltpu.make_async_copy(totals[k], out_grads.at[0, slots[k]], sems.at[2 + k]) for k in range(2)]
    for copy in copies:
        copy.start()

    @pl.when(here_is(0))
    def _():
        for copy in outputs(first_home):
            copy.start()

    @pl.when(jnp.logical_not(here_is(0)))
    def _():
        for copy in outputs(second_home):
            copy.start()

    for copy in copies + outputs(first_home):
        copy.wait()


def run(kernel, operands, outs, spaces=(), aliases=None, out_spaces=(), scratch=(), cost=1, vmem=12):
    spaces = tuple(spaces) + (pltpu.VMEM,) * (len(operands) - len(spaces))
    operands = [
        pltpu.with_memory_space_constraint(operand, space) if space == pltpu.HBM else operand
        for operand, space in zip(operands, spaces)
    ]
    out_spaces = tuple(out_spaces) + (pltpu.VMEM,) * (len(outs) - len(out_spaces))
    return pl.pallas_call(
        kernel,
        out_shape=[jax.ShapeDtypeStruct(s, t) for s, t in outs],
        in_specs=[pl.BlockSpec(memory_space=space) for space in spaces],
        out_specs=[pl.BlockSpec(memory_space=space) for space in out_spaces],
        scratch_shapes=list(scratch),
        input_output_aliases=aliases or {},
        compiler_params=pltpu.CompilerParams(vmem_limit_bytes=vmem * 2**20),
        cost_estimate=pl.CostEstimate(flops=cost, bytes_accessed=1, transcendentals=0),
    )(*operands)


def run_section(body, plane, matrices, operands, outs, elsewhere=None, aliases=None, cost=1):
    elsewhere = elsewhere or {}

    def kernel(*refs):
        take, rest = refs[: len(matrices)], refs[len(matrices) :]

        @pl.when(here_is(plane))
        def _():
            body(take, *rest)

        if elsewhere:

            @pl.when(jnp.logical_not(here_is(plane)))
            def _():
                for source, target in elsewhere.items():
                    rest[target][...] = rest[source][...]

    aliases = {len(matrices) + source: target for source, target in (aliases or {}).items()}
    return run(kernel, tuple(matrices) + tuple(operands), outs, aliases=aliases, cost=cost)


def shards(
    inputs,
    cotangent,
    w_send,
    w_recv,
    w_message,
    w_node,
    w_aggregate,
    gains,
    edge_send,
    edge_recv,
    edge_count,
    halo_send,
):
    sections = lax.axis_size("pipe")
    pairs_total = lax.axis_size("dom") // 2
    phase = lax.axis_index("pipe")
    y = lax.rem(lax.axis_index("dom"), 2)
    plane_here = phase // 2
    rows, latent = inputs.shape[1:]
    edge_blocks, block = edge_send.shape
    edges = edge_blocks * block

    def send(value, rule):
        table = []
        for z in range(pairs_total):
            for which in range(2):
                for x in range(sections // 2):
                    for c in range(2):
                        if (target := rule(z, which, x, c)) is None:
                            continue
                        tz, ty, tx, tc = target
                        target = (2 * (tz % pairs_total) + ty) * sections + 2 * (tx % (sections // 2)) + tc
                        table.append(((2 * z + which) * sections + 2 * x + c, target))
        return lax.ppermute(value, AXES, table)

    def flip_y(value):
        return send(value, lambda z, y, x, c: (z, 1 - y, x, c))

    def flip_core(value):
        return send(value, lambda z, y, x, c: (z, y, x, 1 - c))

    def go_home(first, second, plane=None):
        return (
            send(first, lambda z, y, x, c: (z, c, x, y) if plane in (None, x) else None),
            send(second, lambda z, y, x, c: (z, c, x, 1 - y) if plane in (None, x) else None),
        )

    def towards(value, side, step):
        if side == INNER:
            return send(value, lambda z, y, x, c: (z, y, x, 1 - c))
        return send(value, lambda z, y, x, c: (z + 2 * c - 1, y, x + step, 1 - c) if x + min(step, 0) >= 0 else None)

    def across(value):
        return send(value, lambda z, y, x, c: (z, y, x + 1, c))

    wide = (rows, latent)
    edge_wide = (edges, latent)
    narrow = (block, latent)
    both_wide = (2 * rows, latent)
    unit = 2 * rows * latent * latent
    dma = pltpu.SemaphoreType.DMA

    here, there, boundary, packed = run(
        prepare_kernel,
        (edge_count, jnp.swapaxes(halo_send, 1, 2), inputs, cotangent, edge_send, edge_recv),
        [(wide, BF16), ((rows + 16, latent), BF16), (narrow, BF16), ((16, block), BF16)],
        spaces=(pltpu.HBM,) * 6,
        scratch=[
            pltpu.SMEM((edge_blocks,), jnp.int32),
            pltpu.SMEM((1, 1, 2), jnp.int32),
            pltpu.VMEM(wide, BF16),
            pltpu.VMEM((2, 8, block), jnp.int32),
            dma((7,)),
        ],
    )
    there = send(there, lambda z, y, x, c: (z, 1 - y, x, c) if c == y else (z, y, x, 1 - c))
    outer = send(boundary, lambda z, y, x, c: (z + 2 * y - 1, c, x, 1 - y))
    gown, gown_t, ghalo, ghalo_t, lists, home_lists = run(
        functools.partial(graph_kernel, edge_blocks),
        (packed, there),
        [
            ((2 * edges, rows), BF16),
            ((rows, 2 * edges), BF16),
            ((edges, 2 * block), BF16),
            ((2 * block, edges), BF16),
            ((2, block), jnp.int32),
            ((2, block), jnp.int32),
        ],
    )
    hidden, inner = run(entry_kernel, (here, there, outer, lists), [(wide, BF16), (narrow, BF16)], cost=LONG * 3 // 2)
    inner = towards(inner, INNER, 0)

    [weights] = run(
        weights_kernel,
        (w_send[0], w_recv[0], w_node[0], w_message[0], w_aggregate[0]),
        [((4 * latent, latent), BF16)],
        spaces=(pltpu.HBM,) * 5,
        scratch=[pltpu.VMEM((2, latent, latent), BF16), dma((5,))],
    )
    pair = run(place_mine_kernel, (weights,), [((4 * latent, latent), BF16)] * 2)
    matrices = run(
        place_swapped_kernel, (flip_core(weights), hidden, *pair), [((4 * latent, latent), BF16)] * 2, aliases={2: 0, 3: 1}
    )
    both_gains = (gains, flip_core(gains))
    upstream = hidden

    saved = ()
    arrived = ()
    for tick in range(sections):
        plane, parity = tick // 2, tick % 2
        packed = matrices[parity]
        a_own, u_own = run_section(
            forward_own_kernel, plane, (packed,), (hidden, gown) + arrived, [(edge_wide, F32), (wide, F32)], cost=BESIDE
        )
        if tick == sections - 1:
            outputs, a_own = lax.optimization_barrier((saved[3], a_own))
            first_home = go_home(*run(order_kernel, (outputs,), [(wide, BF16)] * 2), plane=0)
        step = (tick + 1) // 2 - plane if tick < sections - 1 else None
        to_send = [(narrow, BF16)] * {0: 2, 1: 1, None: 0}[step]
        last = tick == sections - 1
        state = [(both_wide, BF16), (both_wide, BF16), ((2 * edges, latent), BF16), (both_wide, BF16)]
        made = run_section(
            functools.partial(forward_kernel, parity, last),
            plane,
            (packed, *both_gains),
            (lists, hidden, a_own, u_own, inner, outer, ghalo, gown_t) + (tuple(saved) if last else ()),
            state if last else [(wide, BF16), (edge_wide, F32), (wide, F32)] + to_send,
            aliases={8 + k: k for k in range(4)} if last else None,
            cost=BESIDE // 2 if last else 1,
        )
        if last:
            saved = made
            break
        hidden, a, u, *to = made
        produced = hidden
        if step == 0:
            outer = towards(to[-1], OUTER, step)
            inner = towards(to[0], INNER, step)
            arrived = (inner,)
        elif step:
            hidden = across(hidden)
            inner = towards(*run(inner_kernel, (lists, hidden), [(narrow, BF16)]), INNER, 0)
            arrived = ()
        saved = run(
            functools.partial(save_kernel, plane, parity),
            (a, u, produced) + tuple(saved),
            state,
            aliases={3 + k: k for k in range(4)} if saved else None,
            cost=1 if step else BESIDE,
        )
        if step:
            to_outer, *saved = lax.optimization_barrier((to[-1], *saved))
            outer = towards(to_outer, OUTER, step)

    *states, both = saved
    halos = {}
    finished = {}
    second_home = ()
    for tick in range(sections - 1, -1, -1):
        plane, parity = tick // 2, tick % 2
        packed = matrices[parity]
        step = (tick - 1) // 2 - plane if tick else 0
        finish = bool(halos) and tick % 2 == 0
        outs = [(wide, F32), (wide, BF16), (edge_wide, BF16), (edge_wide, BF16)]
        outs += [(wide, BF16)] if finish else []
        outs += [(narrow, BF16)] * 2
        kept = (to_outer,) if tick == 1 else ()
        c, du, da, es, *done, to_inner, to_outer = run_section(
            functools.partial(backward_kernel, tuple(halos), finish, parity, len(kept)),
            plane,
            (packed, *both_gains),
            kept + (lists, upstream) + tuple(halos.values()) + tuple(states) + (gown, ghalo_t),
            outs,
            elsewhere={0: -1} if tick == 1 else {},
            cost=1 if tick else BESIDE // 2,
        )
        if done:
            finished[tick + 1] = done[0]
        inner = towards(to_inner, INNER, 0)
        halos = {OUTER: towards(to_outer, OUTER, step)} if tick else {}
        add_inner = tick == 0 or step != 0
        last = tuple(ends) + (finished[1],) if tick == 0 else ()
        beside = (lists, inner) if add_inner else (inner,)
        upstream, *rest = run_section(
            functools.partial(backward_own_kernel, add_inner, bool(last)),
            plane,
            (packed,),
            last + beside + tuple({sections - 1: first_home, 0: second_home}.get(tick, ())) + (c, du, da, es, gown_t),
            [(wide, BF16)] * 2 if last else [(wide, BF16 if step else F32)],
            elsewhere={0: -2, 1: -1} if last else {},
            cost=BESIDE if tick else 1,
        )
        if not add_inner:
            halos = {INNER: inner, **halos}
        if step:
            own = upstream
            upstream = across(upstream)
            halos = {OUTER: run(spread_kernel, (lists, halos[OUTER]), [(wide, F32)], cost=LONG)[0]}
        elif tick == 1:
            outputs, upstream = lax.optimization_barrier((both, upstream))
            second_home = go_home(*run(order_kernel, (outputs,), [(wide, BF16)] * 2), plane=1)
            ends = run(
                add_kernel,
                (lists, own, halos[OUTER], finished[3]),
                [(wide, BF16)] * 2,
                scratch=[pltpu.VMEM(wide, F32)],
            )

    final_outer = send(to_outer, lambda z, y, x, c: (z + 2 * c - 1, 1 - c, x, y))
    ends = go_home(upstream, *rest)
    placed = run(
        place_kernel, (home_lists, final_outer, flip_core(final_outer)), [(wide, BF16)] * 2
    )
    totals = run(sum_kernel, tuple(ends) + tuple(placed), [(wide, BF16)] * 2, cost=LONG)
    return tuple(
        run(
            write_kernel,
            tuple(first_home) + tuple(second_home) + tuple(totals),
            [((1, 2) + wide, BF16)] * 2,
            out_spaces=(pltpu.HBM,) * 2,
            scratch=[dma((4,))],
        )
    )


def solution(mesh):
    in_specs = (
        P(None, "dom", None),
        P(None, "dom", None),
        P("pipe", None, None),
        P("pipe", None, None),
        P("pipe", None, None),
        P("pipe", None, None),
        P("pipe", None, None),
        P("pipe", None),
        P("dom", None),
        P("dom", None),
        P("dom"),
        P("dom", None, None),
    )
    out_specs = (P("pipe", None, "dom", None), P("pipe", None, "dom", None))
    return jax.shard_map(shards, mesh=mesh, in_specs=in_specs, out_specs=out_specs, check_vma=False)
```

```python
import functools

import jax
import jax.numpy as jnp
from jax import lax
from jax.experimental import pallas as pl
from jax.experimental.pallas import tpu as pltpu
from jax.sharding import PartitionSpec as P

EPSILON = 1e-05
F32 = jnp.float32
BF16 = jnp.bfloat16
AXES = ("dom", "pipe")
INNER, OUTER = 0, 1
BESIDE = 2 * 10**9
LONG = 2 * 10**10


def mul(a, b):
    return jnp.dot(a, b, preferred_element_type=F32)


def mul_t(a, b):
    return lax.dot_general(a, b, (((1,), (1,)), ((), ())), preferred_element_type=F32)


def slope(v):
    s = jax.nn.sigmoid(v)
    return s * (1.0 + v * (1.0 - s))


def normalize(z):
    centred = z - jnp.mean(z, axis=-1, keepdims=True)
    inverse = lax.rsqrt(jnp.mean(centred * centred, axis=-1, keepdims=True) + EPSILON)
    return centred * inverse, inverse


def quarters(packed):
    depth = packed.shape[0] // 4
    return [packed.at[pl.ds(number * depth, depth), :] for number in range(4)]


def here_is(plane=None, parity=None):
    pipe = lax.axis_index("pipe")
    wanted = jnp.bool_(True)
    if plane is not None:
        wanted = pipe // 2 == plane
    if parity is not None:
        wanted = wanted & (pipe % 2 == parity)
    return wanted


def is_local():
    return lax.axis_index("pipe") % 2 == lax.axis_index("dom") % 2


def listed(at, value, block):
    picked = value[:block]
    for number in range(1, value.shape[0] // block):
        picked = jnp.where(at == number, value[number * block : (number + 1) * block], picked)
    return picked


def add_listed(at, target, value, block):
    for number in range(target.shape[0] // block):
        rows = slice(number * block, (number + 1) * block)
        target[rows, :] = target[rows, :] + jnp.where(at == number, value, 0.0)


def encode(values):
    high = lax.shift_right_logical(values, 4)
    low = values - high * 16
    return jnp.concatenate([high.astype(F32), low.astype(F32)], axis=0).astype(BF16)


def decode(tile):
    half = tile.shape[0] // 2
    tile = tile.astype(F32)
    return (tile[:half] * 16.0 + tile[half:]).astype(jnp.int32)


def prepare_kernel(
    count_in,
    halo_in,
    inputs,
    cotangent,
    send_in,
    recv_in,
    here,
    there,
    boundary,
    packed,
    count,
    halo,
    blocks,
    edges,
    sems,
):
    micro = lax.axis_index("dom") % 2
    block = boundary.shape[0]
    edge_blocks = send_in.shape[0]
    rows = here.shape[0]
    lists = [
        pltpu.make_async_copy(halo_in, halo, sems.at[0]),
        pltpu.make_async_copy(count_in, count, sems.at[1]),
    ]
    ids = [
        pltpu.make_async_copy(ref, edges.at[k, pl.ds(0, edge_blocks), :], sems.at[2 + k])
        for k, ref in enumerate((send_in, recv_in))
    ]
    def fetch(source):
        return [
            pltpu.make_async_copy(source.at[1 - micro], there.at[pl.ds(0, rows), :], sems.at[4]),
            pltpu.make_async_copy(source.at[micro], here, sems.at[5]),
        ]

    whole = pltpu.make_async_copy(inputs.at[lax.axis_index("pipe") % 2], blocks, sems.at[6])

    for copy in lists + ids:
        copy.start()

    @pl.when(here_is(0))
    def _():
        for copy in fetch(inputs):
            copy.start()

    @pl.when(jnp.logical_not(here_is(0)))
    def _():
        for copy in fetch(cotangent):
            copy.start()

    whole.start()
    for copy in lists:
        copy.wait()
    number = jnp.where(micro == 1, halo[0, 0, 0], halo[0, 0, 1])
    for copy in ids:
        copy.wait()
    lane = lax.broadcasted_iota(jnp.int32, (1, block), 1)
    tail = jnp.where(lane == 0, halo[0, 0, 0], jnp.where(lane == 1, halo[0, 0, 1], 0))
    for place in range(edge_blocks):
        tail = jnp.where(lane == 2 + place, count[place], tail)
    spare = jnp.zeros((7 - 2 * edge_blocks, block), jnp.int32)
    tile = encode(jnp.concatenate([edges[0, :edge_blocks, :], edges[1, :edge_blocks, :], tail, spare], axis=0))
    packed[...] = tile
    there[rows:, :] = jnp.zeros((there.shape[0] - rows, there.shape[1]), BF16)
    there[rows:, :block] = tile
    for copy in fetch(inputs):
        copy.wait()
    whole.wait()
    boundary[...] = blocks[pl.ds(pl.multiple_of(number * block, block), block), :]


def weights_kernel(w_send, w_recv, w_node, w_message, w_aggregate, out, factors, sems):
    depth = w_send.shape[0]
    copies = [pltpu.make_async_copy(ref, factors.at[k], sems.at[k]) for k, ref in enumerate((w_message, w_aggregate))]
    copies += [
        pltpu.make_async_copy(ref, out.at[pl.ds(k * depth, depth), :], sems.at[2 + k])
        for k, ref in enumerate((w_send, w_recv, w_node))
    ]
    for copy in copies:
        copy.start()
    for copy in copies[:2]:
        copy.wait()
    out[3 * depth :, :] = mul(factors[0], factors[1]).astype(BF16)
    for copy in copies[2:]:
        copy.wait()


def place_mine_kernel(mine, even, odd):
    @pl.when(here_is(parity=0))
    def _():
        even[...] = mine[...]

    @pl.when(here_is(parity=1))
    def _():
        odd[...] = mine[...]


def place_swapped_kernel(swapped, _, even_in, odd_in, even, odd):
    del even_in, odd_in

    @pl.when(here_is(parity=0))
    def _():
        odd[...] = swapped[...]

    @pl.when(here_is(parity=1))
    def _():
        even[...] = swapped[...]


def graph_kernel(edge_blocks, packed, there, gown, gown_t, ghalo, ghalo_t, lists, home_lists):
    block = packed.shape[1]
    rows = gown_t.shape[0]
    edges = edge_blocks * block
    local = is_local()
    first_core = lax.axis_index("pipe") % 2 == 0
    last = 2 * edge_blocks
    tiles = decode(packed[...]), decode(there[rows:, :block])
    mine = jnp.where(local, *tiles)
    tails = [tile[last : last + 1] for tile in (mine, tiles[0])]
    lane = lax.broadcasted_iota(jnp.int32, (1, block), 1)
    row = lax.broadcasted_iota(jnp.int32, (rows, block), 0)
    halo_row = lax.broadcasted_iota(jnp.int32, (2 * block, block), 0)
    for number in range(edge_blocks):
        live = lane < tails[0][:, 2 + number : 3 + number]
        sender = jnp.where(live, mine[number : number + 1], -1)
        receiver = jnp.where(live, mine[edge_blocks + number : edge_blocks + number + 1], -1)
        outside = sender - rows
        turned = jnp.where(outside < block, outside + block, outside - block)
        outside = jnp.where(outside >= 0, jnp.where(first_core, turned, outside), -1)
        here = slice(number * block, (number + 1) * block)
        received = slice(edges + number * block, edges + (number + 1) * block)
        for index, at, table, table_t in (
            (sender, here, gown, gown_t),
            (receiver, received, gown, gown_t),
            (outside, here, ghalo, ghalo_t),
        ):
            hot = (index == (halo_row if table is ghalo else row)).astype(F32)
            table_t[:, at] = hot.astype(BF16)
            table[at, :] = hot.T.astype(BF16)

    def whole(tail, place):
        return jnp.broadcast_to(tail[:1, place : place + 1], (1, block))

    to_next, to_prev = whole(tails[0], 0), whole(tails[0], 1)
    lists[0:1, :] = jnp.where(first_core, to_next, to_prev)
    lists[1:2, :] = jnp.where(first_core, to_prev, to_next)
    to_next, to_prev = whole(tails[1], 0), whole(tails[1], 1)
    home_first = lax.axis_index("dom") % 2 == 0
    home_lists[0:1, :] = jnp.where(home_first, to_next, to_prev)
    home_lists[1:2, :] = jnp.where(home_first, to_prev, to_next)


def entry_kernel(here, there, _, lists, hidden, to_inner):
    @pl.when(is_local())
    def _():
        hidden[...] = here[...]

    @pl.when(jnp.logical_not(is_local()))
    def _():
        hidden[...] = there[: hidden.shape[0], :]

    to_inner[...] = listed(lists[INNER : INNER + 1, :1], hidden[...], to_inner.shape[0])


def forward_own_kernel(take, h, gown, *refs):
    w_send, w_recv, w_node, _ = quarters(take[0])
    a_out, u_out = refs[-2:]
    edges = gown.shape[0] // 2
    own = mul(gown[...], h[...]).astype(BF16)
    a_out[...] = mul(own[:edges], w_send[...]) + mul(own[edges:], w_recv[...])
    u_out[...] = mul(h[...], w_node[...])


def forward_kernel(parity, last, take, lists, h, a_own, u_own, inner, outer, ghalo, gown_t, *refs):
    packed, *gains = take
    w_send, _, _, w_fold = quarters(packed)
    gain = jnp.where(here_is(parity=parity), gains[0][...], gains[1][...])
    edges = ghalo.shape[0]
    block = inner.shape[0]
    halo = mul(ghalo[...], jnp.concatenate([inner[...], outer[...]], axis=0)).astype(BF16)
    a = a_own[...] + mul(halo, w_send[...])
    q = (a * jax.nn.sigmoid(a)).astype(BF16)
    u = u_own[...] + mul(mul(gown_t[:, edges:], q).astype(BF16), w_fold[...])
    t, inverse = normalize(u * jax.nn.sigmoid(u))
    out = (h[...].astype(F32) + t * gain).astype(BF16)
    if last:
        keep(parity, a, u, t, inverse, out, *refs[-4:])
        return
    h_out, a_out, u_out, *to = refs
    a_out[...] = a
    u_out[...] = u
    h_out[...] = out
    for side, ref in zip((OUTER, INNER), reversed(to)):
        ref[...] = listed(lists[side : side + 1, :1], out, block)


def inner_kernel(lists, h, out):
    out[...] = listed(lists[INNER : INNER + 1, :1], h[...], out.shape[0])


def keep(parity, a, u, t, inverse, h, t_out, r_out, s_out, h_out):
    rows, edges = h.shape[0], a.shape[0]
    at = slice(parity * rows, (parity + 1) * rows)
    s_out[parity * edges : (parity + 1) * edges, :] = slope(a).astype(BF16)
    t_out[at, :] = t.astype(BF16)
    r_out[at, :] = (inverse * slope(u)).astype(BF16)
    h_out[at, :] = h


def save_kernel(plane, parity, a, u, h, *refs):
    @pl.when(here_is(plane))
    def _():
        u_value = u[...]
        t, inverse = normalize(u_value * jax.nn.sigmoid(u_value))
        keep(parity, a[...], u_value, t, inverse, h[...], *refs[-4:])


def backward_kernel(sides, finish, parity, kept, take, *refs):
    packed, *gains = take
    w_send, _, _, w_fold = quarters(packed)
    gain = jnp.where(here_is(parity=parity), gains[0][...], gains[1][...])
    lists, upstream, *refs = refs[kept:]
    arrived, refs = refs[: len(sides)], refs[len(sides) :]
    t_in, r_in, s_in, gown, ghalo_t, c_out, du_out, da_out, es_out, *done, to_inner, to_outer = refs
    edges = gown.shape[0] // 2
    rows = upstream.shape[0]
    block = to_inner.shape[0]
    at = slice(parity * rows, (parity + 1) * rows)
    at_edges = slice(parity * edges, (parity + 1) * edges)
    c_out[...] = upstream[...].astype(F32)
    for side, ref in zip(sides, arrived):
        if ref.shape == c_out.shape:
            c_out[...] = c_out[...] + ref[...]
        else:
            add_listed(lists[side : side + 1, :1], c_out, ref[...].astype(F32), block)
    if finish:
        done[0][...] = c_out[...].astype(BF16)
    g = c_out[...] * gain
    t = t_in[at, :].astype(F32)
    centre = jnp.mean(g, axis=-1, keepdims=True)
    along = jnp.mean(g * t, axis=-1, keepdims=True)
    du = ((g - centre - t * along) * r_in[at, :].astype(F32)).astype(BF16)
    du_out[...] = du
    spread = mul(gown[edges:, :], du).astype(BF16)
    da = (mul_t(spread, w_fold[...]) * s_in[at_edges, :].astype(F32)).astype(BF16)
    da_out[...] = da
    es = mul_t(da, w_send[...]).astype(BF16)
    es_out[...] = es
    halo = mul(ghalo_t[...], es).astype(BF16)
    to_inner[...] = halo[:block]
    to_outer[...] = halo[block:]


def backward_own_kernel(add_inner, last, take, *refs):
    _, w_recv, w_node, _ = quarters(take[0])
    if last:
        _, _, other, *refs = refs
    if add_inner:
        lists, inner, *refs = refs
    refs, out = (refs[:-2], refs[-2:]) if last else (refs[:-1], refs[-1:])
    *_, c, du, da, es, gown_t = refs
    er = mul_t(da[...], w_recv[...]).astype(BF16)
    both = jnp.concatenate([es[...], er], axis=0)
    total = c[...] + mul_t(du[...], w_node[...]) + mul(gown_t[...], both)
    if add_inner:
        block = inner.shape[0]
        at = lists[INNER : INNER + 1, :1]
        value = inner[...].astype(F32)
        total = total + jnp.concatenate(
            [jnp.where(at == number, value, 0.0) for number in range(total.shape[0] // block)], axis=0
        )
    if last:
        order(total.astype(BF16), other[...], *out)
    else:
        out[0][...] = total.astype(out[0].dtype)


def order(even, odd, first, second):
    zero = lax.axis_index("dom") % 2 == 0

    @pl.when(zero)
    def _():
        first[...] = even
        second[...] = odd

    @pl.when(jnp.logical_not(zero))
    def _():
        first[...] = odd
        second[...] = even


def order_kernel(both, first, second):
    rows = first.shape[0]
    order(both[:rows, :], both[rows:, :], first, second)


def add_kernel(lists, value, outer, other, first, second, total):
    @pl.when(here_is(1))
    def _():
        total[...] = value[...].astype(F32)
        add_listed(lists[OUTER : OUTER + 1, :1], total, outer[...].astype(F32), outer.shape[0])
        order(total[...].astype(BF16), other[...], first, second)


def spread_kernel(lists, outer, out):
    block = outer.shape[0]
    at = lists[OUTER : OUTER + 1, :1]
    value = outer[...].astype(F32)
    for number in range(out.shape[0] // block):
        out[number * block : (number + 1) * block, :] = jnp.where(at == number, value, 0.0)


def place_kernel(lists, outer, flipped, first, second):
    block = outer.shape[0]
    at = lists[OUTER : OUTER + 1, :1]
    for value, out in ((outer, first), (flipped, second)):
        for number in range(out.shape[0] // block):
            covered = jnp.broadcast_to(at == number, value.shape) & here_is(0, 0)
            out[number * block : (number + 1) * block, :] = jnp.where(covered, value[...].astype(F32), 0.0).astype(BF16)


def sum_kernel(*refs):
    ends, placed, totals = (refs[2 * k : 2 * k + 2] for k in range(3))
    for k in range(2):
        totals[k][...] = (ends[k][...].astype(F32) + placed[k][...].astype(F32)).astype(BF16)


def write_kernel(*refs):
    first_home, second_home, totals = (refs[2 * k : 2 * k + 2] for k in range(3))
    out_home, out_grads, sems = refs[6:]
    core = lax.axis_index("pipe") % 2
    slots = core, 1 - core

    def outputs(source):
        return [pltpu.make_async_copy(source[k], out_home.at[0, slots[k]], sems.at[k]) for k in range(2)]

    copies = [pltpu.make_async_copy(totals[k], out_grads.at[0, slots[k]], sems.at[2 + k]) for k in range(2)]
    for copy in copies:
        copy.start()

    @pl.when(here_is(0))
    def _():
        for copy in outputs(first_home):
            copy.start()

    @pl.when(jnp.logical_not(here_is(0)))
    def _():
        for copy in outputs(second_home):
            copy.start()

    for copy in copies + outputs(first_home):
        copy.wait()


def run(kernel, operands, outs, spaces=(), aliases=None, out_spaces=(), scratch=(), cost=1, vmem=12):
    spaces = tuple(spaces) + (pltpu.VMEM,) * (len(operands) - len(spaces))
    operands = [
        pltpu.with_memory_space_constraint(operand, space) if space == pltpu.HBM else operand
        for operand, space in zip(operands, spaces)
    ]
    out_spaces = tuple(out_spaces) + (pltpu.VMEM,) * (len(outs) - len(out_spaces))
    return pl.pallas_call(
        kernel,
        out_shape=[jax.ShapeDtypeStruct(s, t) for s, t in outs],
        in_specs=[pl.BlockSpec(memory_space=space) for space in spaces],
        out_specs=[pl.BlockSpec(memory_space=space) for space in out_spaces],
        scratch_shapes=list(scratch),
        input_output_aliases=aliases or {},
        compiler_params=pltpu.CompilerParams(vmem_limit_bytes=vmem * 2**20),
        cost_estimate=pl.CostEstimate(flops=cost, bytes_accessed=1, transcendentals=0),
    )(*operands)


def run_section(body, plane, matrices, operands, outs, elsewhere=None, aliases=None, cost=1):
    elsewhere = elsewhere or {}

    def kernel(*refs):
        take, rest = refs[: len(matrices)], refs[len(matrices) :]

        @pl.when(here_is(plane))
        def _():
            body(take, *rest)

        if elsewhere:

            @pl.when(jnp.logical_not(here_is(plane)))
            def _():
                for source, target in elsewhere.items():
                    rest[target][...] = rest[source][...]

    aliases = {len(matrices) + source: target for source, target in (aliases or {}).items()}
    return run(kernel, tuple(matrices) + tuple(operands), outs, aliases=aliases, cost=cost)


def shards(
    inputs,
    cotangent,
    w_send,
    w_recv,
    w_message,
    w_node,
    w_aggregate,
    gains,
    edge_send,
    edge_recv,
    edge_count,
    halo_send,
):
    sections = lax.axis_size("pipe")
    pairs_total = lax.axis_size("dom") // 2
    phase = lax.axis_index("pipe")
    y = lax.rem(lax.axis_index("dom"), 2)
    plane_here = phase // 2
    rows, latent = inputs.shape[1:]
    edge_blocks, block = edge_send.shape
    edges = edge_blocks * block

    def send(value, rule):
        table = []
        for z in range(pairs_total):
            for which in range(2):
                for x in range(sections // 2):
                    for c in range(2):
                        if (target := rule(z, which, x, c)) is None:
                            continue
                        tz, ty, tx, tc = target
                        target = (2 * (tz % pairs_total) + ty) * sections + 2 * (tx % (sections // 2)) + tc
                        table.append(((2 * z + which) * sections + 2 * x + c, target))
        return lax.ppermute(value, AXES, table)

    def flip_y(value):
        return send(value, lambda z, y, x, c: (z, 1 - y, x, c))

    def flip_core(value):
        return send(value, lambda z, y, x, c: (z, y, x, 1 - c))

    def go_home(first, second, plane=None):
        return (
            send(first, lambda z, y, x, c: (z, c, x, y) if plane in (None, x) else None),
            send(second, lambda z, y, x, c: (z, c, x, 1 - y) if plane in (None, x) else None),
        )

    def towards(value, side, step):
        if side == INNER:
            return send(value, lambda z, y, x, c: (z, y, x, 1 - c))
        return send(value, lambda z, y, x, c: (z + 2 * c - 1, y, x + step, 1 - c) if x + min(step, 0) >= 0 else None)

    def across(value):
        return send(value, lambda z, y, x, c: (z, y, x + 1, c))

    wide = (rows, latent)
    edge_wide = (edges, latent)
    narrow = (block, latent)
    both_wide = (2 * rows, latent)
    unit = 2 * rows * latent * latent
    dma = pltpu.SemaphoreType.DMA

    here, there, boundary, packed = run(
        prepare_kernel,
        (edge_count, jnp.swapaxes(halo_send, 1, 2), inputs, cotangent, edge_send, edge_recv),
        [(wide, BF16), ((rows + 16, latent), BF16), (narrow, BF16), ((16, block), BF16)],
        spaces=(pltpu.HBM,) * 6,
        scratch=[
            pltpu.SMEM((edge_blocks,), jnp.int32),
            pltpu.SMEM((1, 1, 2), jnp.int32),
            pltpu.VMEM(wide, BF16),
            pltpu.VMEM((2, 8, block), jnp.int32),
            dma((7,)),
        ],
    )
    there = send(there, lambda z, y, x, c: (z, 1 - y, x, c) if c == y else (z, y, x, 1 - c))
    outer = send(boundary, lambda z, y, x, c: (z + 2 * y - 1, c, x, 1 - y))
    gown, gown_t, ghalo, ghalo_t, lists, home_lists = run(
        functools.partial(graph_kernel, edge_blocks),
        (packed, there),
        [
            ((2 * edges, rows), BF16),
            ((rows, 2 * edges), BF16),
            ((edges, 2 * block), BF16),
            ((2 * block, edges), BF16),
            ((2, block), jnp.int32),
            ((2, block), jnp.int32),
        ],
    )
    hidden, inner = run(entry_kernel, (here, there, outer, lists), [(wide, BF16), (narrow, BF16)], cost=LONG * 3 // 2)
    inner = towards(inner, INNER, 0)

    [weights] = run(
        weights_kernel,
        (w_send[0], w_recv[0], w_node[0], w_message[0], w_aggregate[0]),
        [((4 * latent, latent), BF16)],
        spaces=(pltpu.HBM,) * 5,
        scratch=[pltpu.VMEM((2, latent, latent), BF16), dma((5,))],
    )
    pair = run(place_mine_kernel, (weights,), [((4 * latent, latent), BF16)] * 2)
    matrices = run(
        place_swapped_kernel, (flip_core(weights), hidden, *pair), [((4 * latent, latent), BF16)] * 2, aliases={2: 0, 3: 1}
    )
    both_gains = (gains, flip_core(gains))
    upstream = hidden

    saved = ()
    arrived = ()
    for tick in range(sections):
        plane, parity = tick // 2, tick % 2
        packed = matrices[parity]
        a_own, u_own = run_section(
            forward_own_kernel, plane, (packed,), (hidden, gown) + arrived, [(edge_wide, F32), (wide, F32)], cost=BESIDE
        )
        if tick == sections - 1:
            outputs, a_own = lax.optimization_barrier((saved[3], a_own))
            first_home = go_home(*run(order_kernel, (outputs,), [(wide, BF16)] * 2), plane=0)
        step = (tick + 1) // 2 - plane if tick < sections - 1 else None
        to_send = [(narrow, BF16)] * {0: 2, 1: 1, None: 0}[step]
        last = tick == sections - 1
        state = [(both_wide, BF16), (both_wide, BF16), ((2 * edges, latent), BF16), (both_wide, BF16)]
        made = run_section(
            functools.partial(forward_kernel, parity, last),
            plane,
            (packed, *both_gains),
            (lists, hidden, a_own, u_own, inner, outer, ghalo, gown_t) + (tuple(saved) if last else ()),
            state if last else [(wide, BF16), (edge_wide, F32), (wide, F32)] + to_send,
            aliases={8 + k: k for k in range(4)} if last else None,
            cost=BESIDE // 2 if last else 1,
        )
        if last:
            saved = made
            break
        hidden, a, u, *to = made
        produced = hidden
        if step == 0:
            outer = towards(to[-1], OUTER, step)
            inner = towards(to[0], INNER, step)
            arrived = (inner,)
        elif step:
            hidden = across(hidden)
            inner = towards(*run(inner_kernel, (lists, hidden), [(narrow, BF16)]), INNER, 0)
            arrived = ()
        saved = run(
            functools.partial(save_kernel, plane, parity),
            (a, u, produced) + tuple(saved),
            state,
            aliases={3 + k: k for k in range(4)} if saved else None,
            cost=1 if step else BESIDE,
        )
        if step:
            to_outer, *saved = lax.optimization_barrier((to[-1], *saved))
            outer = towards(to_outer, OUTER, step)

    *states, both = saved
    halos = {}
    finished = {}
    second_home = ()
    for tick in range(sections - 1, -1, -1):
        plane, parity = tick // 2, tick % 2
        packed = matrices[parity]
        step = (tick - 1) // 2 - plane if tick else 0
        finish = bool(halos) and tick % 2 == 0
        outs = [(wide, F32), (wide, BF16), (edge_wide, BF16), (edge_wide, BF16)]
        outs += [(wide, BF16)] if finish else []
        outs += [(narrow, BF16)] * 2
        kept = (to_outer,) if tick == 1 else ()
        c, du, da, es, *done, to_inner, to_outer = run_section(
            functools.partial(backward_kernel, tuple(halos), finish, parity, len(kept)),
            plane,
            (packed, *both_gains),
            kept + (lists, upstream) + tuple(halos.values()) + tuple(states) + (gown, ghalo_t),
            outs,
            elsewhere={0: -1} if tick == 1 else {},
            cost=1 if tick else BESIDE // 2,
        )
        if done:
            finished[tick + 1] = done[0]
        inner = towards(to_inner, INNER, 0)
        halos = {OUTER: towards(to_outer, OUTER, step)} if tick else {}
        add_inner = tick == 0 or step != 0
        last = tuple(ends) + (finished[1],) if tick == 0 else ()
        beside = (lists, inner) if add_inner else (inner,)
        upstream, *rest = run_section(
            functools.partial(backward_own_kernel, add_inner, bool(last)),
            plane,
            (packed,),
            last + beside + tuple({sections - 1: first_home, 0: second_home}.get(tick, ())) + (c, du, da, es, gown_t),
            [(wide, BF16)] * 2 if last else [(wide, BF16 if step else F32)],
            elsewhere={0: -2, 1: -1} if last else {},
            cost=BESIDE if tick else 1,
        )
        if not add_inner:
            halos = {INNER: inner, **halos}
        if step:
            own = upstream
            upstream = across(upstream)
            halos = {OUTER: run(spread_kernel, (lists, halos[OUTER]), [(wide, F32)], cost=LONG)[0]}
        elif tick == 1:
            outputs, upstream = lax.optimization_barrier((both, upstream))
            second_home = go_home(*run(order_kernel, (outputs,), [(wide, BF16)] * 2), plane=1)
            ends = run(
                add_kernel,
                (lists, own, halos[OUTER], finished[3]),
                [(wide, BF16)] * 2,
                scratch=[pltpu.VMEM(wide, F32)],
            )

    final_outer = send(to_outer, lambda z, y, x, c: (z + 2 * c - 1, 1 - c, x, y))
    ends = go_home(upstream, *rest)
    placed = run(
        place_kernel, (home_lists, final_outer, flip_core(final_outer)), [(wide, BF16)] * 2
    )
    totals = run(sum_kernel, tuple(ends) + tuple(placed), [(wide, BF16)] * 2, cost=LONG)
    return tuple(
        run(
            write_kernel,
            tuple(first_home) + tuple(second_home) + tuple(totals),
            [((1, 2) + wide, BF16)] * 2,
            out_spaces=(pltpu.HBM,) * 2,
            scratch=[dma((4,))],
        )
    )


def solution(mesh):
    in_specs = (
        P(None, "dom", None),
        P(None, "dom", None),
        P("pipe", None, None),
        P("pipe", None, None),
        P("pipe", None, None),
        P("pipe", None, None),
        P("pipe", None, None),
        P("pipe", None),
        P("dom", None),
        P("dom", None),
        P("dom"),
        P("dom", None, None),
    )
    out_specs = (P("pipe", None, "dom", None), P("pipe", None, "dom", None))
    return jax.shard_map(shards, mesh=mesh, in_specs=in_specs, out_specs=out_specs, check_vma=False)
```

```python
import functools

import jax
import jax.numpy as jnp
from jax import lax
from jax.experimental import pallas as pl
from jax.experimental.pallas import tpu as pltpu
from jax.sharding import PartitionSpec as P

EPSILON = 1e-05
F32 = jnp.float32
BF16 = jnp.bfloat16
AXES = ("dom", "pipe")
INNER, OUTER = 0, 1
BESIDE = 2 * 10**9
LONG = 2 * 10**10


def mul(a, b):
    return jnp.dot(a, b, preferred_element_type=F32)


def mul_t(a, b):
    return lax.dot_general(a, b, (((1,), (1,)), ((), ())), preferred_element_type=F32)


def slope(v):
    s = jax.nn.sigmoid(v)
    return s * (1.0 + v * (1.0 - s))


def normalize(z):
    centred = z - jnp.mean(z, axis=-1, keepdims=True)
    inverse = lax.rsqrt(jnp.mean(centred * centred, axis=-1, keepdims=True) + EPSILON)
    return centred * inverse, inverse


def quarters(packed):
    depth = packed.shape[0] // 4
    return [packed.at[pl.ds(number * depth, depth), :] for number in range(4)]


def here_is(plane=None, parity=None):
    pipe = lax.axis_index("pipe")
    wanted = jnp.bool_(True)
    if plane is not None:
        wanted = pipe // 2 == plane
    if parity is not None:
        wanted = wanted & (pipe % 2 == parity)
    return wanted


def is_local():
    return lax.axis_index("pipe") % 2 == lax.axis_index("dom") % 2


def listed(at, value, block):
    picked = value[:block]
    for number in range(1, value.shape[0] // block):
        picked = jnp.where(at == number, value[number * block : (number + 1) * block], picked)
    return picked


def add_listed(at, target, value, block):
    for number in range(target.shape[0] // block):
        rows = slice(number * block, (number + 1) * block)
        target[rows, :] = target[rows, :] + jnp.where(at == number, value, 0.0)


def encode(values):
    high = lax.shift_right_logical(values, 4)
    low = values - high * 16
    return jnp.concatenate([high.astype(F32), low.astype(F32)], axis=0).astype(BF16)


def decode(tile):
    half = tile.shape[0] // 2
    tile = tile.astype(F32)
    return (tile[:half] * 16.0 + tile[half:]).astype(jnp.int32)


def prepare_kernel(
    count_in,
    halo_in,
    inputs,
    cotangent,
    send_in,
    recv_in,
    here,
    there,
    boundary,
    packed,
    count,
    halo,
    blocks,
    edges,
    sems,
):
    micro = lax.axis_index("dom") % 2
    block = boundary.shape[0]
    edge_blocks = send_in.shape[0]
    rows = here.shape[0]
    lists = [
        pltpu.make_async_copy(halo_in, halo, sems.at[0]),
        pltpu.make_async_copy(count_in, count, sems.at[1]),
    ]
    ids = [
        pltpu.make_async_copy(ref, edges.at[k, pl.ds(0, edge_blocks), :], sems.at[2 + k])
        for k, ref in enumerate((send_in, recv_in))
    ]
    def fetch(source):
        return [
            pltpu.make_async_copy(source.at[1 - micro], there.at[pl.ds(0, rows), :], sems.at[4]),
            pltpu.make_async_copy(source.at[micro], here, sems.at[5]),
        ]

    whole = pltpu.make_async_copy(inputs.at[lax.axis_index("pipe") % 2], blocks, sems.at[6])

    for copy in lists + ids:
        copy.start()

    @pl.when(here_is(0))
    def _():
        for copy in fetch(inputs):
            copy.start()

    @pl.when(jnp.logical_not(here_is(0)))
    def _():
        for copy in fetch(cotangent):
            copy.start()

    whole.start()
    for copy in lists:
        copy.wait()
    number = jnp.where(micro == 1, halo[0, 0, 0], halo[0, 0, 1])
    for copy in ids:
        copy.wait()
    lane = lax.broadcasted_iota(jnp.int32, (1, block), 1)
    tail = jnp.where(lane == 0, halo[0, 0, 0], jnp.where(lane == 1, halo[0, 0, 1], 0))
    for place in range(edge_blocks):
        tail = jnp.where(lane == 2 + place, count[place], tail)
    spare = jnp.zeros((7 - 2 * edge_blocks, block), jnp.int32)
    tile = encode(jnp.concatenate([edges[0, :edge_blocks, :], edges[1, :edge_blocks, :], tail, spare], axis=0))
    packed[...] = tile
    there[rows:, :] = jnp.zeros((there.shape[0] - rows, there.shape[1]), BF16)
    there[rows:, :block] = tile
    for copy in fetch(inputs):
        copy.wait()
    whole.wait()
    boundary[...] = blocks[pl.ds(pl.multiple_of(number * block, block), block), :]


def weights_kernel(w_send, w_recv, w_node, w_message, w_aggregate, out, factors, sems):
    depth = w_send.shape[0]
    copies = [pltpu.make_async_copy(ref, factors.at[k], sems.at[k]) for k, ref in enumerate((w_message, w_aggregate))]
    copies += [
        pltpu.make_async_copy(ref, out.at[pl.ds(k * depth, depth), :], sems.at[2 + k])
        for k, ref in enumerate((w_send, w_recv, w_node))
    ]
    for copy in copies:
        copy.start()
    for copy in copies[:2]:
        copy.wait()
    out[3 * depth :, :] = mul(factors[0], factors[1]).astype(BF16)
    for copy in copies[2:]:
        copy.wait()


def place_mine_kernel(mine, even, odd):
    @pl.when(here_is(parity=0))
    def _():
        even[...] = mine[...]

    @pl.when(here_is(parity=1))
    def _():
        odd[...] = mine[...]


def place_swapped_kernel(swapped, _, even_in, odd_in, even, odd):
    del even_in, odd_in

    @pl.when(here_is(parity=0))
    def _():
        odd[...] = swapped[...]

    @pl.when(here_is(parity=1))
    def _():
        even[...] = swapped[...]


def graph_kernel(edge_blocks, packed, there, gown, gown_t, ghalo, ghalo_t, lists, home_lists):
    block = packed.shape[1]
    rows = gown_t.shape[0]
    edges = edge_blocks * block
    local = is_local()
    first_core = lax.axis_index("pipe") % 2 == 0
    last = 2 * edge_blocks
    tiles = decode(packed[...]), decode(there[rows:, :block])
    mine = jnp.where(local, *tiles)
    tails = [tile[last : last + 1] for tile in (mine, tiles[0])]
    lane = lax.broadcasted_iota(jnp.int32, (1, block), 1)
    row = lax.broadcasted_iota(jnp.int32, (rows, block), 0)
    halo_row = lax.broadcasted_iota(jnp.int32, (2 * block, block), 0)
    for number in range(edge_blocks):
        live = lane < tails[0][:, 2 + number : 3 + number]
        sender = jnp.where(live, mine[number : number + 1], -1)
        receiver = jnp.where(live, mine[edge_blocks + number : edge_blocks + number + 1], -1)
        outside = sender - rows
        turned = jnp.where(outside < block, outside + block, outside - block)
        outside = jnp.where(outside >= 0, jnp.where(first_core, turned, outside), -1)
        here = slice(number * block, (number + 1) * block)
        received = slice(edges + number * block, edges + (number + 1) * block)
        for index, at, table, table_t in (
            (sender, here, gown, gown_t),
            (receiver, received, gown, gown_t),
            (outside, here, ghalo, ghalo_t),
        ):
            hot = (index == (halo_row if table is ghalo else row)).astype(F32)
            table_t[:, at] = hot.astype(BF16)
            table[at, :] = hot.T.astype(BF16)

    def whole(tail, place):
        return jnp.broadcast_to(tail[:1, place : place + 1], (1, block))

    to_next, to_prev = whole(tails[0], 0), whole(tails[0], 1)
    lists[0:1, :] = jnp.where(first_core, to_next, to_prev)
    lists[1:2, :] = jnp.where(first_core, to_prev, to_next)
    to_next, to_prev = whole(tails[1], 0), whole(tails[1], 1)
    home_first = lax.axis_index("dom") % 2 == 0
    home_lists[0:1, :] = jnp.where(home_first, to_next, to_prev)
    home_lists[1:2, :] = jnp.where(home_first, to_prev, to_next)


def entry_kernel(here, there, _, lists, hidden, to_inner):
    @pl.when(is_local())
    def _():
        hidden[...] = here[...]

    @pl.when(jnp.logical_not(is_local()))
    def _():
        hidden[...] = there[: hidden.shape[0], :]

    to_inner[...] = listed(lists[INNER : INNER + 1, :1], hidden[...], to_inner.shape[0])


def forward_own_kernel(take, h, gown, *refs):
    w_send, w_recv, w_node, _ = quarters(take[0])
    a_out, u_out = refs[-2:]
    edges = gown.shape[0] // 2
    own = mul(gown[...], h[...]).astype(BF16)
    a_out[...] = mul(own[:edges], w_send[...]) + mul(own[edges:], w_recv[...])
    u_out[...] = mul(h[...], w_node[...])


def forward_kernel(parity, first, last, take, lists, h, a_own, u_own, inner, outer, ghalo, gown_t, *refs):
    packed, *gains = take
    w_send, _, _, w_fold = quarters(packed)
    gain = jnp.where(here_is(parity=parity), gains[0][...], gains[1][...])
    edges = ghalo.shape[0]
    block = inner.shape[0]
    halo = mul(ghalo[...], jnp.concatenate([inner[...], outer[...]], axis=0)).astype(BF16)
    a = a_own[...] + mul(halo, w_send[...])
    q = (a * jax.nn.sigmoid(a)).astype(BF16)
    u = u_own[...] + mul(mul(gown_t[:, edges:], q).astype(BF16), w_fold[...])
    t, inverse = normalize(u * jax.nn.sigmoid(u))
    out = (h[...].astype(F32) + t * gain).astype(BF16)
    if last:
        keep(parity, a, u, t, inverse, out, *refs[-4:])
        return
    if first:
        h_out, *to = refs[:3]
        keep(parity, a, u, t, inverse, out, *refs[3:])
    else:
        h_out, a_out, u_out, *to = refs
        a_out[...] = a
        u_out[...] = u
    h_out[...] = out
    for side, ref in zip((OUTER, INNER), reversed(to)):
        ref[...] = listed(lists[side : side + 1, :1], out, block)


def inner_kernel(lists, h, out):
    out[...] = listed(lists[INNER : INNER + 1, :1], h[...], out.shape[0])


def keep(parity, a, u, t, inverse, h, t_out, r_out, s_out, h_out):
    rows, edges = h.shape[0], a.shape[0]
    at = slice(parity * rows, (parity + 1) * rows)
    s_out[parity * edges : (parity + 1) * edges, :] = slope(a).astype(BF16)
    t_out[at, :] = t.astype(BF16)
    r_out[at, :] = (inverse * slope(u)).astype(BF16)
    h_out[at, :] = h


def save_kernel(plane, parity, a, u, h, *refs):
    @pl.when(here_is(plane))
    def _():
        u_value = u[...]
        t, inverse = normalize(u_value * jax.nn.sigmoid(u_value))
        keep(parity, a[...], u_value, t, inverse, h[...], *refs[-4:])


def backward_kernel(sides, finish, parity, kept, take, *refs):
    packed, *gains = take
    w_send, _, _, w_fold = quarters(packed)
    gain = jnp.where(here_is(parity=parity), gains[0][...], gains[1][...])
    lists, upstream, *refs = refs[kept:]
    arrived, refs = refs[: len(sides)], refs[len(sides) :]
    t_in, r_in, s_in, gown, ghalo_t, c_out, du_out, da_out, es_out, *done, to_inner, to_outer = refs
    edges = gown.shape[0] // 2
    rows = upstream.shape[0]
    block = to_inner.shape[0]
    at = slice(parity * rows, (parity + 1) * rows)
    at_edges = slice(parity * edges, (parity + 1) * edges)
    c_out[...] = upstream[...].astype(F32)
    for side, ref in zip(sides, arrived):
        if ref.shape == c_out.shape:
            c_out[...] = c_out[...] + ref[...]
        else:
            add_listed(lists[side : side + 1, :1], c_out, ref[...].astype(F32), block)
    if finish:
        done[0][...] = c_out[...].astype(BF16)
    g = c_out[...] * gain
    t = t_in[at, :].astype(F32)
    centre = jnp.mean(g, axis=-1, keepdims=True)
    along = jnp.mean(g * t, axis=-1, keepdims=True)
    du = ((g - centre - t * along) * r_in[at, :].astype(F32)).astype(BF16)
    du_out[...] = du
    spread = mul(gown[edges:, :], du).astype(BF16)
    da = (mul_t(spread, w_fold[...]) * s_in[at_edges, :].astype(F32)).astype(BF16)
    da_out[...] = da
    es = mul_t(da, w_send[...]).astype(BF16)
    es_out[...] = es
    halo = mul(ghalo_t[...], es).astype(BF16)
    to_inner[...] = halo[:block]
    to_outer[...] = halo[block:]


def backward_own_kernel(add_inner, last, take, *refs):
    _, w_recv, w_node, _ = quarters(take[0])
    if last:
        _, _, other, *refs = refs
    if add_inner:
        lists, inner, *refs = refs
    refs, out = (refs[:-2], refs[-2:]) if last else (refs[:-1], refs[-1:])
    *_, c, du, da, es, gown_t = refs
    er = mul_t(da[...], w_recv[...]).astype(BF16)
    both = jnp.concatenate([es[...], er], axis=0)
    total = c[...] + mul_t(du[...], w_node[...]) + mul(gown_t[...], both)
    if add_inner:
        block = inner.shape[0]
        at = lists[INNER : INNER + 1, :1]
        value = inner[...].astype(F32)
        total = total + jnp.concatenate(
            [jnp.where(at == number, value, 0.0) for number in range(total.shape[0] // block)], axis=0
        )
    if last:
        order(total.astype(BF16), other[...], *out)
    else:
        out[0][...] = total.astype(out[0].dtype)


def order(even, odd, first, second):
    zero = lax.axis_index("dom") % 2 == 0

    @pl.when(zero)
    def _():
        first[...] = even
        second[...] = odd

    @pl.when(jnp.logical_not(zero))
    def _():
        first[...] = odd
        second[...] = even


def order_kernel(both, first, second):
    rows = first.shape[0]
    order(both[:rows, :], both[rows:, :], first, second)


def add_kernel(lists, value, outer, other, first, second, total):
    @pl.when(here_is(1))
    def _():
        total[...] = value[...].astype(F32)
        add_listed(lists[OUTER : OUTER + 1, :1], total, outer[...].astype(F32), outer.shape[0])
        order(total[...].astype(BF16), other[...], first, second)


def spread_kernel(lists, outer, out):
    block = outer.shape[0]
    at = lists[OUTER : OUTER + 1, :1]
    value = outer[...].astype(F32)
    for number in range(out.shape[0] // block):
        out[number * block : (number + 1) * block, :] = jnp.where(at == number, value, 0.0)


def place_kernel(lists, outer, flipped, first, second):
    block = outer.shape[0]
    at = lists[OUTER : OUTER + 1, :1]
    for value, out in ((outer, first), (flipped, second)):
        for number in range(out.shape[0] // block):
            covered = jnp.broadcast_to(at == number, value.shape) & here_is(0, 0)
            out[number * block : (number + 1) * block, :] = jnp.where(covered, value[...].astype(F32), 0.0).astype(BF16)


def sum_kernel(*refs):
    ends, placed, totals = (refs[2 * k : 2 * k + 2] for k in range(3))
    for k in range(2):
        totals[k][...] = (ends[k][...].astype(F32) + placed[k][...].astype(F32)).astype(BF16)


def write_kernel(*refs):
    first_home, second_home, totals = (refs[2 * k : 2 * k + 2] for k in range(3))
    out_home, out_grads, sems = refs[6:]
    core = lax.axis_index("pipe") % 2
    slots = core, 1 - core

    def outputs(source):
        return [pltpu.make_async_copy(source[k], out_home.at[0, slots[k]], sems.at[k]) for k in range(2)]

    copies = [pltpu.make_async_copy(totals[k], out_grads.at[0, slots[k]], sems.at[2 + k]) for k in range(2)]
    for copy in copies:
        copy.start()

    @pl.when(here_is(0))
    def _():
        for copy in outputs(first_home):
            copy.start()

    @pl.when(jnp.logical_not(here_is(0)))
    def _():
        for copy in outputs(second_home):
            copy.start()

    for copy in copies + outputs(first_home):
        copy.wait()


def run(kernel, operands, outs, spaces=(), aliases=None, out_spaces=(), scratch=(), cost=1, vmem=12):
    spaces = tuple(spaces) + (pltpu.VMEM,) * (len(operands) - len(spaces))
    operands = [
        pltpu.with_memory_space_constraint(operand, space) if space == pltpu.HBM else operand
        for operand, space in zip(operands, spaces)
    ]
    out_spaces = tuple(out_spaces) + (pltpu.VMEM,) * (len(outs) - len(out_spaces))
    return pl.pallas_call(
        kernel,
        out_shape=[jax.ShapeDtypeStruct(s, t) for s, t in outs],
        in_specs=[pl.BlockSpec(memory_space=space) for space in spaces],
        out_specs=[pl.BlockSpec(memory_space=space) for space in out_spaces],
        scratch_shapes=list(scratch),
        input_output_aliases=aliases or {},
        compiler_params=pltpu.CompilerParams(vmem_limit_bytes=vmem * 2**20),
        cost_estimate=pl.CostEstimate(flops=cost, bytes_accessed=1, transcendentals=0),
    )(*operands)


def run_section(body, plane, matrices, operands, outs, elsewhere=None, aliases=None, cost=1):
    elsewhere = elsewhere or {}

    def kernel(*refs):
        take, rest = refs[: len(matrices)], refs[len(matrices) :]

        @pl.when(here_is(plane))
        def _():
            body(take, *rest)

        if elsewhere:

            @pl.when(jnp.logical_not(here_is(plane)))
            def _():
                for source, target in elsewhere.items():
                    rest[target][...] = rest[source][...]

    aliases = {len(matrices) + source: target for source, target in (aliases or {}).items()}
    return run(kernel, tuple(matrices) + tuple(operands), outs, aliases=aliases, cost=cost)


def shards(
    inputs,
    cotangent,
    w_send,
    w_recv,
    w_message,
    w_node,
    w_aggregate,
    gains,
    edge_send,
    edge_recv,
    edge_count,
    halo_send,
):
    sections = lax.axis_size("pipe")
    pairs_total = lax.axis_size("dom") // 2
    phase = lax.axis_index("pipe")
    y = lax.rem(lax.axis_index("dom"), 2)
    plane_here = phase // 2
    rows, latent = inputs.shape[1:]
    edge_blocks, block = edge_send.shape
    edges = edge_blocks * block

    def send(value, rule):
        table = []
        for z in range(pairs_total):
            for which in range(2):
                for x in range(sections // 2):
                    for c in range(2):
                        if (target := rule(z, which, x, c)) is None:
                            continue
                        tz, ty, tx, tc = target
                        target = (2 * (tz % pairs_total) + ty) * sections + 2 * (tx % (sections // 2)) + tc
                        table.append(((2 * z + which) * sections + 2 * x + c, target))
        return lax.ppermute(value, AXES, table)

    def flip_y(value):
        return send(value, lambda z, y, x, c: (z, 1 - y, x, c))

    def flip_core(value):
        return send(value, lambda z, y, x, c: (z, y, x, 1 - c))

    def go_home(first, second, plane=None):
        return (
            send(first, lambda z, y, x, c: (z, c, x, y) if plane in (None, x) else None),
            send(second, lambda z, y, x, c: (z, c, x, 1 - y) if plane in (None, x) else None),
        )

    def towards(value, side, step):
        if side == INNER:
            return send(value, lambda z, y, x, c: (z, y, x, 1 - c))
        return send(value, lambda z, y, x, c: (z + 2 * c - 1, y, x + step, 1 - c) if x + min(step, 0) >= 0 else None)

    def across(value):
        return send(value, lambda z, y, x, c: (z, y, x + 1, c))

    wide = (rows, latent)
    edge_wide = (edges, latent)
    narrow = (block, latent)
    both_wide = (2 * rows, latent)
    unit = 2 * rows * latent * latent
    dma = pltpu.SemaphoreType.DMA

    here, there, boundary, packed = run(
        prepare_kernel,
        (edge_count, jnp.swapaxes(halo_send, 1, 2), inputs, cotangent, edge_send, edge_recv),
        [(wide, BF16), ((rows + 16, latent), BF16), (narrow, BF16), ((16, block), BF16)],
        spaces=(pltpu.HBM,) * 6,
        scratch=[
            pltpu.SMEM((edge_blocks,), jnp.int32),
            pltpu.SMEM((1, 1, 2), jnp.int32),
            pltpu.VMEM(wide, BF16),
            pltpu.VMEM((2, 8, block), jnp.int32),
            dma((7,)),
        ],
    )
    there = send(there, lambda z, y, x, c: (z, 1 - y, x, c) if c == y else (z, y, x, 1 - c))
    outer = send(boundary, lambda z, y, x, c: (z + 2 * y - 1, c, x, 1 - y))
    gown, gown_t, ghalo, ghalo_t, lists, home_lists = run(
        functools.partial(graph_kernel, edge_blocks),
        (packed, there),
        [
            ((2 * edges, rows), BF16),
            ((rows, 2 * edges), BF16),
            ((edges, 2 * block), BF16),
            ((2 * block, edges), BF16),
            ((2, block), jnp.int32),
            ((2, block), jnp.int32),
        ],
    )
    hidden, inner = run(entry_kernel, (here, there, outer, lists), [(wide, BF16), (narrow, BF16)], cost=LONG * 3 // 2)
    inner = towards(inner, INNER, 0)

    [weights] = run(
        weights_kernel,
        (w_send[0], w_recv[0], w_node[0], w_message[0], w_aggregate[0]),
        [((4 * latent, latent), BF16)],
        spaces=(pltpu.HBM,) * 5,
        scratch=[pltpu.VMEM((2, latent, latent), BF16), dma((5,))],
    )
    pair = run(place_mine_kernel, (weights,), [((4 * latent, latent), BF16)] * 2)
    matrices = run(
        place_swapped_kernel, (flip_core(weights), hidden, *pair), [((4 * latent, latent), BF16)] * 2, aliases={2: 0, 3: 1}
    )
    both_gains = (gains, flip_core(gains))
    upstream = hidden

    saved = ()
    arrived = ()
    for tick in range(sections):
        plane, parity = tick // 2, tick % 2
        packed = matrices[parity]
        a_own, u_own = run_section(
            forward_own_kernel, plane, (packed,), (hidden, gown) + arrived, [(edge_wide, F32), (wide, F32)], cost=BESIDE
        )
        if tick == sections - 1:
            outputs, a_own = lax.optimization_barrier((saved[3], a_own))
            first_home = go_home(*run(order_kernel, (outputs,), [(wide, BF16)] * 2), plane=0)
        step = (tick + 1) // 2 - plane if tick < sections - 1 else None
        to_send = [(narrow, BF16)] * {0: 2, 1: 1, None: 0}[step]
        last = tick == sections - 1
        state = [(both_wide, BF16), (both_wide, BF16), ((2 * edges, latent), BF16), (both_wide, BF16)]
        made = run_section(
            functools.partial(forward_kernel, parity, tick == 0, last),
            plane,
            (packed, *both_gains),
            (lists, hidden, a_own, u_own, inner, outer, ghalo, gown_t) + (tuple(saved) if last else ()),
            state
            if last
            else [(wide, BF16)] + to_send + state
            if tick == 0
            else [(wide, BF16), (edge_wide, F32), (wide, F32)] + to_send,
            aliases={8 + k: k for k in range(4)} if last else None,
            cost=BESIDE // 2 if last else 1,
        )
        if last:
            saved = made
            break
        if tick == 0:
            hidden, to, saved = made[0], made[1:3], made[3:]
        else:
            hidden, a, u, *to = made
        produced = hidden
        if step == 0:
            outer = towards(to[-1], OUTER, step)
            inner = towards(to[0], INNER, step)
            arrived = (inner,)
        elif step:
            hidden = across(hidden)
            inner = towards(*run(inner_kernel, (lists, hidden), [(narrow, BF16)]), INNER, 0)
            arrived = ()
        if tick == 0:
            continue
        saved = run(
            functools.partial(save_kernel, plane, parity),
            (a, u, produced) + tuple(saved),
            state,
            aliases={3 + k: k for k in range(4)} if saved else None,
            cost=1 if step else BESIDE,
        )
        if step:
            to_outer, *saved = lax.optimization_barrier((to[-1], *saved))
            outer = towards(to_outer, OUTER, step)

    *states, both = saved
    halos = {}
    finished = {}
    second_home = ()
    for tick in range(sections - 1, -1, -1):
        plane, parity = tick // 2, tick % 2
        packed = matrices[parity]
        step = (tick - 1) // 2 - plane if tick else 0
        finish = bool(halos) and tick % 2 == 0
        outs = [(wide, F32), (wide, BF16), (edge_wide, BF16), (edge_wide, BF16)]
        outs += [(wide, BF16)] if finish else []
        outs += [(narrow, BF16)] * 2
        kept = (to_outer,) if tick == 1 else ()
        c, du, da, es, *done, to_inner, to_outer = run_section(
            functools.partial(backward_kernel, tuple(halos), finish, parity, len(kept)),
            plane,
            (packed, *both_gains),
            kept + (lists, upstream) + tuple(halos.values()) + tuple(states) + (gown, ghalo_t),
            outs,
            elsewhere={0: -1} if tick == 1 else {},
            cost=1 if tick else BESIDE // 2,
        )
        if done:
            finished[tick + 1] = done[0]
        inner = towards(to_inner, INNER, 0)
        halos = {OUTER: towards(to_outer, OUTER, step)} if tick else {}
        add_inner = tick == 0 or step != 0
        last = tuple(ends) + (finished[1],) if tick == 0 else ()
        beside = (lists, inner) if add_inner else (inner,)
        upstream, *rest = run_section(
            functools.partial(backward_own_kernel, add_inner, bool(last)),
            plane,
            (packed,),
            last + beside + tuple({sections - 1: first_home, 0: second_home}.get(tick, ())) + (c, du, da, es, gown_t),
            [(wide, BF16)] * 2 if last else [(wide, BF16 if step else F32)],
            elsewhere={0: -2, 1: -1} if last else {},
            cost=BESIDE if tick else 1,
        )
        if not add_inner:
            halos = {INNER: inner, **halos}
        if step:
            own = upstream
            upstream = across(upstream)
            halos = {OUTER: run(spread_kernel, (lists, halos[OUTER]), [(wide, F32)], cost=LONG)[0]}
        elif tick == 1:
            outputs, upstream = lax.optimization_barrier((both, upstream))
            second_home = go_home(*run(order_kernel, (outputs,), [(wide, BF16)] * 2), plane=1)
            ends = run(
                add_kernel,
                (lists, own, halos[OUTER], finished[3]),
                [(wide, BF16)] * 2,
                scratch=[pltpu.VMEM(wide, F32)],
            )

    final_outer = send(to_outer, lambda z, y, x, c: (z + 2 * c - 1, 1 - c, x, y))
    ends = go_home(upstream, *rest)
    placed = run(
        place_kernel, (home_lists, final_outer, flip_core(final_outer)), [(wide, BF16)] * 2
    )
    totals = run(sum_kernel, tuple(ends) + tuple(placed), [(wide, BF16)] * 2, cost=LONG)
    return tuple(
        run(
            write_kernel,
            tuple(first_home) + tuple(second_home) + tuple(totals),
            [((1, 2) + wide, BF16)] * 2,
            out_spaces=(pltpu.HBM,) * 2,
            scratch=[dma((4,))],
        )
    )


def solution(mesh):
    in_specs = (
        P(None, "dom", None),
        P(None, "dom", None),
        P("pipe", None, None),
        P("pipe", None, None),
        P("pipe", None, None),
        P("pipe", None, None),
        P("pipe", None, None),
        P("pipe", None),
        P("dom", None),
        P("dom", None),
        P("dom"),
        P("dom", None, None),
    )
    out_specs = (P("pipe", None, "dom", None), P("pipe", None, "dom", None))
    return jax.shard_map(shards, mesh=mesh, in_specs=in_specs, out_specs=out_specs, check_vma=False)
```
